128 devices in a mesh: dp: 8 (over y, core), inner: 16 (over x, z).
Axes of the slice: x: 4, y: 4, z: 4, core: 2. Of those that a mesh axis runs over, the one named last changes fastest.
Arguments:
- patches: bfloat16 [49152, 1280], P(('dp', 'inner')), may hold values from -5 to 5
- segments: int32 [384, 128], P(('dp', 'inner')), may hold values from 0 to 63, as said below
- owners: int32 [384], P(('dp', 'inner')), may hold values from 0 to 7, as said below
- norm_gain: float32 [1280], replicated, may hold values from 0.1 to 1.9
- qkv_weight: bfloat16 [1280, 3840], P(('dp', 'inner')), may hold values from -0.12633784 to 0.12633784
- cotangent: bfloat16 [49152, 1280], P(('dp', 'inner')), may hold values from -6 to 6
Outputs:
- attended: bfloat16 [49152, 1280], P(('dp', 'inner'))
- grad_patches: bfloat16 [49152, 1280], P(('dp', 'inner'))
- grad_qkv: float32 [1280, 3840], P(('dp', 'inner'))
- grad_gain: float32 [1280], replicated
The draws below stay inside these ranges and needn't reach their ends.
Inputs may be any that keep to these rules, and one draw needn't show every extreme that they name: `segments`: within a tile the ids start at 0 and grow by 0 or 1 from one patch to the next, growing only at even positions of the tile; patches of one image share an id. `owners`: the 3 tiles of one device go to 3 different groups, and for every inner index each group is owner of exactly 3 tiles.
All inputs are finite; a program needn't handle non-finite values.
Results may differ from the reference program's by a relative error of at most 0.017.
Values may be sent and summed in bfloat16 or wider, within the bound.
No kernel may reach another device: no remote copies, remote signals or barrier semaphores. Data moves between devices by JAX's collectives and lax.ppermute only.
A program may use at most 192 MiB of HBM per device.

```python
import jax
import jax.numpy as jnp
from jax import lax

D = 1280
HEADS = 16
HDIM = 80
TILE = 128
TILES = 3
TILES_ALL = 384
TOKENS = 49152
N_DP = 8
N_INNER = 16


def draw_patches(key, part):
    key = jax.random.fold_in(key, 31)
    sample_key = jax.random.fold_in(key, 0)
    samples = jnp.clip(jax.random.normal(sample_key, (TOKENS, D), jnp.float32), -5.0, 5.0)
    return samples.astype(jnp.bfloat16)


def draw_qkv_weight(key, part):
    key = jax.random.fold_in(key, 47)
    spread = D ** (-0.5)
    entries = jnp.clip(jax.random.normal(key, (D, 3 * D), jnp.float32), -4.5, 4.5) * spread
    return entries.astype(jnp.bfloat16)


def draw_segments(key, part):
    key = jax.random.fold_in(key, 11)
    coins = jax.random.randint(key, (TILES_ALL, TILE), 0, TILE // 2)
    even_place = (jnp.arange(TILE) % 2 == 0)[None, :]
    starts = ((coins == 0) & even_place).astype(jnp.int32)
    starts = starts.at[0].set(even_place[0].astype(jnp.int32))
    starts = starts.at[:, 0].set(1)
    return (jnp.cumsum(starts, axis=1) - 1).astype(jnp.int32)


def draw_owners(key, part):
    key = jax.random.fold_in(key, 23)
    column_keys = jax.random.split(key, N_INNER)

    def column(column_key):
        subkeys = jax.random.split(column_key, 3 + N_DP)
        relabel = jax.random.permutation(subkeys[0], N_DP)
        placing = jax.random.permutation(subkeys[1], N_DP)
        offsets = jax.random.permutation(subkeys[2], N_DP)[:TILES]

        def device(device_key, position):
            order = jax.random.permutation(device_key, TILES)
            return relabel[(placing[position] + offsets[order]) % N_DP]
        return jax.vmap(device)(subkeys[3:], jnp.arange(N_DP))
    grid = jax.vmap(column)(column_keys)
    return jnp.transpose(grid, (1, 0, 2)).reshape(TILES_ALL).astype(jnp.int32)


def block_scale(stream_key, shape, cuts, smallest, top_value):
    def one(dim, parts):
        steps = jax.random.uniform(jax.random.fold_in(jax.random.fold_in(stream_key, 6), dim), (parts,), jnp.float32, smallest / len(cuts), top_value / len(cuts))
        return jnp.repeat(jnp.exp(steps), shape[dim] // parts).reshape((-1,) + (1,) * (len(shape) - dim - 1))

    factor_of = one(*cuts[0])
    for cut in cuts[1:]:
        factor_of = factor_of * one(*cut)
    return factor_of


def bell_draw(stream_key, dims, width, most, pieces=(), dtype=jnp.bfloat16):
    drawn = width * jax.random.normal(stream_key, dims, jnp.float32)
    if pieces:
        drawn = drawn * block_scale(stream_key, dims, pieces, -0.22, 0.18)
    return jnp.clip(drawn, -most, most).astype(dtype)


def setup_inputs(seed: int = 0) -> dict:
    keys = jax.random.split(jax.random.key(seed), 7)
    patches = draw_patches(jax.random.fold_in(keys[6], 71), 0)
    segments = draw_segments(jax.random.fold_in(keys[6], 71), 0)
    owners = draw_owners(jax.random.fold_in(keys[6], 71), 0)
    norm_gain = jnp.clip(1.0 + 0.18 * jax.random.normal(keys[3], (D,), jnp.float32), 0.1, 1.9)
    qkv_weight = draw_qkv_weight(jax.random.fold_in(keys[6], 71), 0)
    cotangent = bell_draw(keys[5], (TOKENS, D), 1.0, 6.0, ((0, 128),))
    return {"patches": patches, "segments": segments, "owners": owners, "norm_gain": norm_gain, "qkv_weight": qkv_weight, "cotangent": cotangent}


epsilon_value = 1e-06
masked_score = -1e+30

def normalize(patch_rows, norm_gain):
    widened = patch_rows.astype(jnp.float32)
    row_mean = lax.optimization_barrier(jnp.mean(widened, axis=-1, keepdims=True))
    centred = widened - row_mean
    variance = lax.optimization_barrier(jnp.mean(centred * centred, axis=-1, keepdims=True))
    inv_std = lax.rsqrt(variance + epsilon_value)
    standard = centred * inv_std
    normed = (standard * norm_gain).astype(jnp.bfloat16)
    return (standard, inv_std, normed)

def split_heads(qkv_tiles):
    grouped = qkv_tiles.astype(jnp.float32).reshape(qkv_tiles.shape[0], qkv_tiles.shape[1], 3, HEADS, HDIM)
    return (grouped[:, :, 0], grouped[:, :, 1], grouped[:, :, 2])

def attend(qkv_tiles, seg_tiles):
    queries, key_rows, values = split_heads(qkv_tiles)
    score_scale = HDIM ** (-0.5)
    scores = jnp.einsum('tqhd,tkhd->thqk', queries, key_rows) * score_scale
    same_image = (seg_tiles[:, :, None] == seg_tiles[:, None, :])[:, None]
    scores = jnp.where(same_image, scores, masked_score)
    row_max = lax.optimization_barrier(jnp.max(scores, axis=-1, keepdims=True))
    exponent = jnp.exp(scores - row_max)
    weights = exponent / lax.optimization_barrier(jnp.sum(exponent, axis=-1, keepdims=True))
    rounded_weights = weights.astype(jnp.bfloat16)
    heads_out = jnp.einsum('thqk,tkhd->tqhd', rounded_weights.astype(jnp.float32), values)
    tile_out = heads_out.astype(jnp.bfloat16).reshape(qkv_tiles.shape[0], qkv_tiles.shape[1], HEADS * HDIM)
    return (tile_out, weights, rounded_weights)

def attend_back(qkv_tiles, weights, rounded_weights, d_out):
    queries, key_rows, values = split_heads(qkv_tiles)
    score_scale = HDIM ** (-0.5)
    d_heads = d_out.astype(jnp.float32).reshape(d_out.shape[0], d_out.shape[1], HEADS, HDIM)
    d_probs = jnp.einsum('tqhd,tkhd->thqk', d_heads, values)
    d_values = jnp.einsum('thqk,tqhd->tkhd', rounded_weights.astype(jnp.float32), d_heads)
    row_inner = lax.optimization_barrier(jnp.sum(d_probs * weights, axis=-1, keepdims=True))
    d_scores = (weights * (d_probs - row_inner) * score_scale).astype(jnp.bfloat16).astype(jnp.float32)
    d_queries = jnp.einsum('thqk,tkhd->tqhd', d_scores, key_rows)
    d_keys = jnp.einsum('thqk,tqhd->tkhd', d_scores, queries)
    stacked = jnp.stack([d_queries, d_keys, d_values], axis=2)
    return stacked.astype(jnp.bfloat16).reshape(d_out.shape[0] * d_out.shape[1], 3 * HEADS * HDIM)

def reference(patches, segments, owners, norm_gain, qkv_weight, cotangent):
    device_count = N_DP * N_INNER
    owner_grid = owners.reshape(N_DP, N_INNER, TILES).astype(jnp.int32)
    group_index = jnp.arange(N_DP).astype(jnp.int32)[:, None, None]
    sort_keys = owner_grid * N_DP + group_index
    keys_inner = jnp.transpose(sort_keys, (1, 0, 2)).reshape(N_INNER, N_DP * TILES)
    ranking = jnp.argsort(jnp.argsort(keys_inner, axis=1), axis=1).astype(jnp.int32)
    ranking = jnp.transpose(ranking.reshape(N_INNER, N_DP, TILES), (1, 0, 2))
    inner_index = jnp.arange(N_INNER).astype(jnp.int32)[None, :, None]
    targets = ranking // TILES * (N_INNER * TILES) + inner_index * TILES + ranking % TILES
    targets = targets.reshape(TILES_ALL).astype(jnp.int32)
    cotangent_tiles = cotangent.reshape(TILES_ALL, TILE, D)[targets]
    patch_blocks = patches.reshape(device_count, TILES * TILE, D)
    seg_blocks = segments.reshape(device_count, TILES, TILE)
    cot_blocks = cotangent_tiles.reshape(device_count, TILES, TILE, D)

    def device_step(carry, inputs):
        grad_weight, grad_norm = carry
        patch_rows, seg_tiles, cot_tiles = inputs
        standard, inv_std, normed = normalize(patch_rows, norm_gain)
        qkv = jnp.dot(normed, qkv_weight, preferred_element_type=jnp.float32).astype(jnp.bfloat16)
        qkv = qkv.reshape(TILES, TILE, 3 * D)
        tile_out, weights, rounded_weights = attend(qkv, seg_tiles)
        d_qkv = attend_back(qkv, weights, rounded_weights, cot_tiles)
        grad_weight = grad_weight + jnp.dot(normed.T, d_qkv, preferred_element_type=jnp.float32)
        d_normed = jnp.dot(d_qkv, qkv_weight.T, preferred_element_type=jnp.float32)
        grad_norm = grad_norm + lax.optimization_barrier(jnp.sum(d_normed * standard, axis=0))
        scaled = d_normed * norm_gain
        grad_rows = inv_std * (scaled - lax.optimization_barrier(jnp.mean(scaled, axis=-1, keepdims=True)) - standard * lax.optimization_barrier(jnp.mean(scaled * standard, axis=-1, keepdims=True)))
        return ((grad_weight, grad_norm), (tile_out, grad_rows.astype(jnp.bfloat16)))
    start_carry = (jnp.zeros((D, 3 * D), jnp.float32), jnp.zeros((D,), jnp.float32))
    final_carry, results = lax.scan(device_step, start_carry, (patch_blocks, seg_blocks, cot_blocks))
    grad_qkv, grad_gain = final_carry
    tile_outs, grad_rows = results
    attended = jnp.zeros((TILES_ALL, TILE, D), jnp.bfloat16).at[targets].set(tile_outs.reshape(TILES_ALL, TILE, D))
    return (attended.reshape(TOKENS, D), grad_rows.reshape(TOKENS, D), grad_qkv, grad_gain)
```

```python
import functools

import jax
import jax.numpy as jnp
from jax import lax
from jax.experimental import pallas as pl
from jax.experimental.pallas import tpu as pltpu
from jax.sharding import PartitionSpec as P

D = 1280
HEADS = 16
HDIM = 80
TILE = 128
TILES = 3
N_DP = 8
N_INNER = 16
ROWS = TILES * TILE
PAIR_ROWS = 2 * ROWS
HALF = D // 2
COLS = 3 * HALF
OWN = 10
BLOCK = 80
PART = 160
PIECES = 8
STRIP = 16
MSG = 16
EPS = 1e-6
MASKED = -1e30
SCALE = HDIM ** (-0.5)
LOG2E = 1.4426950408889634
BF = jnp.bfloat16
F32 = jnp.float32
VM = pl.BlockSpec(memory_space=pltpu.VMEM)
SM = pl.BlockSpec(memory_space=pltpu.SMEM)
ANY = pl.BlockSpec(memory_space=pl.ANY)
NT = (((1,), (1,)), ((), ()))
TN = (((0,), (0,)), ((), ()))
NN = (((1,), (0,)), ((), ()))


def params(mib, **more):
    return pltpu.CompilerParams(vmem_limit_bytes=mib * 2**20, **more)


def cost(flops, nbytes, trans=0):
    return pl.CostEstimate(
        flops=flops // 1000, bytes_accessed=nbytes // 1000, transcendentals=trans // 1000
    )


def dot(a, b, dims=NN):
    return lax.dot_general(a, b, dims, preferred_element_type=F32)


def norm_rows(rows):
    wide = rows.astype(F32)
    centred = wide - jnp.mean(wide, axis=-1, keepdims=True)
    variance = jnp.mean(centred * centred, axis=-1, keepdims=True)
    inv_std = lax.rsqrt(variance + EPS)
    return centred * inv_std, inv_std


def build_order(nat_ref, perm_ref):
    for a in range(5):
        cols = slice(256 * a, 256 * (a + 1))
        feature = lax.broadcasted_iota(jnp.int32, (D, 256), 1) + 256 * a
        perm_ref[:, cols] = jnp.where(nat_ref[...] == feature, 1.0, 0.0).astype(BF)


def prep_kernel(patches_ref, gain_ref, nat_ref, normed_ref, normed_t_ref, perm_ref):
    build_order(nat_ref, perm_ref)
    standard, _ = norm_rows(patches_ref[...])
    normed = (standard * gain_ref[...]).astype(BF)
    normed_ref[...] = dot(normed, perm_ref[...], NT).astype(BF)
    normed_t_ref[...] = dot(perm_ref[...], normed, NT).astype(BF)


def prep(patches, gain, nat):
    return pl.pallas_call(
        prep_kernel,
        in_specs=[VM] * 3,
        out_specs=[VM] * 2,
        out_shape=[
            jax.ShapeDtypeStruct((ROWS, D), BF),
            jax.ShapeDtypeStruct((D, ROWS), BF),
        ],
        scratch_shapes=[pltpu.VMEM((D, D), BF)],
        compiler_params=params(32),
        cost_estimate=cost(4 * ROWS * D * D, 6 * ROWS * D),
        name="prep",
    )(patches, gain, nat)


def build_kernel(own_ref, w_ref, seg_ref, out_ref):
    lane = lax.broadcasted_iota(jnp.int32, (1, TILE), 1)
    owners = jnp.zeros((1, TILE), jnp.int32)
    for t in range(TILES):
        owners = jnp.where(lane == t, own_ref[t], owners)
    for d in range(N_DP):
        out_ref[d, OWN:MSG, :] = jnp.zeros((MSG - OWN, COLS), BF)
        for t in range(TILES):
            out_ref[d, OWN : OWN + 1, TILE * t : TILE * (t + 1)] = (
                seg_ref[t : t + 1, :].astype(F32).astype(BF)
            )
        out_ref[d, OWN + 1 : OWN + 2, 0:TILE] = owners.astype(F32).astype(BF)
        for a in range(3):
            start = D * a + HALF * (d % 2)
            out_ref[d, 0:OWN, HALF * a : HALF * (a + 1)] = w_ref[:, start : start + HALF]


def build(owners, weight, segments):
    return pl.pallas_call(
        build_kernel,
        in_specs=[SM, VM, VM],
        out_specs=VM,
        out_shape=jax.ShapeDtypeStruct((N_DP, MSG, COLS), BF),
        cost_estimate=cost(0, 2 * N_DP * MSG * COLS),
        name="build",
    )(owners, weight, segments)


def compact_kernel(group_ref, msg_ref, w_ref, seg_ref, own_ref):
    group = group_ref[0]
    seg_ref[...] = jnp.zeros_like(seg_ref)
    for s in range(N_DP):
        w_ref[OWN * s : OWN * (s + 1), :] = msg_ref[s, 0:OWN, :]
        own_ref[s : s + 1, :] = msg_ref[s, OWN + 1 : OWN + 2, 0:TILE].astype(F32)
    for rel in range(2):
        src = group + rel * (1 - 2 * (group % 2))
        for t in range(TILES):
            seg_ref[TILES * rel + t : TILES * rel + t + 1, :] = msg_ref[
                src, OWN : OWN + 1, TILE * t : TILE * (t + 1)
            ].astype(F32)


def compact(group, messages):
    return pl.pallas_call(
        compact_kernel,
        in_specs=[SM, VM],
        out_specs=[VM] * 3,
        out_shape=[
            jax.ShapeDtypeStruct((BLOCK, COLS), BF),
            jax.ShapeDtypeStruct((8, TILE), F32),
            jax.ShapeDtypeStruct((N_DP, TILE), F32),
        ],
        cost_estimate=cost(0, 4 * N_DP * MSG * COLS),
        name="compact",
    )(group, messages)


def pack_kernel(first_ref, second_ref, out_ref):
    out_ref[:BLOCK, :] = first_ref[...]
    out_ref[BLOCK:, :] = second_ref[...]


def pack(first, second):
    return pl.pallas_call(
        pack_kernel,
        in_specs=[VM] * 2,
        out_specs=VM,
        out_shape=jax.ShapeDtypeStruct((PART, COLS), BF),
        cost_estimate=cost(0, 4 * PART * COLS),
        name="pack",
    )(first, second)


def to_heads_kernel(fwd_ref, in_ref, out_ref):
    for d in range(N_DP):
        half = slice(HALF * (d % 2), HALF * (d % 2 + 1))
        for k in range(2 * TILES):
            u = TILES * (2 * (d // 2) + ((d % 2) ^ (k // TILES))) + k % TILES
            out_ref[d, k] = in_ref[fwd_ref[u], :, half]


def to_heads(fwd, strips):
    return pl.pallas_call(
        to_heads_kernel,
        in_specs=[SM, VM],
        out_specs=VM,
        out_shape=jax.ShapeDtypeStruct((N_DP, 2 * TILES, STRIP, HALF), BF),
        cost_estimate=cost(0, 4 * ROWS * D),
        name="to_heads",
    )(fwd, strips)


def to_owners_kernel(left_ref, right_ref, in_ref, out_ref):
    for v in range(N_DP * TILES):
        out_ref[v, :, :HALF] = in_ref[left_ref[v]]
        out_ref[v, :, HALF:] = in_ref[right_ref[v]]


def to_owners(left, right, strips):
    return pl.pallas_call(
        to_owners_kernel,
        in_specs=[SM, SM, VM],
        out_specs=VM,
        out_shape=jax.ShapeDtypeStruct((N_DP * TILES, STRIP, D), BF),
        cost_estimate=cost(0, 4 * ROWS * D),
        name="to_owners",
    )(left, right, strips)


def window_masks(i):
    lane = lax.broadcasted_iota(jnp.int32, (TILE, 256), 1)
    start = 32 * i
    first = (lane >= start) & (lane < start + HDIM)
    second = (lane >= start + HDIM) & (lane < start + 2 * HDIM)
    return first, second


def stack_heads(window, masks):
    zero = jnp.zeros_like(window)
    return jnp.concatenate([jnp.where(m, window, zero) for m in masks], axis=0)


def pick_heads(stacked, masks):
    zero = jnp.zeros((TILE, 256), F32)
    return jnp.where(
        masks[0], stacked[:TILE], jnp.where(masks[1], stacked[TILE:], zero)
    )


def halves(fn, *arrays):
    return jnp.concatenate(
        [fn(*(a[:, :TILE] for a in arrays)), fn(*(a[:, TILE:] for a in arrays))], axis=1
    )


def wide_max(a):
    return jnp.broadcast_to(jnp.max(a, axis=-1, keepdims=True), a.shape)


def wide_sum(a):
    return jnp.broadcast_to(jnp.sum(a, axis=-1, keepdims=True), a.shape)


def load_weight(pieces, weight, sems):
    start, copies = 0, []
    for b, piece in enumerate(pieces):
        n = piece.shape[0]
        copies.append(
            pltpu.make_async_copy(piece, weight.at[pl.ds(start, n)], sems.at[b])
        )
        start += n
    return copies


def columns(body):
    @pl.loop(0, 2)
    def _(n):
        body(pl.ds(pl.multiple_of(n * 768, 256), 768))

    body(pl.ds(1536, 384))


def main_kernel(
    normed_ref,
    partner_ref,
    seg_ref,
    normed_t_ref,
    partner_t_ref,
    cot_ref,
    *refs,
):
    pieces, (slots_ref, dqkv_ref), grads = refs[:8], refs[8:10], refs[10:12]
    qkv, cot, weight, normed_t, sems, w_sems, t_sem = refs[12:]
    t_copies = load_features(4, 2, (normed_t_ref, partner_t_ref), normed_t, t_sem)
    cot_copies = [
        pltpu.make_async_copy(cot_ref.at[j], cot.at[:, j], sems.at[j])
        for j in range(N_DP)
    ]
    w_copies = load_weight(pieces, weight, w_sems)
    for copy in w_copies + cot_copies + t_copies:
        copy.start()
    for copy in w_copies:
        copy.wait()

    def project(cols):
        qkv[:ROWS, cols] = dot(normed_ref[...], weight[:, cols]).astype(BF)
        qkv[ROWS:, cols] = dot(partner_ref[...], weight[:, cols]).astype(BF)

    columns(project)
    for copy in cot_copies:
        copy.wait()

    @pl.loop(0, 2 * TILES)
    def _(t):
        rows = pl.ds(pl.multiple_of(t * TILE, TILE), TILE)
        seg = jnp.broadcast_to(seg_ref[pl.ds(t, 1), :], (TILE, TILE))
        same = seg == seg.T
        same = jnp.concatenate([same, same], axis=1)
        pairs = range(4)
        masks = [window_masks(i) for i in pairs]
        windows = [slice(128 * i, 128 * i + 256) for i in pairs]

        def window(a, i):
            return qkv[rows, HALF * a + 128 * i : HALF * a + 128 * i + 256]

        q = [window(0, i) for i in pairs]
        d_out = [cot[t, :, :, windows[i]].reshape(TILE, 256) for i in pairs]
        kk = [stack_heads(window(1, i), masks[i]) for i in pairs]
        vv = [stack_heads(window(2, i), masks[i]) for i in pairs]
        scores = [dot(q[i], kk[i], NT) for i in pairs]
        d_probs = [dot(d_out[i], vv[i], NT) for i in pairs]
        scores = [jnp.where(same, x * (SCALE * LOG2E), MASKED) for x in scores]
        tops = [halves(wide_max, x) for x in scores]
        expo = [jnp.exp2(x - m) for x, m in zip(scores, tops)]
        sums = [halves(wide_sum, x) for x in expo]
        weights = [x * (1.0 / total) for x, total in zip(expo, sums)]
        rounded = [x.astype(BF) for x in weights]
        outs = [dot(rounded[i], vv[i]) for i in pairs]
        dvs = [dot(rounded[i], d_out[i], TN) for i in pairs]
        inner = [halves(wide_sum, d_probs[i] * weights[i]) for i in pairs]
        d_scores = [
            (weights[i] * (d_probs[i] - inner[i]) * SCALE).astype(BF) for i in pairs
        ]
        dqs = [dot(d_scores[i], kk[i]) for i in pairs]
        dks = [dot(d_scores[i], q[i], TN) for i in pairs]
        dks = [pick_heads(dks[i], masks[i]) for i in pairs]
        dvs = [pick_heads(dvs[i], masks[i]) for i in pairs]

        def lanes(vals):
            parts = [vals[0][:, :TILE]]
            for i in range(3):
                parts.append(vals[i][:, TILE:] + vals[i + 1][:, :TILE])
            parts.append(vals[3][:, TILE:])
            return jnp.concatenate([p.astype(BF) for p in parts], axis=1)

        out = lanes(outs)
        for j in range(N_DP):
            slots_ref[j, t] = out[STRIP * j : STRIP * (j + 1)]
        for a, vals in enumerate((dqs, dks, dvs)):
            dqkv_ref[rows, HALF * a : HALF * (a + 1)] = lanes(vals)

    for copy in t_copies:
        copy.wait()
    columns(functools.partial(gradient, normed_t, dqkv_ref, grads, ()))


def load_features(first, count, refs, normed_t, sems):
    return [
        pltpu.make_async_copy(
            ref.at[pl.ds(first * PART, count * PART)],
            normed_t.at[:, pl.ds(ROWS * h, ROWS)],
            sems.at[h],
        )
        for h, ref in enumerate(refs)
    ]


def gradient(normed_t, dqkv_ref, outs, arrived, cols):
    for n, out in enumerate(outs):
        part = dot(normed_t[PART * n : PART * (n + 1), :], dqkv_ref[:, cols])
        if arrived:
            part = part + arrived[n][:, cols].astype(F32)
        out[:, cols] = part.astype(BF)


def main(normed, seg, normed_t, cot, pieces):
    return pl.pallas_call(
        main_kernel,
        in_specs=[VM] * 3 + [ANY] * 3 + [ANY] * PIECES,
        out_specs=[VM] * 4,
        out_shape=[
            jax.ShapeDtypeStruct((N_DP, 2 * TILES, STRIP, HALF), BF),
            jax.ShapeDtypeStruct((PAIR_ROWS, COLS), BF),
        ]
        + [jax.ShapeDtypeStruct((PART, COLS), BF)] * 2,
        scratch_shapes=[
            pltpu.VMEM((PAIR_ROWS, COLS), BF),
            pltpu.VMEM((2 * TILES, N_DP, STRIP, HALF), BF),
            pltpu.VMEM((D, COLS), BF),
            pltpu.VMEM((2 * PART, PAIR_ROWS), BF),
            pltpu.SemaphoreType.DMA((N_DP,)),
            pltpu.SemaphoreType.DMA((PIECES,)),
            pltpu.SemaphoreType.DMA((2,)),
        ],
        compiler_params=params(58),
        cost_estimate=cost(8 * 10**9, 20 * 2**20, 10**6),
        name="main",
    )(*normed, seg, *normed_t, cot, *pieces)


def grads_kernel(firsts, normed_t_ref, partner_t_ref, dqkv_ref, *refs):
    arrived, outs, (normed_t, sems) = refs[:-4], refs[-4:-2], refs[-2:]
    copies = []
    for n, first in enumerate(firsts):
        copies += load_features(
            first,
            1,
            (normed_t_ref, partner_t_ref),
            normed_t.at[pl.ds(PART * n, PART)],
            sems.at[n],
        )
    for copy in copies:
        copy.start()
    for copy in copies:
        copy.wait()
    columns(functools.partial(gradient, normed_t, dqkv_ref, outs, arrived))


def grads(firsts, normed_t, dqkv, arrived=()):
    return pl.pallas_call(
        functools.partial(grads_kernel, firsts),
        in_specs=[ANY, ANY, VM] + [VM] * len(arrived),
        out_specs=[VM] * 2,
        out_shape=[jax.ShapeDtypeStruct((PART, COLS), BF)] * 2,
        scratch_shapes=[
            pltpu.VMEM((2 * PART, PAIR_ROWS), BF),
            pltpu.SemaphoreType.DMA((2, 2)),
        ],
        compiler_params=params(32),
        cost_estimate=cost(4 * PART * PAIR_ROWS * COLS, 5 * 2**20),
        name="grads",
    )(*normed_t, dqkv, *arrived)


def back_kernel(dqkv_ref, nat_ref, *refs):
    pieces, (out_ref, weight, perm_ref, sems) = refs[:PIECES], refs[PIECES:]
    copies = load_weight(pieces, weight, sems)
    for copy in copies:
        copy.start()
    build_order(nat_ref, perm_ref)
    for copy in copies:
        copy.wait()
    for half in (1, 0):
        rows = slice(ROWS * half, ROWS * (half + 1))
        d_normed = dot(dqkv_ref[rows, :], weight[...], NT).astype(BF)
        out_ref[half] = dot(d_normed, perm_ref[...]).astype(BF)


def back(dqkv, pieces, nat):
    return pl.pallas_call(
        back_kernel,
        in_specs=[VM, VM] + [ANY] * PIECES,
        out_specs=VM,
        out_shape=jax.ShapeDtypeStruct((2, ROWS, D), BF),
        scratch_shapes=[
            pltpu.VMEM((D, COLS), BF),
            pltpu.VMEM((D, D), BF),
            pltpu.SemaphoreType.DMA((PIECES,)),
        ],
        compiler_params=params(48),
        cost_estimate=cost(2 * PAIR_ROWS * D * (D + COLS), 15 * 2**20),
        name="back",
    )(dqkv, nat, *pieces)


def rows_kernel(patches_ref, gain_ref, mine_ref, other_ref, out_ref, gain_grad_ref):
    standard, inv_std = norm_rows(patches_ref[...])
    d_normed = mine_ref[...].astype(F32) + other_ref[...].astype(F32)
    scaled = d_normed * gain_ref[...]
    back_rows = inv_std * (
        scaled
        - jnp.mean(scaled, axis=-1, keepdims=True)
        - standard * jnp.mean(scaled * standard, axis=-1, keepdims=True)
    )
    out_ref[...] = back_rows.astype(BF)
    part = jnp.sum(d_normed * standard, axis=0, keepdims=True)

    @pl.when(pl.program_id(0) == 0)
    def _():
        gain_grad_ref[...] = jnp.zeros_like(gain_grad_ref)

    for k in range(D // TILE):
        gain_grad_ref[0, k : k + 1, :] += part[:, TILE * k : TILE * (k + 1)]

    @pl.when(pl.program_id(0) == TILES - 1)
    def _():
        for m in range(1, N_INNER):
            gain_grad_ref[m] = gain_grad_ref[0]


def rows_back(patches, gain, mine, other):
    block = pl.BlockSpec((TILE, D), lambda i: (i, 0))
    one = pl.BlockSpec((1, D), lambda i: (0, 0))
    return pl.pallas_call(
        rows_kernel,
        grid=(TILES,),
        in_specs=[block, one, block, block],
        out_specs=[block, pl.BlockSpec((N_INNER, MSG, TILE), lambda i: (0, 0, 0))],
        out_shape=[
            jax.ShapeDtypeStruct((ROWS, D), BF),
            jax.ShapeDtypeStruct((N_INNER, MSG, TILE), F32),
        ],
        compiler_params=params(48),
        cost_estimate=cost(20 * ROWS * D, 8 * ROWS * D),
        name="rows_back",
    )(patches, gain, mine, other)


def split_kernel(rows_ref, one_ref, two_ref, three_ref, gain_ref, out_ref):
    gain = gain_ref[0]
    for m in range(1, N_INNER):
        gain = gain + gain_ref[m]
    hi = gain.astype(BF).astype(F32)
    lo = gain - hi
    total = rows_ref[...].astype(F32)
    for ref in (one_ref, two_ref, three_ref):
        total = total + ref[...].astype(F32)
    total = total.astype(BF)
    for s in range(N_DP):
        out_ref[s, 0:OWN, :] = total[OWN * s : OWN * (s + 1)]
        out_ref[s, OWN:MSG, :] = jnp.zeros((MSG - OWN, COLS), BF)
        for k in range(D // TILE):
            cols = slice(TILE * k, TILE * (k + 1))
            out_ref[s, OWN : OWN + 1, cols] = hi[k : k + 1].astype(BF)
            out_ref[s, OWN + 1 : OWN + 2, cols] = lo[k : k + 1].astype(BF)


def split(rows, others, gain):
    return pl.pallas_call(
        split_kernel,
        in_specs=[VM] * 5,
        out_specs=VM,
        out_shape=jax.ShapeDtypeStruct((N_DP, MSG, COLS), BF),
        cost_estimate=cost(0, 4 * N_DP * MSG * COLS),
        name="split",
    )(rows, *others, gain)


def finish_kernel(msg_ref, out_ref, gain_ref):
    both = jnp.zeros((MSG, COLS), F32)
    for half in range(2):
        total = msg_ref[half].astype(F32)
        for chip in range(1, 4):
            total = total + msg_ref[2 * chip + half].astype(F32)
        both = both + total
        for a in range(3):
            start = D * a + HALF * half
            out_ref[:, start : start + HALF] = total[0:OWN, HALF * a : HALF * (a + 1)]
    gain_ref[...] = both[OWN : OWN + 1, :D] + both[OWN + 1 : OWN + 2, :D]


def finish(messages):
    return pl.pallas_call(
        finish_kernel,
        in_specs=[VM],
        out_specs=[VM, VM],
        out_shape=[
            jax.ShapeDtypeStruct((OWN, 3 * D), F32),
            jax.ShapeDtypeStruct((1, D), F32),
        ],
        cost_estimate=cost(0, 6 * N_DP * MSG * COLS),
        name="finish",
    )(messages)


def ring_pairs(df, ds):
    pairs = []
    for d in range(N_DP):
        dx, dz = (ds, df) if d % 2 else (df, ds)
        for x in range(4):
            for z in range(4):
                src = 4 * ((x + dx) % 4) + (z + dz) % 4
                pairs.append((N_INNER * d + src, N_INNER * d + 4 * x + z))
    return pairs


def from_ring(value, df, ds):
    return lax.ppermute(value, ("dp", "inner"), ring_pairs(df, ds))


def swap_cores(value):
    return lax.ppermute(value, "dp", [(d ^ 1, d) for d in range(N_DP)])


def exchange(value, axis="dp"):
    return lax.all_to_all(value, axis, split_axis=0, concat_axis=0, tiled=True)


def add(*arrays):
    return sum(a.astype(F32) for a in arrays).astype(BF)


def on_device(patches, segments, owners, norm_gain, qkv_weight, cotangent):
    group = lax.axis_index("dp")
    inner = lax.axis_index("inner")
    core, x, z = group % 2, inner // 4, inner % 4
    gain = norm_gain.reshape(1, D)

    messages = exchange(build(owners, qkv_weight, segments))
    block, seg, owners_all = compact(group.reshape(1).astype(jnp.int32), messages)
    partner_patches = swap_cores(patches)

    ring = [block] + [from_ring(block, f, 0) for f in (1, 2, 3)]
    near_a, near_b = pack(ring[0], ring[1]), pack(ring[2], ring[3])
    above_a, below_b = from_ring(near_a, 0, 1), from_ring(near_b, 0, -1)
    above_b, below_a = from_ring(near_b, 0, 1), from_ring(near_a, 0, -1)
    far_a, far_b = from_ring(above_a, 0, 1), from_ring(below_b, 0, -1)
    pieces = [near_a, near_b, above_a, above_b, far_a, far_b, below_a, below_b]

    pos = jnp.arange(N_INNER)
    df, ds = pos % 4, pos // 4
    m = 4 * ((x + jnp.where(core == 0, df, ds)) % 4) + (
        z + jnp.where(core == 0, ds, df)
    ) % 4
    nat = (
        (jnp.arange(N_DP)[None, :, None] * N_INNER + m[:, None, None]) * OWN
        + jnp.arange(OWN)[None, None, :]
    ).reshape(D, 1)
    normed, normed_t = zip(prep(patches, gain, nat), prep(partner_patches, gain, nat))

    owner_of = owners_all[:, :TILES].astype(jnp.int32).reshape(N_DP * TILES)
    u = jnp.arange(N_DP * TILES)
    earlier = (owner_of[:, None] == owner_of[None, :]) & (
        u[None, :] // TILES < u[:, None] // TILES
    )
    fwd = (TILES * owner_of + jnp.sum(earlier, axis=1)).astype(jnp.int32)
    inv = jnp.sum(jnp.where(fwd[None, :] == u[:, None], u[None, :], 0), axis=1)
    chip, odd, t = inv // (2 * TILES), inv // TILES % 2, inv % TILES
    left = (2 * chip * 2 * TILES + odd * TILES + t).astype(jnp.int32)
    right = ((2 * chip + 1) * 2 * TILES + (1 - odd) * TILES + t).astype(jnp.int32)

    strips = exchange(
        cotangent.reshape(TILES, N_DP, STRIP, D).transpose(1, 0, 2, 3)
    )
    cot = exchange(to_heads(fwd, strips.reshape(N_DP * TILES, STRIP, D)))

    out, dqkv, far_up, far_down = main(normed, seg, normed_t, cot, pieces)

    arrived_up, arrived_down = from_ring(far_up, 0, -1), from_ring(far_down, 0, 1)
    up_b, down_a = grads((3, 6), normed_t, dqkv)
    from_up_b, from_down_a = from_ring(up_b, 0, -1), from_ring(down_a, 0, 1)
    column_a, column_b = grads((0, 1), normed_t, dqkv)
    up_a, down_b = grads((2, 7), normed_t, dqkv, (arrived_up, arrived_down))
    from_up_a, from_down_b = from_ring(up_a, 0, -1), from_ring(down_b, 0, 1)
    column_b = add(column_b, from_up_b, from_down_b)
    two, three = column_b[:BLOCK], column_b[BLOCK:]
    column_a = add(column_a, from_up_a, from_down_a)
    zero, one = column_a[:BLOCK], column_a[BLOCK:]
    others = [from_ring(two, -2, 0), from_ring(three, 1, 0), from_ring(one, -1, 0)]

    out = exchange(out)
    out = to_owners(left, right, out.reshape(N_DP * 2 * TILES, STRIP, HALF))
    out = exchange(out.reshape(N_DP, TILES, STRIP, D))
    attended = out.transpose(1, 0, 2, 3).reshape(ROWS, D)

    dqkv_later, _, _ = lax.optimization_barrier((dqkv, up_a, down_b))
    d_normed = back(dqkv_later, pieces, nat)
    from_partner = swap_cores(d_normed[1])
    grad_rows, gain_part = rows_back(patches, gain, d_normed[0], from_partner)
    gain_parts = exchange(gain_part, "inner")

    grad_qkv, grad_gain = finish(exchange(split(zero, others, gain_parts)))
    return (attended, grad_rows, grad_qkv, grad_gain.reshape(D))


def solution(mesh):
    both = ("dp", "inner")
    placed = (
        P(both, None),
        P(both, None),
        P(both),
        P(),
        P(both, None),
        P(both, None),
    )
    return jax.shard_map(
        on_device,
        mesh=mesh,
        in_specs=placed,
        out_specs=(P(both, None), P(both, None), P(both, None), P()),
        check_vma=False,
    )
```

```python
import functools

import jax
import jax.numpy as jnp
from jax import lax
from jax.experimental import pallas as pl
from jax.experimental.pallas import tpu as pltpu
from jax.sharding import PartitionSpec as P

D = 1280
HEADS = 16
HDIM = 80
TILE = 128
TILES = 3
N_DP = 8
N_INNER = 16
ROWS = TILES * TILE
PAIR_ROWS = 2 * ROWS
HALF = D // 2
COLS = 3 * HALF
OWN = 10
BLOCK = 80
PART = 160
PIECES = 8
STRIP = 16
MSG = 16
EPS = 1e-6
MASKED = -1e30
SCALE = HDIM ** (-0.5)
LOG2E = 1.4426950408889634
BF = jnp.bfloat16
F32 = jnp.float32
VM = pl.BlockSpec(memory_space=pltpu.VMEM)
SM = pl.BlockSpec(memory_space=pltpu.SMEM)
ANY = pl.BlockSpec(memory_space=pltpu.HBM)
NT = (((1,), (1,)), ((), ()))
TN = (((0,), (0,)), ((), ()))
NN = (((1,), (0,)), ((), ()))


def params(mib, **more):
    return pltpu.CompilerParams(vmem_limit_bytes=mib * 2**20, **more)


def cost(flops, nbytes, trans=0):
    return pl.CostEstimate(
        flops=flops // 1000, bytes_accessed=nbytes // 1000, transcendentals=trans // 1000
    )


def dot(a, b, dims=NN):
    return lax.dot_general(a, b, dims, preferred_element_type=F32)


def norm_rows(rows):
    wide = rows.astype(F32)
    centred = wide - jnp.mean(wide, axis=-1, keepdims=True)
    variance = jnp.mean(centred * centred, axis=-1, keepdims=True)
    inv_std = lax.rsqrt(variance + EPS)
    return centred * inv_std, inv_std


def build_order(nat_ref, perm_ref):
    for r in range(D // TILE):
        rows = slice(TILE * r, TILE * (r + 1))
        column = jnp.broadcast_to(nat_ref[:, rows], (TILE, TILE)).T
        for a in range(D // TILE):
            feature = lax.broadcasted_iota(jnp.int32, (TILE, TILE), 1) + TILE * a
            hit = column == feature.astype(F32)
            perm_ref[rows, TILE * a : TILE * (a + 1)] = jnp.where(hit, 1.0, 0.0).astype(BF)


def prep_kernel(patches_ref, gain_ref, nat_ref, normed_ref, normed_t_ref, perm_ref):
    build_order(nat_ref, perm_ref)
    standard, _ = norm_rows(patches_ref[...])
    normed = (standard * gain_ref[...]).astype(BF)
    normed_ref[...] = dot(normed, perm_ref[...], NT).astype(BF)
    normed_t_ref[...] = dot(perm_ref[...], normed, NT).astype(BF)


def prep(patches, gain, nat):
    return pl.pallas_call(
        prep_kernel,
        in_specs=[VM] * 3,
        out_specs=[VM] * 2,
        out_shape=[
            jax.ShapeDtypeStruct((ROWS, D), BF),
            jax.ShapeDtypeStruct((D, ROWS), BF),
        ],
        scratch_shapes=[pltpu.VMEM((D, D), BF)],
        compiler_params=params(58),
        cost_estimate=cost(4 * ROWS * D * D, 6 * ROWS * D),
        name="prep",
    )(patches, gain, nat)


def build_kernel(core_ref, own_ref, w_ref, seg_ref, same_ref, other_ref):
    swap = core_ref[0] == 1
    lane = lax.broadcasted_iota(jnp.int32, (1, TILE), 1)
    owners = jnp.zeros((1, TILE), jnp.int32)
    for t in range(TILES):
        owners = jnp.where(lane == t, own_ref[t], owners)
    for out in (same_ref, other_ref):
        out[OWN:MSG, :] = jnp.zeros((MSG - OWN, COLS), BF)
        for t in range(TILES):
            out[OWN : OWN + 1, TILE * t : TILE * (t + 1)] = (
                seg_ref[t : t + 1, :].astype(F32).astype(BF)
            )
        out[OWN + 1 : OWN + 2, 0:TILE] = owners.astype(F32).astype(BF)
    for a in range(3):
        first = w_ref[:, D * a : D * a + HALF].astype(F32)
        second = w_ref[:, D * a + HALF : D * (a + 1)].astype(F32)
        cols = slice(HALF * a, HALF * (a + 1))
        same_ref[0:OWN, cols] = jnp.where(swap, second, first).astype(BF)
        other_ref[0:OWN, cols] = jnp.where(swap, first, second).astype(BF)


def build(core, owners, weight, segments):
    return pl.pallas_call(
        build_kernel,
        in_specs=[SM, SM, VM, VM],
        out_specs=[VM, VM],
        out_shape=[jax.ShapeDtypeStruct((MSG, COLS), BF)] * 2,
        compiler_params=params(12),
        cost_estimate=cost(0, 8 * MSG * COLS),
        name="build",
    )(core, owners, weight, segments)


def compact_kernel(*refs):
    messages, (w_ref, seg_ref, own_ref) = refs[:N_DP], refs[N_DP:]
    seg_ref[...] = jnp.zeros_like(seg_ref)
    for s, msg_ref in enumerate(messages):
        w_ref[OWN * s : OWN * (s + 1), :] = msg_ref[0:OWN, :]
        own_ref[s : s + 1, :] = msg_ref[OWN + 1 : OWN + 2, 0:TILE].astype(F32)
    for rel in range(2):
        for t in range(TILES):
            seg_ref[TILES * rel + t : TILES * rel + t + 1, :] = messages[rel][
                OWN : OWN + 1, TILE * t : TILE * (t + 1)
            ].astype(F32)


def compact(messages):
    return pl.pallas_call(
        compact_kernel,
        in_specs=[VM] * N_DP,
        out_specs=[VM] * 3,
        out_shape=[
            jax.ShapeDtypeStruct((BLOCK, COLS), BF),
            jax.ShapeDtypeStruct((8, TILE), F32),
            jax.ShapeDtypeStruct((N_DP, TILE), F32),
        ],
        compiler_params=params(12),
        cost_estimate=cost(0, 4 * N_DP * MSG * COLS),
        name="compact",
    )(*messages)


def pack_kernel(first_ref, second_ref, out_ref):
    out_ref[:BLOCK, :] = first_ref[...]
    out_ref[BLOCK:, :] = second_ref[...]


def pack(first, second):
    return pl.pallas_call(
        pack_kernel,
        in_specs=[VM] * 2,
        out_specs=VM,
        out_shape=jax.ShapeDtypeStruct((PART, COLS), BF),
        cost_estimate=cost(0, 4 * PART * COLS),
        compiler_params=params(12),
        name="pack",
    )(first, second)


def to_heads_kernel(fwd_ref, in_ref, out_ref):
    for d in range(N_DP):
        half = slice(HALF * (d % 2), HALF * (d % 2 + 1))
        for k in range(2 * TILES):
            u = TILES * (2 * (d // 2) + ((d % 2) ^ (k // TILES))) + k % TILES
            out_ref[d, k] = in_ref[fwd_ref[u], :, half]


def to_heads(fwd, strips):
    return pl.pallas_call(
        to_heads_kernel,
        in_specs=[SM, VM],
        out_specs=VM,
        out_shape=jax.ShapeDtypeStruct((N_DP, 2 * TILES, STRIP, HALF), BF),
        cost_estimate=cost(0, 4 * ROWS * D),
        compiler_params=params(12),
        name="to_heads",
    )(fwd, strips)


def place_kernel(idx_ref, left_ref, right_ref, out_ref):
    out_ref[0, :, :HALF] = left_ref[0, 0]
    out_ref[0, :, HALF:] = right_ref[0, 0]


def place(index, slots):
    def half(c):
        return pl.BlockSpec(
            (1, 1, TILE, HALF), lambda p, g: (g[p] + c, g[TILES + p], 0, 0)
        )

    spec = pltpu.PrefetchScalarGridSpec(
        num_scalar_prefetch=1,
        grid=(TILES,),
        in_specs=[half(0), half(1)],
        out_specs=pl.BlockSpec((1, TILE, D), lambda p, g: (p, 0, 0)),
    )
    return pl.pallas_call(
        place_kernel,
        grid_spec=spec,
        out_shape=jax.ShapeDtypeStruct((TILES, TILE, D), BF),
        compiler_params=params(12),
        cost_estimate=cost(0, 4 * ROWS * D),
        name="place",
    )(index, slots, slots)


def window_masks(i):
    lane = lax.broadcasted_iota(jnp.int32, (TILE, 256), 1)
    start = 32 * i
    first = (lane >= start) & (lane < start + HDIM)
    second = (lane >= start + HDIM) & (lane < start + 2 * HDIM)
    return first, second


def stack_heads(window, masks):
    zero = jnp.zeros_like(window)
    return jnp.concatenate([jnp.where(m, window, zero) for m in masks], axis=0)


def pick_heads(stacked, masks):
    zero = jnp.zeros((TILE, 256), F32)
    return jnp.where(
        masks[0], stacked[:TILE], jnp.where(masks[1], stacked[TILE:], zero)
    )


def halves(fn, *arrays):
    return jnp.concatenate(
        [fn(*(a[:, :TILE] for a in arrays)), fn(*(a[:, TILE:] for a in arrays))], axis=1
    )


def wide_max(a):
    return jnp.broadcast_to(jnp.max(a, axis=-1, keepdims=True), a.shape)


def wide_sum(a):
    return jnp.broadcast_to(jnp.sum(a, axis=-1, keepdims=True), a.shape)


CHUNKS = [pl.ds(0, 768), pl.ds(768, 768), pl.ds(1536, 384)]


def start(copies):
    for copy in copies:
        copy.start()


def wait(copies):
    for copy in copies:
        copy.wait()


def load_weight(pieces, weight, sems):
    return [
        [
            pltpu.make_async_copy(
                piece.at[:, cols],
                weight.at[pl.ds(PART * b, PART), cols],
                sems.at[n, b],
            )
            for b, piece in enumerate(pieces)
        ]
        for n, cols in enumerate(CHUNKS)
    ]


def load_rows(refs, rows, sems):
    return [
        pltpu.make_async_copy(ref, rows.at[pl.ds(ROWS * h, ROWS)], sems.at[h])
        for h, ref in enumerate(refs)
    ]


def load_features(refs, normed_t, sems):
    return [
        pltpu.make_async_copy(ref, normed_t.at[:, pl.ds(ROWS * h, ROWS)], sems.at[h])
        for h, ref in enumerate(refs)
    ]


def gradient(normed_t, dqkv, outs, staged, sems):
    copies = []
    for c, cols in enumerate(CHUNKS):
        for n in range(0, PIECES, 2):
            both = dot(normed_t[PART * n : PART * (n + 2), :], dqkv[:, cols]).astype(BF)
            for k in (n, n + 1):
                staged[k, :, cols] = both[PART * (k - n) : PART * (k - n + 1)]
                copies.append(
                    pltpu.make_async_copy(
                        staged.at[k, :, cols], outs[k].at[:, cols], sems.at[c, k]
                    )
                )
                copies[-1].start()
    wait(copies)


def main_kernel(
    idx_ref,
    seg_ref,
    normed_ref,
    partner_ref,
    normed_t_ref,
    partner_t_ref,
    cot_ref,
    *refs,
):
    pieces, slots_ref, dqkv_ref = refs[:PIECES], refs[PIECES], refs[PIECES + 1]
    grads = refs[PIECES + 2 : 2 * PIECES + 2]
    (
        normed,
        qkv,
        cot,
        weight,
        normed_t,
        dqkv,
        out_tiles,
        staged,
        row_sems,
        cot_sems,
        w_sems,
        t_sems,
        slot_sems,
        dqkv_sems,
        grad_sems,
    ) = refs[2 * PIECES + 2 :]
    row_copies = load_rows((normed_ref, partner_ref), normed, row_sems)
    w_copies = load_weight(pieces, weight, w_sems)
    cot_copies = [
        pltpu.make_async_copy(cot_ref.at[j], cot.at[:, j], cot_sems.at[j])
        for j in range(N_DP)
    ]
    t_copies = load_features((normed_t_ref, partner_t_ref), normed_t, t_sems)
    start(row_copies)
    for copies in w_copies:
        start(copies)
    start(cot_copies)
    start(t_copies)
    wait(row_copies)
    for c, cols in enumerate(CHUNKS):
        wait(w_copies[c])
        qkv[:, cols] = dot(normed[...], weight[:, cols]).astype(BF)
    wait(cot_copies)

    def leave(t):
        rows = pl.ds(pl.multiple_of(t * TILE, TILE), TILE)
        return [
            pltpu.make_async_copy(
                out_tiles.at[t],
                slots_ref.at[idx_ref[t], idx_ref[2 * TILES + t]],
                slot_sems.at[t],
            ),
            pltpu.make_async_copy(dqkv.at[rows], dqkv_ref.at[rows], dqkv_sems.at[t]),
        ]

    @pl.loop(0, 2 * TILES)
    def _(t):
        rows = pl.ds(pl.multiple_of(t * TILE, TILE), TILE)
        seg = jnp.broadcast_to(seg_ref[pl.ds(t, 1), :], (TILE, TILE))
        same = seg == seg.T
        same = jnp.concatenate([same, same], axis=1)
        pairs = range(4)
        masks = [window_masks(i) for i in pairs]
        windows = [slice(128 * i, 128 * i + 256) for i in pairs]

        def window(a, i):
            return qkv[rows, HALF * a + 128 * i : HALF * a + 128 * i + 256]

        q = [window(0, i) for i in pairs]
        d_out = [cot[t, :, :, windows[i]].reshape(TILE, 256) for i in pairs]
        kk = [stack_heads(window(1, i), masks[i]) for i in pairs]
        vv = [stack_heads(window(2, i), masks[i]) for i in pairs]
        scores = [dot(q[i], kk[i], NT) for i in pairs]
        d_probs = [dot(d_out[i], vv[i], NT) for i in pairs]
        scores = [jnp.where(same, x * (SCALE * LOG2E), MASKED) for x in scores]
        tops = [halves(wide_max, x) for x in scores]
        expo = [jnp.exp2(x - m) for x, m in zip(scores, tops)]
        sums = [halves(wide_sum, x) for x in expo]
        weights = [x * (1.0 / total) for x, total in zip(expo, sums)]
        rounded = [x.astype(BF) for x in weights]
        outs = [dot(rounded[i], vv[i]) for i in pairs]
        dvs = [dot(rounded[i], d_out[i], TN) for i in pairs]
        inner = [halves(wide_sum, d_probs[i] * weights[i]) for i in pairs]
        d_scores = [
            (weights[i] * (d_probs[i] - inner[i]) * SCALE).astype(BF) for i in pairs
        ]
        dqs = [dot(d_scores[i], kk[i]) for i in pairs]
        dks = [dot(d_scores[i], q[i], TN) for i in pairs]
        dks = [pick_heads(dks[i], masks[i]) for i in pairs]
        dvs = [pick_heads(dvs[i], masks[i]) for i in pairs]

        def lanes(vals):
            parts = [vals[0][:, :TILE]]
            for i in range(3):
                parts.append(vals[i][:, TILE:] + vals[i + 1][:, :TILE])
            parts.append(vals[3][:, TILE:])
            return jnp.concatenate([p.astype(BF) for p in parts], axis=1)

        out_tiles[t] = lanes(outs)
        for a, vals in enumerate((dqs, dks, dvs)):
            dqkv[rows, HALF * a : HALF * (a + 1)] = lanes(vals)
        start(leave(t))

    wait(t_copies)
    gradient(normed_t, dqkv, grads, staged, grad_sems)
    for t in range(2 * TILES):
        wait(leave(t))


def main(index, seg, normed, normed_t, cot, pieces):
    return pl.pallas_call(
        main_kernel,
        in_specs=[SM, VM] + [ANY] * (5 + PIECES),
        out_specs=[ANY] * (2 + PIECES),
        out_shape=[
            jax.ShapeDtypeStruct((N_DP, 2, TILE, HALF), BF),
            jax.ShapeDtypeStruct((PAIR_ROWS, COLS), BF),
        ]
        + [jax.ShapeDtypeStruct((PART, COLS), BF)] * PIECES,
        scratch_shapes=[
            pltpu.VMEM((PAIR_ROWS, D), BF),
            pltpu.VMEM((PAIR_ROWS, COLS), BF),
            pltpu.VMEM((2 * TILES, N_DP, STRIP, HALF), BF),
            pltpu.VMEM((D, COLS), BF),
            pltpu.VMEM((D, PAIR_ROWS), BF),
            pltpu.VMEM((PAIR_ROWS, COLS), BF),
            pltpu.VMEM((2 * TILES, TILE, HALF), BF),
            pltpu.VMEM((PIECES, PART, COLS), BF),
            pltpu.SemaphoreType.DMA((2,)),
            pltpu.SemaphoreType.DMA((N_DP,)),
            pltpu.SemaphoreType.DMA((len(CHUNKS), PIECES)),
            pltpu.SemaphoreType.DMA((2,)),
            pltpu.SemaphoreType.DMA((2 * TILES,)),
            pltpu.SemaphoreType.DMA((2 * TILES,)),
            pltpu.SemaphoreType.DMA((len(CHUNKS), PIECES)),
        ],
        compiler_params=params(58),
        cost_estimate=cost(8 * 10**9, 20 * 2**20, 10**6),
        name="main",
    )(index, seg, *normed, *normed_t, cot, *pieces)


def add_kernel(counts, cuts, *refs):
    outs, used = refs[sum(counts) :], 0
    for n, count in enumerate(counts):
        total = refs[used][...].astype(F32)
        for k in range(1, count):
            total = total + refs[used + k][...].astype(F32)
        used += count
        size = PART // cuts
        for k in range(cuts):
            outs[cuts * n + k][...] = total[size * k : size * (k + 1)].astype(BF)


def add(groups, cuts=1):
    arrays = [a for group in groups for a in group]
    shape = jax.ShapeDtypeStruct((PART // cuts, COLS), BF)
    return pl.pallas_call(
        functools.partial(add_kernel, [len(group) for group in groups], cuts),
        in_specs=[VM] * len(arrays),
        out_specs=[VM] * (cuts * len(groups)),
        out_shape=[shape] * (cuts * len(groups)),
        compiler_params=params(12),
        cost_estimate=cost(0, 4 * len(arrays) * PART * COLS),
        name="add",
    )(*arrays)


def back_kernel(
    nat_ref, gain_ref, dqkv_ref, normed_ref, partner_ref, *refs
):
    pieces, outs, gain_grad_ref = refs[:PIECES], refs[PIECES : PIECES + 2], refs[PIECES + 2]
    weight, perm_ref, dqkv, normed, w_sems, q_sems, row_sems = refs[PIECES + 3 :]
    w_copies = load_weight(pieces, weight, w_sems)
    q_copies = [
        pltpu.make_async_copy(
            dqkv_ref.at[pl.ds(ROWS * h, ROWS)], dqkv.at[pl.ds(ROWS * h, ROWS)], q_sems.at[h]
        )
        for h in range(2)
    ]
    row_copies = load_rows((normed_ref, partner_ref), normed, row_sems)
    start(q_copies)
    for copies in w_copies:
        start(copies)
    start(row_copies)
    build_order(nat_ref, perm_ref)
    wait(q_copies)
    for copies in w_copies:
        wait(copies)
    wait(row_copies)
    total = jnp.zeros((1, D), F32)
    for half in (1, 0):
        rows = slice(ROWS * half, ROWS * (half + 1))
        d_normed = dot(dqkv[rows, :], weight[...], NT)
        total = total + jnp.sum(
            d_normed * normed[rows, :].astype(F32), axis=0, keepdims=True
        )
        outs[half][...] = dot(d_normed.astype(BF), perm_ref[...]).astype(BF)
    terms, rest = [], total
    for _ in range(3):
        term = rest.astype(BF)
        rest = rest - term.astype(F32)
        terms.append(jnp.broadcast_to(term.astype(F32), (MSG, D)).astype(BF))
    part = sum(dot(term, perm_ref[...]) for term in terms)[0:1] / gain_ref[...]
    gain_grad_ref[...] = jnp.zeros_like(gain_grad_ref)
    for k in range(D // TILE):
        gain_grad_ref[k : k + 1, :] = part[:, TILE * k : TILE * (k + 1)]


def back(dqkv, pieces, nat, gain, normed):
    return pl.pallas_call(
        back_kernel,
        in_specs=[VM] * 2 + [ANY] * (3 + PIECES),
        out_specs=[VM] * 3,
        out_shape=[jax.ShapeDtypeStruct((ROWS, D), BF)] * 2
        + [jax.ShapeDtypeStruct((MSG, TILE), F32)],
        scratch_shapes=[
            pltpu.VMEM((D, COLS), BF),
            pltpu.VMEM((D, D), BF),
            pltpu.VMEM((PAIR_ROWS, COLS), BF),
            pltpu.VMEM((PAIR_ROWS, D), BF),
            pltpu.SemaphoreType.DMA((len(CHUNKS), PIECES)),
            pltpu.SemaphoreType.DMA((2,)),
            pltpu.SemaphoreType.DMA((2,)),
        ],
        compiler_params=params(58),
        cost_estimate=cost(2 * PAIR_ROWS * D * (D + COLS), 15 * 2**20),
        name="back",
    )(nat, gain, dqkv, *normed, *pieces)


def rows_kernel(patches_ref, gain_ref, mine_ref, other_ref, out_ref):
    standard, inv_std = norm_rows(patches_ref[...])
    d_normed = mine_ref[...].astype(F32) + other_ref[...].astype(F32)
    scaled = d_normed * gain_ref[...]
    back_rows = inv_std * (
        scaled
        - jnp.mean(scaled, axis=-1, keepdims=True)
        - standard * jnp.mean(scaled * standard, axis=-1, keepdims=True)
    )
    out_ref[...] = back_rows.astype(BF)


def rows_back(patches, gain, mine, other):
    block = pl.BlockSpec((TILE, D), lambda i: (i, 0))
    return pl.pallas_call(
        rows_kernel,
        grid=(TILES,),
        in_specs=[block, pl.BlockSpec((1, D), lambda i: (0, 0)), block, block],
        out_specs=block,
        out_shape=jax.ShapeDtypeStruct((ROWS, D), BF),
        compiler_params=params(58),
        cost_estimate=cost(20 * ROWS * D, 8 * ROWS * D),
        name="rows_back",
    )(patches, gain, mine, other)


def split_kernel(rows_ref, one_ref, two_ref, three_ref, gain_ref, *out_refs):
    gain = gain_ref[...]
    hi = gain.astype(BF).astype(F32)
    lo = gain - hi
    total = rows_ref[...].astype(F32)
    for ref in (one_ref, two_ref, three_ref):
        total = total + ref[...].astype(F32)
    total = total.astype(BF)
    for s, out_ref in enumerate(out_refs):
        out_ref[0:OWN, :] = total[OWN * s : OWN * (s + 1)]
        out_ref[OWN:MSG, :] = jnp.zeros((MSG - OWN, COLS), BF)
        for k in range(D // TILE):
            cols = slice(TILE * k, TILE * (k + 1))
            out_ref[OWN : OWN + 1, cols] = hi[k : k + 1].astype(BF)
            out_ref[OWN + 1 : OWN + 2, cols] = lo[k : k + 1].astype(BF)


def split(rows, others, gain):
    return pl.pallas_call(
        split_kernel,
        in_specs=[VM] * 5,
        out_specs=[VM] * N_DP,
        out_shape=[jax.ShapeDtypeStruct((MSG, COLS), BF)] * N_DP,
        compiler_params=params(12),
        cost_estimate=cost(0, 4 * N_DP * MSG * COLS),
        name="split",
    )(rows, *others, gain)


def finish_kernel(core_ref, *refs):
    messages, out_ref, gain_ref = refs[:N_DP], refs[N_DP], refs[N_DP + 1]
    sums = []
    for dc in range(2):
        total = messages[dc][...].astype(F32)
        for dy in range(1, 4):
            total = total + messages[2 * dy + dc][...].astype(F32)
        sums.append(total)
    both = sums[0] + sums[1]
    total = both[OWN : OWN + 1, :D] + both[OWN + 1 : OWN + 2, :D]
    for k in range(D // TILE):
        gain_ref[k : k + 1, :] = total[:, TILE * k : TILE * (k + 1)]
    swap = core_ref[0] == 1
    for half in range(2):
        chosen = jnp.where(swap, sums[1 - half], sums[half])
        for a in range(3):
            start = D * a + HALF * half
            out_ref[:, start : start + HALF] = chosen[0:OWN, HALF * a : HALF * (a + 1)]


def finish(core, messages):
    return pl.pallas_call(
        finish_kernel,
        in_specs=[SM] + [VM] * N_DP,
        out_specs=[VM, VM],
        out_shape=[
            jax.ShapeDtypeStruct((OWN, 3 * D), F32),
            jax.ShapeDtypeStruct((D // TILE, TILE), F32),
        ],
        compiler_params=params(12),
        cost_estimate=cost(0, 6 * N_DP * MSG * COLS),
        name="finish",
    )(core, *messages)


def dp_pairs(dy, dc):
    return [
        (2 * ((y + dy) % 4) + (c ^ dc), 2 * y + c) for y in range(4) for c in range(2)
    ]


def ring_pairs(df, ds):
    pairs = []
    for d in range(N_DP):
        dx, dz = (ds, df) if d % 2 else (df, ds)
        for x in range(4):
            for z in range(4):
                src = 4 * ((x + dx) % 4) + (z + dz) % 4
                pairs.append((N_INNER * d + src, N_INNER * d + 4 * x + z))
    return pairs


def from_ring(value, df, ds):
    return lax.ppermute(value, ("dp", "inner"), ring_pairs(df, ds))


def swap_cores(value):
    return lax.ppermute(value, "dp", [(d ^ 1, d) for d in range(N_DP)])


def exchange(value, axis="dp"):
    return lax.all_to_all(value, axis, split_axis=0, concat_axis=0, tiled=True)


def on_device(patches, segments, owners, norm_gain, qkv_weight, cotangent):
    group = lax.axis_index("dp")
    inner = lax.axis_index("inner")
    y, core, x, z = group // 2, group % 2, inner // 4, inner % 4
    core_1 = core.reshape(1).astype(jnp.int32)
    s = jnp.arange(N_DP)
    members = 2 * ((y + s // 2) % 4) + (core ^ (s % 2))
    gain = norm_gain.reshape(1, D)

    pos = jnp.arange(N_INNER)
    df, ds = pos % 4, pos // 4
    m = 4 * ((x + jnp.where(core == 0, df, ds)) % 4) + (
        z + jnp.where(core == 0, ds, df)
    ) % 4
    nat = (
        (members[None, :, None] * N_INNER + m[:, None, None]) * OWN
        + jnp.arange(OWN)[None, None, :]
    ).reshape(1, D).astype(F32)

    same_half, other_half = build(core_1, owners, qkv_weight, segments)
    messages = []
    for dy in range(4):
        for dc in range(2):
            msg = other_half if dc else same_half
            if dy or dc:
                msg = lax.ppermute(msg, "dp", dp_pairs(dy, dc))
            messages.append(msg)
    partner_patches = swap_cores(patches)
    own_prep = prep(patches, gain, nat)
    strips = exchange(
        cotangent.reshape(TILES, N_DP, STRIP, D).transpose(1, 0, 2, 3)
    )
    messages[-1], own_prep = lax.optimization_barrier((messages[-1], own_prep))
    block, seg, owners_rel = compact(messages)

    owner_of = jnp.sum(
        jnp.where(
            (members[None, :] == s[:, None])[:, :, None], owners_rel[None, :, :TILES], 0
        ),
        axis=1,
    )
    owner_of = owner_of.astype(jnp.int32).reshape(N_DP * TILES)
    u = jnp.arange(N_DP * TILES)
    earlier = (owner_of[:, None] == owner_of[None, :]) & (
        u[None, :] // TILES < u[:, None] // TILES
    )
    fwd = (TILES * owner_of + jnp.sum(earlier, axis=1)).astype(jnp.int32)
    wanted = fwd[None, :] == TILES * group + jnp.arange(TILES)[:, None]
    source = jnp.sum(jnp.where(wanted, u[None, :] // TILES, 0), axis=1)
    place_index = jnp.concatenate([2 * (source // 2), source % 2]).astype(jnp.int32)
    mine = jnp.arange(2)[:, None] ^ core
    tile = (TILES * (group - core + mine) + jnp.arange(TILES)[None, :]).reshape(-1)
    owner_here = jnp.sum(jnp.where(tile[:, None] == u[None, :], owner_of, 0), axis=1)
    slot_index = jnp.concatenate(
        [owner_here, jnp.broadcast_to(mine, (2, TILES)).reshape(-1)]
    ).astype(jnp.int32)

    heads = to_heads(fwd, strips.reshape(N_DP * TILES, STRIP, D))
    cot = exchange(heads)

    ring = [block] + [from_ring(block, f, 0) for f in (1, 2, 3)]
    ring[1], _ = lax.optimization_barrier((ring[1], heads))
    near_a, near_b = pack(ring[0], ring[1]), pack(ring[2], ring[3])
    above_a, below_b = from_ring(near_a, 0, 1), from_ring(near_b, 0, -1)
    above_b, below_a = from_ring(near_b, 0, 1), from_ring(near_a, 0, -1)
    partner_prep = prep(partner_patches, gain, nat)
    above_a, below_b, partner_prep = lax.optimization_barrier(
        (above_a, below_b, partner_prep)
    )
    far_a, far_b = from_ring(above_a, 0, 1), from_ring(below_b, 0, -1)
    pieces = [near_a, near_b, above_a, above_b, far_a, far_b, below_a, below_b]
    normed, normed_t = zip(own_prep, partner_prep)

    out, dqkv, col_a, col_b, up_a, up_b, far_up, far_down, down_a, down_b = main(
        slot_index, seg, normed, normed_t, cot, pieces
    )

    arrived_up, arrived_down = from_ring(far_up, 0, -1), from_ring(far_down, 0, 1)
    from_up_b, from_down_a = from_ring(up_b, 0, -1), from_ring(down_a, 0, 1)
    up_a, down_b = add([(up_a, arrived_up), (down_b, arrived_down)])
    from_up_a, from_down_b = from_ring(up_a, 0, -1), from_ring(down_b, 0, 1)
    zero, one, two, three = add(
        [(col_a, from_up_a, from_down_a), (col_b, from_up_b, from_down_b)], 2
    )
    others = [from_ring(two, -2, 0), from_ring(three, 1, 0), from_ring(one, -1, 0)]

    slots = exchange(out)
    others[0], slots = lax.optimization_barrier((others[0], slots))
    attended = place(place_index, slots).reshape(ROWS, D)

    dqkv_later, _, _ = lax.optimization_barrier((dqkv, up_a, down_b))
    mine, partners, gain_part = back(dqkv_later, pieces, nat, gain, normed)
    for shifts in ([(0, 1), (0, 2), (0, 3)], [(1, 0), (2, 0), (3, 0)]):
        gain_part = gain_part + sum(from_ring(gain_part, *shift) for shift in shifts)
    partners, _ = lax.optimization_barrier((partners, zero))
    grad_rows = rows_back(patches, gain, mine, swap_cores(partners))

    outgoing = split(zero, others, gain_part)
    incoming = []
    for dy in range(4):
        for dc in range(2):
            msg = outgoing[2 * dy + dc]
            if dy or dc:
                pairs = [(b, a) for a, b in dp_pairs(dy, dc)]
                msg = lax.ppermute(msg, "dp", pairs)
            incoming.append(msg)
    grad_qkv, grad_gain = finish(core_1, incoming)
    return (attended, grad_rows, grad_qkv, grad_gain.reshape(D))


def solution(mesh):
    both = ("dp", "inner")
    placed = (
        P(both, None),
        P(both, None),
        P(both),
        P(),
        P(both, None),
        P(both, None),
    )
    return jax.shard_map(
        on_device,
        mesh=mesh,
        in_specs=placed,
        out_specs=(P(both, None), P(both, None), P(both, None), P()),
        check_vma=False,
    )
```

```python
import functools

import jax
import jax.numpy as jnp
from jax import lax
from jax.experimental import pallas as pl
from jax.experimental.pallas import tpu as pltpu
from jax.sharding import PartitionSpec as P

D = 1280
HEADS = 16
HDIM = 80
TILE = 128
TILES = 3
N_DP = 8
N_INNER = 16
ROWS = TILES * TILE
PAIR_ROWS = 2 * ROWS
HALF = D // 2
COLS = 3 * HALF
OWN = 10
BLOCK = 80
PART = 160
PIECES = 8
STRIP = 16
MSG = 16
EPS = 1e-6
MASKED = -1e30
SCALE = HDIM ** (-0.5)
LOG2E = 1.4426950408889634
BF = jnp.bfloat16
F32 = jnp.float32
VM = pl.BlockSpec(memory_space=pltpu.VMEM)
SM = pl.BlockSpec(memory_space=pltpu.SMEM)
ANY = pl.BlockSpec(memory_space=pltpu.HBM)
NT = (((1,), (1,)), ((), ()))
TN = (((0,), (0,)), ((), ()))
NN = (((1,), (0,)), ((), ()))


def params(mib, **more):
    return pltpu.CompilerParams(vmem_limit_bytes=mib * 2**20, **more)


def cost(flops, nbytes, trans=0):
    return pl.CostEstimate(
        flops=flops // 1000, bytes_accessed=nbytes // 1000, transcendentals=trans // 1000
    )


def dot(a, b, dims=NN):
    return lax.dot_general(a, b, dims, preferred_element_type=F32)


def norm_rows(rows):
    wide = rows.astype(F32)
    centred = wide - jnp.mean(wide, axis=-1, keepdims=True)
    variance = jnp.mean(centred * centred, axis=-1, keepdims=True)
    inv_std = lax.rsqrt(variance + EPS)
    return centred * inv_std, inv_std


def build_order(nat_ref, perm_ref):
    for r in range(D // TILE):
        rows = slice(TILE * r, TILE * (r + 1))
        column = jnp.broadcast_to(nat_ref[:, rows], (TILE, TILE)).T
        for a in range(D // TILE):
            feature = lax.broadcasted_iota(jnp.int32, (TILE, TILE), 1) + TILE * a
            hit = column == feature.astype(F32)
            perm_ref[rows, TILE * a : TILE * (a + 1)] = jnp.where(hit, 1.0, 0.0).astype(BF)


def prep_kernel(patches_ref, gain_ref, nat_ref, normed_ref, normed_t_ref, perm_ref):
    build_order(nat_ref, perm_ref)
    standard, _ = norm_rows(patches_ref[...])
    normed = (standard * gain_ref[...]).astype(BF)
    normed_ref[...] = dot(normed, perm_ref[...], NT).astype(BF)
    normed_t_ref[...] = dot(perm_ref[...], normed, NT).astype(BF)


def prep(patches, gain, nat):
    return pl.pallas_call(
        prep_kernel,
        in_specs=[VM] * 3,
        out_specs=[VM] * 2,
        out_shape=[
            jax.ShapeDtypeStruct((ROWS, D), BF),
            jax.ShapeDtypeStruct((D, ROWS), BF),
        ],
        scratch_shapes=[pltpu.VMEM((D, D), BF)],
        compiler_params=params(58),
        cost_estimate=cost(4 * ROWS * D * D, 6 * ROWS * D),
        name="prep",
    )(patches, gain, nat)


def build_kernel(own_ref, w_ref, seg_ref, out_ref):
    lane = lax.broadcasted_iota(jnp.int32, (1, TILE), 1)
    owners = jnp.zeros((1, TILE), jnp.int32)
    for t in range(TILES):
        owners = jnp.where(lane == t, own_ref[t], owners)
    for d in range(N_DP):
        out_ref[d, OWN:MSG, :] = jnp.zeros((MSG - OWN, COLS), BF)
        for t in range(TILES):
            out_ref[d, OWN : OWN + 1, TILE * t : TILE * (t + 1)] = (
                seg_ref[t : t + 1, :].astype(F32).astype(BF)
            )
        out_ref[d, OWN + 1 : OWN + 2, 0:TILE] = owners.astype(F32).astype(BF)
        for a in range(3):
            start = D * a + HALF * (d % 2)
            out_ref[d, 0:OWN, HALF * a : HALF * (a + 1)] = w_ref[:, start : start + HALF]


def build(owners, weight, segments):
    return pl.pallas_call(
        build_kernel,
        in_specs=[SM, VM, VM],
        out_specs=VM,
        out_shape=jax.ShapeDtypeStruct((N_DP, MSG, COLS), BF),
        cost_estimate=cost(0, 2 * N_DP * MSG * COLS),
        compiler_params=params(12),
        name="build",
    )(owners, weight, segments)


def compact_kernel(group_ref, msg_ref, w_ref, seg_ref, own_ref):
    group = group_ref[0]
    seg_ref[...] = jnp.zeros_like(seg_ref)
    for s in range(N_DP):
        w_ref[OWN * s : OWN * (s + 1), :] = msg_ref[s, 0:OWN, :]
        own_ref[s : s + 1, :] = msg_ref[s, OWN + 1 : OWN + 2, 0:TILE].astype(F32)
    for rel in range(2):
        src = group + rel * (1 - 2 * (group % 2))
        for t in range(TILES):
            seg_ref[TILES * rel + t : TILES * rel + t + 1, :] = msg_ref[
                src, OWN : OWN + 1, TILE * t : TILE * (t + 1)
            ].astype(F32)


def compact(group, messages):
    return pl.pallas_call(
        compact_kernel,
        in_specs=[SM, VM],
        out_specs=[VM] * 3,
        out_shape=[
            jax.ShapeDtypeStruct((BLOCK, COLS), BF),
            jax.ShapeDtypeStruct((8, TILE), F32),
            jax.ShapeDtypeStruct((N_DP, TILE), F32),
        ],
        cost_estimate=cost(0, 4 * N_DP * MSG * COLS),
        compiler_params=params(12),
        name="compact",
    )(group, messages)


def to_heads_kernel(fwd_ref, in_ref, out_ref):
    for d in range(N_DP):
        half = slice(HALF * (d % 2), HALF * (d % 2 + 1))
        for k in range(2 * TILES):
            u = TILES * (2 * (d // 2) + ((d % 2) ^ (k // TILES))) + k % TILES
            out_ref[d, k] = in_ref[fwd_ref[u], :, half]


def to_heads(fwd, strips):
    return pl.pallas_call(
        to_heads_kernel,
        in_specs=[SM, VM],
        out_specs=VM,
        out_shape=jax.ShapeDtypeStruct((N_DP, 2 * TILES, STRIP, HALF), BF),
        cost_estimate=cost(0, 4 * ROWS * D),
        compiler_params=params(12),
        name="to_heads",
    )(fwd, strips)


def place_kernel(idx_ref, left_ref, right_ref, out_ref):
    out_ref[0, :, :HALF] = left_ref[0, 0]
    out_ref[0, :, HALF:] = right_ref[0, 0]


def place(index, slots):
    def half(c):
        return pl.BlockSpec(
            (1, 1, TILE, HALF), lambda p, g: (g[p] + c, g[TILES + p], 0, 0)
        )

    spec = pltpu.PrefetchScalarGridSpec(
        num_scalar_prefetch=1,
        grid=(TILES,),
        in_specs=[half(0), half(1)],
        out_specs=pl.BlockSpec((1, TILE, D), lambda p, g: (p, 0, 0)),
    )
    return pl.pallas_call(
        place_kernel,
        grid_spec=spec,
        out_shape=jax.ShapeDtypeStruct((TILES, TILE, D), BF),
        compiler_params=params(12),
        cost_estimate=cost(0, 4 * ROWS * D),
        name="place",
    )(index, slots, slots)


def window_masks(i):
    lane = lax.broadcasted_iota(jnp.int32, (TILE, 256), 1)
    start = 32 * i
    first = (lane >= start) & (lane < start + HDIM)
    second = (lane >= start + HDIM) & (lane < start + 2 * HDIM)
    return first, second


def stack_heads(window, masks):
    zero = jnp.zeros_like(window)
    return jnp.concatenate([jnp.where(m, window, zero) for m in masks], axis=0)


def pick_heads(stacked, masks):
    zero = jnp.zeros((TILE, 256), F32)
    return jnp.where(
        masks[0], stacked[:TILE], jnp.where(masks[1], stacked[TILE:], zero)
    )


def halves(fn, *arrays):
    return jnp.concatenate(
        [fn(*(a[:, :TILE] for a in arrays)), fn(*(a[:, TILE:] for a in arrays))], axis=1
    )


def wide_max(a):
    return jnp.broadcast_to(jnp.max(a, axis=-1, keepdims=True), a.shape)


def wide_sum(a):
    return jnp.broadcast_to(jnp.sum(a, axis=-1, keepdims=True), a.shape)


CHUNKS = [pl.ds(0, 768), pl.ds(768, 768), pl.ds(1536, 384)]


def start(copies):
    for copy in copies:
        copy.start()


def wait(copies):
    for copy in copies:
        copy.wait()


def load_weight(pieces, weight, sems):
    return [
        [
            pltpu.make_async_copy(
                piece.at[:, cols],
                weight.at[pl.ds(PART * b, PART), cols],
                sems.at[n, b],
            )
            for b, piece in enumerate(pieces)
        ]
        for n, cols in enumerate(CHUNKS)
    ]


def load_rows(refs, rows, sems):
    return [
        pltpu.make_async_copy(ref, rows.at[pl.ds(ROWS * h, ROWS)], sems.at[h])
        for h, ref in enumerate(refs)
    ]


def load_features(refs, normed_t, sems):
    return [
        pltpu.make_async_copy(ref, normed_t.at[:, pl.ds(ROWS * h, ROWS)], sems.at[h])
        for h, ref in enumerate(refs)
    ]


def gradient(normed_t, dqkv, weight, outs, staged, gain_part, sems):
    copies = []
    places = [(0, 0), (1, 0), (2, 0), (4, PART), (4, 0), (5, 0), (5, PART), (3, 0)]
    for c, cols in enumerate(CHUNKS):
        for n in range(0, PIECES, 2):
            rows = slice(PART * n, PART * (n + 2))
            both = dot(normed_t[rows, :], dqkv[:, cols])
            product = both * weight[rows, cols].astype(F32)
            lanes = sum(
                product[:, TILE * k : TILE * (k + 1)] for k in range(cols.size // TILE)
            )
            gain_part[rows, :] = lanes if c == 0 else gain_part[rows, :] + lanes
            both = both.astype(BF)
            for k in (n, n + 1):
                staged[k, :, cols] = both[PART * (k - n) : PART * (k - n + 1)]
                copies.append(
                    pltpu.make_async_copy(
                        staged.at[k, :, cols],
                        outs[places[k][0]].at[pl.ds(places[k][1], PART), cols],
                        sems.at[c, k],
                    )
                )
                copies[-1].start()
    wait(copies)


def main_kernel(
    idx_ref,
    seg_ref,
    normed_ref,
    partner_ref,
    normed_t_ref,
    partner_t_ref,
    cot_ref,
    *refs,
):
    pieces, slots_ref, dqkv_ref = refs[:PIECES], refs[PIECES], refs[PIECES + 1]
    grads, gain_ref = refs[PIECES + 2 : PIECES + 8], refs[PIECES + 8]
    (
        normed,
        qkv,
        cot,
        weight,
        normed_t,
        dqkv,
        out_tiles,
        staged,
        row_sems,
        cot_sems,
        w_sems,
        t_sems,
        slot_sems,
        dqkv_sems,
        grad_sems,
    ) = refs[PIECES + 9 :]
    row_copies = load_rows((normed_ref, partner_ref), normed, row_sems)
    w_copies = load_weight(pieces, weight, w_sems)
    cot_copies = [
        pltpu.make_async_copy(cot_ref.at[j], cot.at[:, j], cot_sems.at[j])
        for j in range(N_DP)
    ]
    t_copies = load_features((normed_t_ref, partner_t_ref), normed_t, t_sems)
    start(row_copies)
    for copies in w_copies:
        start(copies)
    start(cot_copies)
    start(t_copies)
    wait(row_copies)
    for c, cols in enumerate(CHUNKS):
        wait(w_copies[c])
        qkv[:, cols] = dot(normed[...], weight[:, cols]).astype(BF)
    wait(cot_copies)

    def leave(t):
        rows = pl.ds(pl.multiple_of(t * TILE, TILE), TILE)
        return [
            pltpu.make_async_copy(
                out_tiles.at[t],
                slots_ref.at[idx_ref[t], idx_ref[2 * TILES + t]],
                slot_sems.at[t],
            ),
            pltpu.make_async_copy(dqkv.at[rows], dqkv_ref.at[rows], dqkv_sems.at[t]),
        ]

    @pl.loop(0, TILES)
    def _(step):
        pairs = range(8)
        tiles = [2 * step, 2 * step + 1]
        rows = [pl.ds(pl.multiple_of(t * TILE, TILE), TILE) for t in tiles]
        same = []
        for t in tiles:
            seg = jnp.broadcast_to(seg_ref[pl.ds(t, 1), :], (TILE, TILE))
            equal = seg == seg.T
            same.append(jnp.concatenate([equal, equal], axis=1))
        masks = [window_masks(i % 4) for i in pairs]
        windows = [slice(128 * (i % 4), 128 * (i % 4) + 256) for i in pairs]

        def window(a, i):
            first = HALF * a + 128 * (i % 4)
            return qkv[rows[i // 4], first : first + 256]

        q = [window(0, i) for i in pairs]
        d_out = [
            cot[tiles[i // 4], :, :, windows[i]].reshape(TILE, 256) for i in pairs
        ]
        kk = [stack_heads(window(1, i), masks[i]) for i in pairs]
        vv = [stack_heads(window(2, i), masks[i]) for i in pairs]
        scores = [dot(q[i], kk[i], NT) for i in pairs]
        d_probs = [dot(d_out[i], vv[i], NT) for i in pairs]
        scores = [
            jnp.where(same[i // 4], scores[i] * (SCALE * LOG2E), MASKED) for i in pairs
        ]
        tops = [halves(wide_max, x) for x in scores]
        expo = [jnp.exp2(x - m) for x, m in zip(scores, tops)]
        sums = [halves(wide_sum, x) for x in expo]
        weights = [x * (1.0 / total) for x, total in zip(expo, sums)]
        rounded = [x.astype(BF) for x in weights]
        outs = [dot(rounded[i], vv[i]) for i in pairs]
        dvs = [dot(rounded[i], d_out[i], TN) for i in pairs]
        inner = [halves(wide_sum, d_probs[i] * weights[i]) for i in pairs]
        d_scores = [
            (weights[i] * (d_probs[i] - inner[i]) * SCALE).astype(BF) for i in pairs
        ]
        dqs = [dot(d_scores[i], kk[i]) for i in pairs]
        dks = [dot(d_scores[i], q[i], TN) for i in pairs]
        dks = [pick_heads(dks[i], masks[i]) for i in pairs]
        dvs = [pick_heads(dvs[i], masks[i]) for i in pairs]

        def lanes(vals):
            parts = [vals[0][:, :TILE]]
            for i in range(3):
                parts.append(vals[i][:, TILE:] + vals[i + 1][:, :TILE])
            parts.append(vals[3][:, TILE:])
            return jnp.concatenate([p.astype(BF) for p in parts], axis=1)

        for n, t in enumerate(tiles):
            part = slice(4 * n, 4 * n + 4)
            out_tiles[t] = lanes(outs[part])
            for a, vals in enumerate((dqs, dks, dvs)):
                dqkv[rows[n], HALF * a : HALF * (a + 1)] = lanes(vals[part])
            start(leave(t))

    wait(t_copies)
    gradient(normed_t, dqkv, weight, grads, staged, gain_ref, grad_sems)
    for t in range(2 * TILES):
        wait(leave(t))


def main(index, seg, normed, normed_t, cot, pieces):
    return pl.pallas_call(
        main_kernel,
        in_specs=[SM, VM] + [ANY] * (5 + PIECES),
        out_specs=[ANY] * 8 + [VM],
        out_shape=[
            jax.ShapeDtypeStruct((N_DP, 2, TILE, HALF), BF),
            jax.ShapeDtypeStruct((PAIR_ROWS, COLS), BF),
        ]
        + [jax.ShapeDtypeStruct((PART, COLS), BF)] * 4
        + [jax.ShapeDtypeStruct((2 * PART, COLS), BF)] * 2
        + [jax.ShapeDtypeStruct((D, TILE), F32)],
        scratch_shapes=[
            pltpu.VMEM((PAIR_ROWS, D), BF),
            pltpu.VMEM((PAIR_ROWS, COLS), BF),
            pltpu.VMEM((2 * TILES, N_DP, STRIP, HALF), BF),
            pltpu.VMEM((D, COLS), BF),
            pltpu.VMEM((D, PAIR_ROWS), BF),
            pltpu.VMEM((PAIR_ROWS, COLS), BF),
            pltpu.VMEM((2 * TILES, TILE, HALF), BF),
            pltpu.VMEM((PIECES, PART, COLS), BF),
            pltpu.SemaphoreType.DMA((2,)),
            pltpu.SemaphoreType.DMA((N_DP,)),
            pltpu.SemaphoreType.DMA((len(CHUNKS), PIECES)),
            pltpu.SemaphoreType.DMA((2,)),
            pltpu.SemaphoreType.DMA((2 * TILES,)),
            pltpu.SemaphoreType.DMA((2 * TILES,)),
            pltpu.SemaphoreType.DMA((len(CHUNKS), PIECES)),
        ],
        compiler_params=params(58),
        cost_estimate=cost(8 * 10**9, 20 * 2**20, 10**6),
        name="main",
    )(index, seg, *normed, *normed_t, cot, *pieces)


def add_kernel(counts, firsts, cuts, *refs):
    outs, used = refs[sum(counts) :], 0
    for n, count in enumerate(counts):
        total = jnp.zeros((PART, COLS), F32)
        for k in range(used, used + count):
            total = total + refs[k][firsts[k] : firsts[k] + PART, :].astype(F32)
        used += count
        size = PART // cuts
        for k in range(cuts):
            outs[cuts * n + k][...] = total[size * k : size * (k + 1)].astype(BF)


def add(groups, cuts=1):
    parts = [part for group in groups for part in group]
    shape = jax.ShapeDtypeStruct((PART // cuts, COLS), BF)
    return pl.pallas_call(
        functools.partial(
            add_kernel, [len(group) for group in groups], [f for _, f in parts], cuts
        ),
        in_specs=[VM] * len(parts),
        out_specs=[VM] * (cuts * len(groups)),
        out_shape=[shape] * (cuts * len(groups)),
        compiler_params=params(12),
        cost_estimate=cost(0, 4 * len(parts) * PART * COLS),
        name="add",
    )(*[array for array, _ in parts])


def gain_kernel(part_ref, nat_ref, gain_ref, out_ref, perm_ref):
    build_order(nat_ref, perm_ref)
    rest = jnp.sum(part_ref[...], axis=1, keepdims=True)
    rest = jnp.broadcast_to(rest, (D, TILE))
    total = jnp.zeros((1, D), F32)
    for _ in range(3):
        term = rest.astype(BF)
        rest = rest - term.astype(F32)
        total = total + dot(term, perm_ref[...], TN)[0:1]
    total = total / gain_ref[...]
    out_ref[...] = jnp.zeros_like(out_ref)
    for k in range(D // TILE):
        out_ref[k : k + 1, :] = total[:, TILE * k : TILE * (k + 1)]


def gain_back(part, nat, gain):
    return pl.pallas_call(
        gain_kernel,
        in_specs=[VM] * 3,
        out_specs=VM,
        out_shape=jax.ShapeDtypeStruct((MSG, TILE), F32),
        scratch_shapes=[pltpu.VMEM((D, D), BF)],
        compiler_params=params(24),
        cost_estimate=cost(0, 4 * D * TILE),
        name="gain",
    )(part, nat, gain)


def back_kernel(half, nat_ref, dqkv_ref, *refs):
    pieces, (out_ref, weight, perm_ref, dqkv, w_sems, q_sem) = (
        refs[:PIECES],
        refs[PIECES:],
    )
    w_copies = load_weight(pieces, weight, w_sems)
    q_copy = pltpu.make_async_copy(dqkv_ref.at[pl.ds(ROWS * half, ROWS)], dqkv, q_sem)
    q_copy.start()
    for copies in w_copies:
        start(copies)
    build_order(nat_ref, perm_ref)
    q_copy.wait()
    for copies in w_copies:
        wait(copies)
    d_normed = dot(dqkv[...], weight[...], NT).astype(BF)
    out_ref[...] = dot(d_normed, perm_ref[...]).astype(BF)


def back(half, dqkv, pieces, nat):
    return pl.pallas_call(
        functools.partial(back_kernel, half),
        in_specs=[VM] + [ANY] * (1 + PIECES),
        out_specs=VM,
        out_shape=jax.ShapeDtypeStruct((ROWS, D), BF),
        scratch_shapes=[
            pltpu.VMEM((D, COLS), BF),
            pltpu.VMEM((D, D), BF),
            pltpu.VMEM((ROWS, COLS), BF),
            pltpu.SemaphoreType.DMA((len(CHUNKS), PIECES)),
            pltpu.SemaphoreType.DMA,
        ],
        compiler_params=params(58),
        cost_estimate=cost(2 * ROWS * D * (D + COLS), 15 * 2**20),
        name="back",
    )(nat, dqkv, *pieces)


def rows_kernel(patches_ref, gain_ref, mine_ref, other_ref, out_ref):
    standard, inv_std = norm_rows(patches_ref[...])
    d_normed = mine_ref[...].astype(F32) + other_ref[...].astype(F32)
    scaled = d_normed * gain_ref[...]
    back_rows = inv_std * (
        scaled
        - jnp.mean(scaled, axis=-1, keepdims=True)
        - standard * jnp.mean(scaled * standard, axis=-1, keepdims=True)
    )
    out_ref[...] = back_rows.astype(BF)


def rows_back(patches, gain, mine, other):
    block = pl.BlockSpec((TILE, D), lambda i: (i, 0))
    return pl.pallas_call(
        rows_kernel,
        grid=(TILES,),
        in_specs=[block, pl.BlockSpec((1, D), lambda i: (0, 0)), block, block],
        out_specs=block,
        out_shape=jax.ShapeDtypeStruct((ROWS, D), BF),
        compiler_params=params(58),
        cost_estimate=cost(20 * ROWS * D, 8 * ROWS * D),
        name="rows_back",
    )(patches, gain, mine, other)


def split_kernel(rows_ref, one_ref, two_ref, three_ref, gain_ref, out_ref):
    gain = gain_ref[...]
    hi = gain.astype(BF).astype(F32)
    lo = gain - hi
    total = rows_ref[...].astype(F32)
    for ref in (one_ref, two_ref, three_ref):
        total = total + ref[...].astype(F32)
    total = total.astype(BF)
    for s in range(N_DP):
        out_ref[s, 0:OWN, :] = total[OWN * s : OWN * (s + 1)]
        out_ref[s, OWN:MSG, :] = jnp.zeros((MSG - OWN, COLS), BF)
        for k in range(D // TILE):
            cols = slice(TILE * k, TILE * (k + 1))
            out_ref[s, OWN : OWN + 1, cols] = hi[k : k + 1].astype(BF)
            out_ref[s, OWN + 1 : OWN + 2, cols] = lo[k : k + 1].astype(BF)


def split(rows, others, gain):
    return pl.pallas_call(
        split_kernel,
        in_specs=[VM] * 5,
        out_specs=VM,
        out_shape=jax.ShapeDtypeStruct((N_DP, MSG, COLS), BF),
        cost_estimate=cost(0, 4 * N_DP * MSG * COLS),
        compiler_params=params(12),
        name="split",
    )(rows, *others, gain)


def finish_kernel(msg_ref, out_ref, gain_ref):
    both = jnp.zeros((MSG, COLS), F32)
    for half in range(2):
        total = msg_ref[half].astype(F32)
        for chip in range(1, 4):
            total = total + msg_ref[2 * chip + half].astype(F32)
        both = both + total
        for a in range(3):
            start = D * a + HALF * half
            out_ref[:, start : start + HALF] = total[0:OWN, HALF * a : HALF * (a + 1)]
    total = both[OWN : OWN + 1, :D] + both[OWN + 1 : OWN + 2, :D]
    for k in range(D // TILE):
        gain_ref[k : k + 1, :] = total[:, TILE * k : TILE * (k + 1)]


def finish(messages):
    return pl.pallas_call(
        finish_kernel,
        in_specs=[VM],
        out_specs=[VM, VM],
        out_shape=[
            jax.ShapeDtypeStruct((OWN, 3 * D), F32),
            jax.ShapeDtypeStruct((D // TILE, TILE), F32),
        ],
        cost_estimate=cost(0, 6 * N_DP * MSG * COLS),
        compiler_params=params(12),
        name="finish",
    )(messages)


def ring_pairs(df, ds):
    pairs = []
    for d in range(N_DP):
        dx, dz = (ds, df) if d % 2 else (df, ds)
        for x in range(4):
            for z in range(4):
                src = 4 * ((x + dx) % 4) + (z + dz) % 4
                pairs.append((N_INNER * d + src, N_INNER * d + 4 * x + z))
    return pairs


def double_pairs(f_bits, s_bits):
    pairs = []
    for d in range(N_DP):
        x_bits, z_bits = (s_bits, f_bits) if d % 2 else (f_bits, s_bits)
        flip = 4 * x_bits + z_bits
        pairs += [(N_INNER * d + (m ^ flip), N_INNER * d + m) for m in range(N_INNER)]
    return pairs


def from_ring(value, df, ds):
    return lax.ppermute(value, ("dp", "inner"), ring_pairs(df, ds))


def swap_cores(value):
    return lax.ppermute(value, "dp", [(d ^ 1, d) for d in range(N_DP)])


def exchange(value, axis="dp"):
    return lax.all_to_all(value, axis, split_axis=0, concat_axis=0, tiled=True)


def on_device(patches, segments, owners, norm_gain, qkv_weight, cotangent):
    group = lax.axis_index("dp")
    inner = lax.axis_index("inner")
    core, x, z = group % 2, inner // 4, inner % 4
    gain = norm_gain.reshape(1, D)

    pos = jnp.arange(N_INNER)
    df, ds = pos % 4, pos // 4
    m = 4 * ((x + jnp.where(core == 0, df, ds)) % 4) + (
        z + jnp.where(core == 0, ds, df)
    ) % 4
    nat = (
        (jnp.arange(N_DP)[None, :, None] * N_INNER + m[:, None, None]) * OWN
        + jnp.arange(OWN)[None, None, :]
    ).reshape(1, D).astype(F32)

    messages = exchange(build(owners, qkv_weight, segments))
    partner_patches = swap_cores(patches)
    own_prep = prep(patches, gain, nat)
    strips = cotangent.reshape(TILES, N_DP, STRIP, D).transpose(1, 0, 2, 3)
    messages, own_prep, strips = lax.optimization_barrier((messages, own_prep, strips))
    block, seg, owners_all = compact(group.reshape(1).astype(jnp.int32), messages)
    strips = exchange(strips)

    owner_of = owners_all[:, :TILES].astype(jnp.int32).reshape(N_DP * TILES)
    u = jnp.arange(N_DP * TILES)
    earlier = (owner_of[:, None] == owner_of[None, :]) & (
        u[None, :] // TILES < u[:, None] // TILES
    )
    fwd = (TILES * owner_of + jnp.sum(earlier, axis=1)).astype(jnp.int32)
    wanted = fwd[None, :] == TILES * group + jnp.arange(TILES)[:, None]
    source = jnp.sum(jnp.where(wanted, u[None, :] // TILES, 0), axis=1)
    place_index = jnp.concatenate([2 * (source // 2), source % 2]).astype(jnp.int32)
    mine = jnp.arange(2)[:, None] ^ core
    tile = (TILES * (group - core + mine) + jnp.arange(TILES)[None, :]).reshape(-1)
    owner_here = jnp.sum(jnp.where(tile[:, None] == u[None, :], owner_of, 0), axis=1)
    slot_index = jnp.concatenate(
        [owner_here, jnp.broadcast_to(mine, (2, TILES)).reshape(-1)]
    ).astype(jnp.int32)

    heads = to_heads(fwd, strips.reshape(N_DP * TILES, STRIP, D))
    cot = exchange(heads)

    ring = [block] + [from_ring(block, f, 0) for f in (1, 2, 3)]
    near_a, near_b = jnp.concatenate(ring[:2]), jnp.concatenate(ring[2:])
    above_a, below_b = from_ring(near_a, 0, 1), from_ring(near_b, 0, -1)
    above_b, below_a = from_ring(near_b, 0, 1), from_ring(near_a, 0, -1)
    above_a, above_b, below_a, below_b = lax.optimization_barrier(
        (above_a, above_b, below_a, below_b)
    )
    far_a, far_b = from_ring(above_a, 0, 1), from_ring(below_b, 0, -1)
    pieces = [near_a, near_b, above_a, above_b, far_a, far_b, below_a, below_b]
    normed, normed_t = zip(own_prep, prep(partner_patches, gain, nat))

    out, dqkv, col_a, col_b, up_a, down_b, up, down, gain_part = main(
        slot_index, seg, normed, normed_t, cot, pieces
    )

    up, down = from_ring(up, 0, -1), from_ring(down, 0, 1)
    slots = exchange(out)
    gain_part = gain_back(gain_part, nat, gain)
    both = ("dp", "inner")
    gain_part = gain_part + lax.ppermute(gain_part, both, double_pairs(0, 1))
    gain_part = gain_part + lax.ppermute(gain_part, both, double_pairs(0, 3))
    partners = back(1, dqkv, pieces, nat)
    up, down, gain_part, partners = lax.optimization_barrier(
        (up, down, gain_part, partners)
    )
    other = swap_cores(partners)
    up_a, down_b = add([[(up_a, 0), (up, 0)], [(down_b, 0), (down, 0)]])
    from_up_a, from_down_b = from_ring(up_a, 0, -1), from_ring(down_b, 0, 1)
    dqkv, gain_part, _ = lax.optimization_barrier((dqkv, gain_part, up_a))
    mine = back(0, dqkv, pieces, nat)
    gain_part = gain_part + lax.ppermute(gain_part, both, double_pairs(1, 0))
    gain_part = gain_part + lax.ppermute(gain_part, both, double_pairs(3, 0))
    from_up_a, from_down_b, mine, gain_part = lax.optimization_barrier(
        (from_up_a, from_down_b, mine, gain_part)
    )
    zero, one, two, three = add(
        [
            [(col_a, 0), (from_up_a, 0), (down, PART)],
            [(col_b, 0), (up, PART), (from_down_b, 0)],
        ],
        2,
    )
    others = [from_ring(two, -2, 0), from_ring(three, 1, 0), from_ring(one, -1, 0)]
    others[0], slots = lax.optimization_barrier((others[0], slots))

    attended = place(place_index, slots).reshape(ROWS, D)
    grad_rows = rows_back(patches, gain, mine, other)
    grad_qkv, grad_gain = finish(exchange(split(zero, others, gain_part)))
    return (attended, grad_rows, grad_qkv, grad_gain.reshape(D))


def solution(mesh):
    both = ("dp", "inner")
    placed = (
        P(both, None),
        P(both, None),
        P(both),
        P(),
        P(both, None),
        P(both, None),
    )
    return jax.shard_map(
        on_device,
        mesh=mesh,
        in_specs=placed,
        out_specs=(P(both, None), P(both, None), P(both, None), P()),
        check_vma=False,
    )
```

```python
import functools

import jax
import jax.numpy as jnp
from jax import lax
from jax.experimental import pallas as pl
from jax.experimental.pallas import tpu as pltpu
from jax.sharding import PartitionSpec as P

D = 1280
HEADS = 16
HDIM = 80
TILE = 128
TILES = 3
N_DP = 8
N_INNER = 16
ROWS = TILES * TILE
PAIR_ROWS = 2 * ROWS
HALF = D // 2
COLS = 3 * HALF
OWN = 10
BLOCK = 80
PART = 160
PIECES = 8
RIDE = 88
STRIP = 16
MSG = 16
EPS = 1e-6
MASKED = -1e30
SCALE = HDIM ** (-0.5)
LOG2E = 1.4426950408889634
BF = jnp.bfloat16
F32 = jnp.float32
VM = pl.BlockSpec(memory_space=pltpu.VMEM)
SM = pl.BlockSpec(memory_space=pltpu.SMEM)
ANY = pl.BlockSpec(memory_space=pltpu.HBM)
NT = (((1,), (1,)), ((), ()))
TN = (((0,), (0,)), ((), ()))
NN = (((1,), (0,)), ((), ()))


def params(mib, **more):
    return pltpu.CompilerParams(vmem_limit_bytes=mib * 2**20, **more)


def cost(flops, nbytes, trans=0):
    return pl.CostEstimate(
        flops=flops // 1000, bytes_accessed=nbytes // 1000, transcendentals=trans // 1000
    )


def dot(a, b, dims=NN):
    return lax.dot_general(a, b, dims, preferred_element_type=F32)


def norm_rows(rows):
    wide = rows.astype(F32)
    centred = wide - jnp.mean(wide, axis=-1, keepdims=True)
    variance = jnp.mean(centred * centred, axis=-1, keepdims=True)
    inv_std = lax.rsqrt(variance + EPS)
    return centred * inv_std, inv_std


def build_order(nat_ref, perm_ref):
    for r in range(D // TILE):
        rows = slice(TILE * r, TILE * (r + 1))
        column = jnp.broadcast_to(nat_ref[:, rows], (TILE, TILE)).T
        for a in range(D // TILE):
            feature = lax.broadcasted_iota(jnp.int32, (TILE, TILE), 1) + TILE * a
            hit = column == feature.astype(F32)
            perm_ref[rows, TILE * a : TILE * (a + 1)] = jnp.where(hit, 1.0, 0.0).astype(BF)


def prep_kernel(patches_ref, gain_ref, nat_ref, normed_ref, normed_t_ref, perm_ref):
    build_order(nat_ref, perm_ref)
    standard, _ = norm_rows(patches_ref[...])
    normed = (standard * gain_ref[...]).astype(BF)
    normed_ref[...] = dot(normed, perm_ref[...], NT).astype(BF)
    normed_t_ref[...] = dot(perm_ref[...], normed, NT).astype(BF)


def prep(patches, gain, nat):
    return pl.pallas_call(
        prep_kernel,
        in_specs=[VM] * 3,
        out_specs=[VM] * 2,
        out_shape=[
            jax.ShapeDtypeStruct((ROWS, D), BF),
            jax.ShapeDtypeStruct((D, ROWS), BF),
        ],
        scratch_shapes=[pltpu.VMEM((D, D), BF)],
        compiler_params=params(58),
        cost_estimate=cost(4 * ROWS * D * D, 6 * ROWS * D),
        name="prep",
    )(patches, gain, nat)


def build_kernel(own_ref, w_ref, seg_ref, out_ref):
    lane = lax.broadcasted_iota(jnp.int32, (1, TILE), 1)
    owners = jnp.zeros((1, TILE), jnp.int32)
    for t in range(TILES):
        owners = jnp.where(lane == t, own_ref[t], owners)
    for d in range(N_DP):
        out_ref[d, OWN:MSG, :] = jnp.zeros((MSG - OWN, COLS), BF)
        for t in range(TILES):
            out_ref[d, OWN : OWN + 1, TILE * t : TILE * (t + 1)] = (
                seg_ref[t : t + 1, :].astype(F32).astype(BF)
            )
        out_ref[d, OWN + 1 : OWN + 2, 0:TILE] = owners.astype(F32).astype(BF)
        for a in range(3):
            start = D * a + HALF * (d % 2)
            out_ref[d, 0:OWN, HALF * a : HALF * (a + 1)] = w_ref[:, start : start + HALF]


def build(owners, weight, segments):
    return pl.pallas_call(
        build_kernel,
        in_specs=[SM, VM, VM],
        out_specs=VM,
        out_shape=jax.ShapeDtypeStruct((N_DP, MSG, COLS), BF),
        cost_estimate=cost(0, 2 * N_DP * MSG * COLS),
        compiler_params=params(58),
        name="build",
    )(owners, weight, segments)


def compact_kernel(group_ref, msg_ref, w_ref, seg_ref, own_ref):
    group = group_ref[0]
    seg_ref[...] = jnp.zeros_like(seg_ref)
    for s in range(N_DP):
        w_ref[OWN * s : OWN * (s + 1), :] = msg_ref[s, 0:OWN, :]
        own_ref[s : s + 1, :] = msg_ref[s, OWN + 1 : OWN + 2, 0:TILE].astype(F32)
    for rel in range(2):
        src = group + rel * (1 - 2 * (group % 2))
        for t in range(TILES):
            seg_ref[TILES * rel + t : TILES * rel + t + 1, :] = msg_ref[
                src, OWN : OWN + 1, TILE * t : TILE * (t + 1)
            ].astype(F32)


def compact(group, messages):
    return pl.pallas_call(
        compact_kernel,
        in_specs=[SM, VM],
        out_specs=[VM] * 3,
        out_shape=[
            jax.ShapeDtypeStruct((BLOCK, COLS), BF),
            jax.ShapeDtypeStruct((8, TILE), F32),
            jax.ShapeDtypeStruct((N_DP, TILE), F32),
        ],
        cost_estimate=cost(0, 4 * N_DP * MSG * COLS),
        compiler_params=params(12),
        name="compact",
    )(group, messages)


def to_heads_kernel(fwd_ref, in_ref, out_ref):
    for d in range(N_DP):
        half = slice(HALF * (d % 2), HALF * (d % 2 + 1))
        for k in range(2 * TILES):
            u = TILES * (2 * (d // 2) + ((d % 2) ^ (k // TILES))) + k % TILES
            out_ref[d, k] = in_ref[fwd_ref[u], :, half]


def to_heads(fwd, strips):
    return pl.pallas_call(
        to_heads_kernel,
        in_specs=[SM, VM],
        out_specs=VM,
        out_shape=jax.ShapeDtypeStruct((N_DP, 2 * TILES, STRIP, HALF), BF),
        cost_estimate=cost(0, 4 * ROWS * D),
        compiler_params=params(12),
        name="to_heads",
    )(fwd, strips)


def place_kernel(idx_ref, left_ref, right_ref, out_ref):
    out_ref[0, :, :HALF] = left_ref[0, 0]
    out_ref[0, :, HALF:] = right_ref[0, 0]


def place(index, slots):
    def half(c):
        return pl.BlockSpec(
            (1, 1, TILE, HALF), lambda p, g: (g[p] + c, g[TILES + p], 0, 0)
        )

    spec = pltpu.PrefetchScalarGridSpec(
        num_scalar_prefetch=1,
        grid=(TILES,),
        in_specs=[half(0), half(1)],
        out_specs=pl.BlockSpec((1, TILE, D), lambda p, g: (p, 0, 0)),
    )
    return pl.pallas_call(
        place_kernel,
        grid_spec=spec,
        out_shape=jax.ShapeDtypeStruct((TILES, TILE, D), BF),
        compiler_params=params(12),
        cost_estimate=cost(0, 4 * ROWS * D),
        name="place",
    )(index, slots, slots)


def window_masks(i):
    lane = lax.broadcasted_iota(jnp.int32, (TILE, 256), 1)
    start = 32 * i
    first = (lane >= start) & (lane < start + HDIM)
    second = (lane >= start + HDIM) & (lane < start + 2 * HDIM)
    return first, second


def stack_heads(window, masks):
    zero = jnp.zeros_like(window)
    return jnp.concatenate([jnp.where(m, window, zero) for m in masks], axis=0)


def pick_heads(stacked, masks):
    zero = jnp.zeros((TILE, 256), F32)
    return jnp.where(
        masks[0], stacked[:TILE], jnp.where(masks[1], stacked[TILE:], zero)
    )


def halves(fn, *arrays):
    return jnp.concatenate(
        [fn(*(a[:, :TILE] for a in arrays)), fn(*(a[:, TILE:] for a in arrays))], axis=1
    )


def wide_max(a):
    return jnp.broadcast_to(jnp.max(a, axis=-1, keepdims=True), a.shape)


def wide_sum(a):
    return jnp.broadcast_to(jnp.sum(a, axis=-1, keepdims=True), a.shape)


CHUNKS = [pl.ds(0, 768), pl.ds(768, 768), pl.ds(1536, 384)]


def start(copies):
    for copy in copies:
        copy.start()


def wait(copies):
    for copy in copies:
        copy.wait()


def load_weight(pieces, weight, sems):
    return [
        [
            pltpu.make_async_copy(
                piece.at[:, cols],
                weight.at[pl.ds(PART * b, PART), cols],
                sems.at[n, b],
            )
            for b, piece in enumerate(pieces)
        ]
        for n, cols in enumerate(CHUNKS)
    ]


def load_rows(refs, rows, sems):
    return [
        pltpu.make_async_copy(ref, rows.at[pl.ds(ROWS * h, ROWS)], sems.at[h])
        for h, ref in enumerate(refs)
    ]


def load_features(refs, normed_t, sems):
    return [
        pltpu.make_async_copy(ref, normed_t.at[:, pl.ds(ROWS * h, ROWS)], sems.at[h])
        for h, ref in enumerate(refs)
    ]


def gradient(normed_t, dqkv, weight, outs, staged, gain_part, sems):
    copies = []
    places = [(0, 0), (1, 0), (2, 0), (4, PART), (4, 0), (5, 0), (5, PART), (3, 0)]
    for c, cols in enumerate(CHUNKS):
        for n in range(0, PIECES, 2):
            rows = slice(PART * n, PART * (n + 2))
            both = dot(normed_t[rows, :], dqkv[:, cols])
            product = both * weight[rows, cols].astype(F32)
            lanes = sum(
                product[:, TILE * k : TILE * (k + 1)] for k in range(cols.size // TILE)
            )
            gain_part[rows, :] = lanes if c == 0 else gain_part[rows, :] + lanes
            both = both.astype(BF)
            for k in (n, n + 1):
                staged[k, :, cols] = both[PART * (k - n) : PART * (k - n + 1)]
                copies.append(
                    pltpu.make_async_copy(
                        staged.at[k, :, cols],
                        outs[places[k][0]].at[pl.ds(places[k][1], PART), cols],
                        sems.at[c, k],
                    )
                )
                copies[-1].start()
    wait(copies)


def main_kernel(
    idx_ref,
    seg_ref,
    normed_ref,
    partner_ref,
    normed_t_ref,
    partner_t_ref,
    cot_ref,
    *refs,
):
    pieces, slots_ref, dqkv_ref = refs[:PIECES], refs[PIECES], refs[PIECES + 1]
    grads, gain_ref = refs[PIECES + 2 : PIECES + 8], refs[PIECES + 8]
    (
        normed,
        qkv,
        cot,
        weight,
        normed_t,
        dqkv,
        out_tiles,
        staged,
        row_sems,
        cot_sems,
        w_sems,
        t_sems,
        slot_sems,
        dqkv_sems,
        grad_sems,
    ) = refs[PIECES + 9 :]
    row_copies = load_rows((normed_ref, partner_ref), normed, row_sems)
    w_copies = load_weight(pieces, weight, w_sems)
    cot_copies = [
        pltpu.make_async_copy(cot_ref.at[j], cot.at[:, j], cot_sems.at[j])
        for j in range(N_DP)
    ]
    t_copies = load_features((normed_t_ref, partner_t_ref), normed_t, t_sems)
    start(row_copies)
    for copies in w_copies:
        start(copies)
    start(cot_copies)
    start(t_copies)
    wait(row_copies)
    for c, cols in enumerate(CHUNKS):
        wait(w_copies[c])
        qkv[:, cols] = dot(normed[...], weight[:, cols]).astype(BF)
    wait(cot_copies)

    def leave(t):
        rows = pl.ds(pl.multiple_of(t * TILE, TILE), TILE)
        return [
            pltpu.make_async_copy(
                out_tiles.at[t],
                slots_ref.at[idx_ref[t], idx_ref[2 * TILES + t]],
                slot_sems.at[t],
            ),
            pltpu.make_async_copy(dqkv.at[rows], dqkv_ref.at[rows], dqkv_sems.at[t]),
        ]

    @pl.loop(0, TILES)
    def _(step):
        pairs = range(8)
        tiles = [2 * step, 2 * step + 1]
        rows = [pl.ds(pl.multiple_of(t * TILE, TILE), TILE) for t in tiles]
        same = []
        for t in tiles:
            seg = jnp.broadcast_to(seg_ref[pl.ds(t, 1), :], (TILE, TILE))
            equal = seg == seg.T
            same.append(jnp.concatenate([equal, equal], axis=1))
        masks = [window_masks(i % 4) for i in pairs]
        windows = [slice(128 * (i % 4), 128 * (i % 4) + 256) for i in pairs]

        def window(a, i):
            first = HALF * a + 128 * (i % 4)
            return qkv[rows[i // 4], first : first + 256]

        q = [window(0, i) for i in pairs]
        d_out = [
            cot[tiles[i // 4], :, :, windows[i]].reshape(TILE, 256) for i in pairs
        ]
        kk = [stack_heads(window(1, i), masks[i]) for i in pairs]
        vv = [stack_heads(window(2, i), masks[i]) for i in pairs]
        scores = [dot(q[i], kk[i], NT) for i in pairs]
        d_probs = [dot(d_out[i], vv[i], NT) for i in pairs]
        scores = [
            jnp.where(same[i // 4], scores[i] * (SCALE * LOG2E), MASKED) for i in pairs
        ]
        tops = [halves(wide_max, x) for x in scores]
        expo = [jnp.exp2(x - m) for x, m in zip(scores, tops)]
        sums = [halves(wide_sum, x) for x in expo]
        weights = [x * (1.0 / total) for x, total in zip(expo, sums)]
        rounded = [x.astype(BF) for x in weights]
        outs = [dot(rounded[i], vv[i]) for i in pairs]
        dvs = [dot(rounded[i], d_out[i], TN) for i in pairs]
        inner = [halves(wide_sum, d_probs[i] * weights[i]) for i in pairs]
        d_scores = [
            (weights[i] * (d_probs[i] - inner[i]) * SCALE).astype(BF) for i in pairs
        ]
        dqs = [dot(d_scores[i], kk[i]) for i in pairs]
        dks = [dot(d_scores[i], q[i], TN) for i in pairs]
        dks = [pick_heads(dks[i], masks[i]) for i in pairs]
        dvs = [pick_heads(dvs[i], masks[i]) for i in pairs]

        def lanes(vals):
            parts = [vals[0][:, :TILE]]
            for i in range(3):
                parts.append(vals[i][:, TILE:] + vals[i + 1][:, :TILE])
            parts.append(vals[3][:, TILE:])
            return jnp.concatenate([p.astype(BF) for p in parts], axis=1)

        for n, t in enumerate(tiles):
            part = slice(4 * n, 4 * n + 4)
            out_tiles[t] = lanes(outs[part])
            for a, vals in enumerate((dqs, dks, dvs)):
                dqkv[rows[n], HALF * a : HALF * (a + 1)] = lanes(vals[part])
            start(leave(t))

    wait(t_copies)
    gradient(normed_t, dqkv, weight, grads, staged, gain_ref, grad_sems)
    for t in range(2 * TILES):
        wait(leave(t))


def main(index, seg, normed, normed_t, cot, pieces):
    return pl.pallas_call(
        main_kernel,
        in_specs=[SM, VM] + [ANY] * (5 + PIECES),
        out_specs=[ANY] * 8 + [VM],
        out_shape=[
            jax.ShapeDtypeStruct((N_DP, 2, TILE, HALF), BF),
            jax.ShapeDtypeStruct((PAIR_ROWS, COLS), BF),
        ]
        + [jax.ShapeDtypeStruct((PART, COLS), BF)] * 4
        + [jax.ShapeDtypeStruct((2 * PART, COLS), BF)] * 2
        + [jax.ShapeDtypeStruct((D, TILE), F32)],
        scratch_shapes=[
            pltpu.VMEM((PAIR_ROWS, D), BF),
            pltpu.VMEM((PAIR_ROWS, COLS), BF),
            pltpu.VMEM((2 * TILES, N_DP, STRIP, HALF), BF),
            pltpu.VMEM((D, COLS), BF),
            pltpu.VMEM((D, PAIR_ROWS), BF),
            pltpu.VMEM((PAIR_ROWS, COLS), BF),
            pltpu.VMEM((2 * TILES, TILE, HALF), BF),
            pltpu.VMEM((PIECES, PART, COLS), BF),
            pltpu.SemaphoreType.DMA((2,)),
            pltpu.SemaphoreType.DMA((N_DP,)),
            pltpu.SemaphoreType.DMA((len(CHUNKS), PIECES)),
            pltpu.SemaphoreType.DMA((2,)),
            pltpu.SemaphoreType.DMA((2 * TILES,)),
            pltpu.SemaphoreType.DMA((2 * TILES,)),
            pltpu.SemaphoreType.DMA((len(CHUNKS), PIECES)),
        ],
        compiler_params=params(58),
        cost_estimate=cost(8 * 10**9, 20 * 2**20, 10**6),
        name="main",
    )(index, seg, *normed, *normed_t, cot, *pieces)


def add_parts(counts, firsts, refs):
    totals, used = [], 0
    for count in counts:
        total = jnp.zeros((PART, COLS), F32)
        for k in range(used, used + count):
            total = total + refs[k][firsts[k] : firsts[k] + PART, :].astype(F32)
        used += count
        totals.append(total)
    return totals


def add_kernel(counts, firsts, *refs):
    totals = add_parts(counts, firsts, refs)
    for out_ref, total in zip(refs[sum(counts) :], totals):
        out_ref[...] = total.astype(BF)


def column_kernel(counts, firsts, gain_ref, other_ref, *refs):
    gain = gain_ref[...] + other_ref[...]
    outs = refs[sum(counts) :]
    totals = add_parts(counts, firsts, refs)
    for n, out_ref in enumerate(outs):
        block = totals[n // 2][BLOCK * (n % 2) : BLOCK * (n % 2 + 1)]
        out_ref[0:BLOCK, :] = block.astype(BF)
        put_gain(gain, out_ref, BLOCK, RIDE)


def put_gain(gain, ref, first, last):
    hi = gain.astype(BF).astype(F32)
    lo = gain - hi
    ref[first:last, :] = jnp.zeros((last - first, COLS), BF)
    for k in range(D // TILE):
        cols = slice(TILE * k, TILE * (k + 1))
        ref[first : first + 1, cols] = hi[k : k + 1].astype(BF)
        ref[first + 1 : first + 2, cols] = lo[k : k + 1].astype(BF)


def add(groups, gains=()):
    parts = [part for group in groups for part in group]
    rows, n = (RIDE, 2 * len(groups)) if gains else (PART, len(groups))
    return pl.pallas_call(
        functools.partial(
            column_kernel if gains else add_kernel,
            [len(group) for group in groups],
            [first for _, first in parts],
        ),
        in_specs=[VM] * (len(gains) + len(parts)),
        out_specs=[VM] * n,
        out_shape=[jax.ShapeDtypeStruct((rows, COLS), BF)] * n,
        compiler_params=params(12),
        cost_estimate=cost(0, 4 * len(parts) * PART * COLS),
        name="add",
    )(*gains, *[array for array, _ in parts])


def gain_kernel(part_ref, nat_ref, gain_ref, out_ref, perm_ref):
    build_order(nat_ref, perm_ref)
    rest = jnp.sum(part_ref[...], axis=1, keepdims=True)
    rest = jnp.broadcast_to(rest, (D, TILE))
    total = jnp.zeros((1, D), F32)
    for _ in range(3):
        term = rest.astype(BF)
        rest = rest - term.astype(F32)
        total = total + dot(term, perm_ref[...], TN)[0:1]
    total = total / gain_ref[...]
    out_ref[...] = jnp.zeros_like(out_ref)
    for k in range(D // TILE):
        out_ref[k : k + 1, :] = total[:, TILE * k : TILE * (k + 1)]


def gain_back(part, nat, gain):
    return pl.pallas_call(
        gain_kernel,
        in_specs=[VM] * 3,
        out_specs=VM,
        out_shape=jax.ShapeDtypeStruct((MSG, TILE), F32),
        scratch_shapes=[pltpu.VMEM((D, D), BF)],
        compiler_params=params(24),
        cost_estimate=cost(0, 4 * D * TILE),
        name="gain",
    )(part, nat, gain)


def back_kernel(half, nat_ref, dqkv_ref, *refs):
    pieces, (out_ref, weight, perm_ref, dqkv, w_sems, q_sem) = (
        refs[:PIECES],
        refs[PIECES:],
    )
    w_copies = load_weight(pieces, weight, w_sems)
    q_copy = pltpu.make_async_copy(dqkv_ref.at[pl.ds(ROWS * half, ROWS)], dqkv, q_sem)
    q_copy.start()
    for copies in w_copies:
        start(copies)
    build_order(nat_ref, perm_ref)
    q_copy.wait()
    for copies in w_copies:
        wait(copies)
    d_normed = dot(dqkv[...], weight[...], NT).astype(BF)
    out_ref[...] = dot(d_normed, perm_ref[...]).astype(BF)


def back(half, dqkv, pieces, nat):
    return pl.pallas_call(
        functools.partial(back_kernel, half),
        in_specs=[VM] + [ANY] * (1 + PIECES),
        out_specs=VM,
        out_shape=jax.ShapeDtypeStruct((ROWS, D), BF),
        scratch_shapes=[
            pltpu.VMEM((D, COLS), BF),
            pltpu.VMEM((D, D), BF),
            pltpu.VMEM((ROWS, COLS), BF),
            pltpu.SemaphoreType.DMA((len(CHUNKS), PIECES)),
            pltpu.SemaphoreType.DMA,
        ],
        compiler_params=params(58),
        cost_estimate=cost(2 * ROWS * D * (D + COLS), 15 * 2**20),
        name="back",
    )(nat, dqkv, *pieces)


def rows_kernel(patches_ref, gain_ref, mine_ref, other_ref, out_ref):
    standard, inv_std = norm_rows(patches_ref[...])
    d_normed = mine_ref[...].astype(F32) + other_ref[...].astype(F32)
    scaled = d_normed * gain_ref[...]
    back_rows = inv_std * (
        scaled
        - jnp.mean(scaled, axis=-1, keepdims=True)
        - standard * jnp.mean(scaled * standard, axis=-1, keepdims=True)
    )
    out_ref[...] = back_rows.astype(BF)


def rows_back(patches, gain, mine, other):
    block = pl.BlockSpec((TILE, D), lambda i: (i, 0))
    return pl.pallas_call(
        rows_kernel,
        grid=(TILES,),
        in_specs=[block, pl.BlockSpec((1, D), lambda i: (0, 0)), block, block],
        out_specs=block,
        out_shape=jax.ShapeDtypeStruct((ROWS, D), BF),
        compiler_params=params(58),
        cost_estimate=cost(20 * ROWS * D, 8 * ROWS * D),
        name="rows_back",
    )(patches, gain, mine, other)


def split_kernel(rows_ref, one_ref, two_ref, three_ref, out_ref):
    total = rows_ref[...].astype(F32)
    for ref in (one_ref, two_ref, three_ref):
        total = total + ref[...].astype(F32)
    both = total[BLOCK : BLOCK + 1, :D] + total[BLOCK + 1 : BLOCK + 2, :D]
    hi = both.astype(BF)
    lo = (both - hi.astype(F32)).astype(BF)
    total = total.astype(BF)
    for s in range(N_DP):
        out_ref[s, 0:OWN, :] = total[OWN * s : OWN * (s + 1)]
        out_ref[s, OWN:MSG, :] = jnp.zeros((MSG - OWN, COLS), BF)
        out_ref[s, OWN : OWN + 1, :D] = hi
        out_ref[s, OWN + 1 : OWN + 2, :D] = lo


def split(rows, others):
    return pl.pallas_call(
        split_kernel,
        in_specs=[VM] * 4,
        out_specs=VM,
        out_shape=jax.ShapeDtypeStruct((N_DP, MSG, COLS), BF),
        cost_estimate=cost(0, 4 * N_DP * MSG * COLS),
        compiler_params=params(12),
        name="split",
    )(rows, *others)


def finish_kernel(msg_ref, out_ref, gain_ref):
    both = jnp.zeros((MSG, COLS), F32)
    for half in range(2):
        total = msg_ref[half].astype(F32)
        for chip in range(1, 4):
            total = total + msg_ref[2 * chip + half].astype(F32)
        both = both + total
        for a in range(3):
            start = D * a + HALF * half
            out_ref[:, start : start + HALF] = total[0:OWN, HALF * a : HALF * (a + 1)]
    total = both[OWN : OWN + 1, :D] + both[OWN + 1 : OWN + 2, :D]
    for k in range(D // TILE):
        gain_ref[k : k + 1, :] = total[:, TILE * k : TILE * (k + 1)]


def finish(messages):
    return pl.pallas_call(
        finish_kernel,
        in_specs=[VM],
        out_specs=[VM, VM],
        out_shape=[
            jax.ShapeDtypeStruct((OWN, 3 * D), F32),
            jax.ShapeDtypeStruct((D // TILE, TILE), F32),
        ],
        cost_estimate=cost(0, 6 * N_DP * MSG * COLS),
        compiler_params=params(12),
        name="finish",
    )(messages)


def ring_pairs(df, ds):
    pairs = []
    for d in range(N_DP):
        dx, dz = (ds, df) if d % 2 else (df, ds)
        for x in range(4):
            for z in range(4):
                src = 4 * ((x + dx) % 4) + (z + dz) % 4
                pairs.append((N_INNER * d + src, N_INNER * d + 4 * x + z))
    return pairs


def double_pairs(f_bits, s_bits):
    pairs = []
    for d in range(N_DP):
        x_bits, z_bits = (s_bits, f_bits) if d % 2 else (f_bits, s_bits)
        flip = 4 * x_bits + z_bits
        pairs += [(N_INNER * d + (m ^ flip), N_INNER * d + m) for m in range(N_INNER)]
    return pairs


def from_ring(value, df, ds):
    return lax.ppermute(value, ("dp", "inner"), ring_pairs(df, ds))


def swap_cores(value):
    return lax.ppermute(value, "dp", [(d ^ 1, d) for d in range(N_DP)])


def exchange(value, axis="dp"):
    return lax.all_to_all(value, axis, split_axis=0, concat_axis=0, tiled=True)


def on_device(patches, segments, owners, norm_gain, qkv_weight, cotangent):
    group = lax.axis_index("dp")
    inner = lax.axis_index("inner")
    core, x, z = group % 2, inner // 4, inner % 4
    gain = norm_gain.reshape(1, D)

    pos = jnp.arange(N_INNER)
    df, ds = pos % 4, pos // 4
    m = 4 * ((x + jnp.where(core == 0, df, ds)) % 4) + (
        z + jnp.where(core == 0, ds, df)
    ) % 4
    nat = (
        (jnp.arange(N_DP)[None, :, None] * N_INNER + m[:, None, None]) * OWN
        + jnp.arange(OWN)[None, None, :]
    ).reshape(1, D).astype(F32)

    messages = exchange(build(owners, qkv_weight, segments))
    partner_patches = swap_cores(patches)
    own_prep = prep(patches, gain, nat)
    strips = cotangent.reshape(TILES, N_DP, STRIP, D).transpose(1, 0, 2, 3)
    messages, own_prep, strips = lax.optimization_barrier((messages, own_prep, strips))
    block, seg, owners_all = compact(group.reshape(1).astype(jnp.int32), messages)
    strips = exchange(strips)

    owner_of = owners_all[:, :TILES].astype(jnp.int32).reshape(N_DP * TILES)
    u = jnp.arange(N_DP * TILES)
    earlier = (owner_of[:, None] == owner_of[None, :]) & (
        u[None, :] // TILES < u[:, None] // TILES
    )
    fwd = (TILES * owner_of + jnp.sum(earlier, axis=1)).astype(jnp.int32)
    wanted = fwd[None, :] == TILES * group + jnp.arange(TILES)[:, None]
    source = jnp.sum(jnp.where(wanted, u[None, :] // TILES, 0), axis=1)
    place_index = jnp.concatenate([2 * (source // 2), source % 2]).astype(jnp.int32)
    mine = jnp.arange(2)[:, None] ^ core
    tile = (TILES * (group - core + mine) + jnp.arange(TILES)[None, :]).reshape(-1)
    owner_here = jnp.sum(jnp.where(tile[:, None] == u[None, :], owner_of, 0), axis=1)
    slot_index = jnp.concatenate(
        [owner_here, jnp.broadcast_to(mine, (2, TILES)).reshape(-1)]
    ).astype(jnp.int32)

    heads = to_heads(fwd, strips.reshape(N_DP * TILES, STRIP, D))
    cot = exchange(heads)

    ring = [block] + [from_ring(block, f, 0) for f in (1, 2, 3)]
    near_a, near_b = jnp.concatenate(ring[:2]), jnp.concatenate(ring[2:])
    above_a, below_b = from_ring(near_a, 0, 1), from_ring(near_b, 0, -1)
    above_b, below_a = from_ring(near_b, 0, 1), from_ring(near_a, 0, -1)
    above_a, above_b, below_a, below_b = lax.optimization_barrier(
        (above_a, above_b, below_a, below_b)
    )
    far_a, far_b = from_ring(above_a, 0, 1), from_ring(below_b, 0, -1)
    pieces = [near_a, near_b, above_a, above_b, far_a, far_b, below_a, below_b]
    normed, normed_t = zip(own_prep, prep(partner_patches, gain, nat))

    out, dqkv, col_a, col_b, up_a, down_b, up, down, gain_part = main(
        slot_index, seg, normed, normed_t, cot, pieces
    )

    up, down = from_ring(up, 0, -1), from_ring(down, 0, 1)
    slots = exchange(out)
    gain_part = gain_back(gain_part, nat, gain)
    gain_other = lax.ppermute(gain_part, ("dp", "inner"), double_pairs(0, 1))
    partners = back(1, dqkv, pieces, nat)
    up, down, gain_part, gain_other, partners = lax.optimization_barrier(
        (up, down, gain_part, gain_other, partners)
    )
    other = swap_cores(partners)
    up_a, down_b = add([[(up_a, 0), (up, 0)], [(down_b, 0), (down, 0)]])
    from_up_a, from_down_b = from_ring(up_a, 0, -1), from_ring(down_b, 0, 1)
    gain_part = gain_part + gain_other
    gain_other = lax.ppermute(gain_part, ("dp", "inner"), double_pairs(0, 3))
    zero, one, two, three = add(
        [
            [(col_a, 0), (from_up_a, 0), (down, PART)],
            [(col_b, 0), (up, PART), (from_down_b, 0)],
        ],
        (gain_part, gain_other),
    )
    dqkv, _ = lax.optimization_barrier((dqkv, zero))
    mine = back(0, dqkv, pieces, nat)
    others = [from_ring(two, -2, 0), from_ring(three, 1, 0), from_ring(one, -1, 0)]
    others[0], slots, mine = lax.optimization_barrier((others[0], slots, mine))

    attended = place(place_index, slots).reshape(ROWS, D)
    grad_rows = rows_back(patches, gain, mine, other)
    grad_qkv, grad_gain = finish(exchange(split(zero, others)))
    return (attended, grad_rows, grad_qkv, grad_gain.reshape(D))


def solution(mesh):
    both = ("dp", "inner")
    placed = (
        P(both, None),
        P(both, None),
        P(both),
        P(),
        P(both, None),
        P(both, None),
    )
    return jax.shard_map(
        on_device,
        mesh=mesh,
        in_specs=placed,
        out_specs=(P(both, None), P(both, None), P(both, None), P()),
        check_vma=False,
    )
```

```python
import functools

import jax
import jax.numpy as jnp
from jax import lax
from jax.experimental import pallas as pl
from jax.experimental.pallas import tpu as pltpu
from jax.sharding import PartitionSpec as P

D = 1280
HEADS = 16
HDIM = 80
TILE = 128
TILES = 3
N_DP = 8
N_INNER = 16
ROWS = TILES * TILE
PAIR_ROWS = 2 * ROWS
HALF = D // 2
COLS = 3 * HALF
OWN = 10
BLOCK = 80
PART = 160
PIECES = 8
RIDE = 88
STRIP = 16
MSG = 160
LANES = COLS // TILE
EPS = 1e-6
MASKED = -1e30
SCALE = HDIM ** (-0.5)
LOG2E = 1.4426950408889634
BF = jnp.bfloat16
F32 = jnp.float32
VM = pl.BlockSpec(memory_space=pltpu.VMEM)
SM = pl.BlockSpec(memory_space=pltpu.SMEM)
ANY = pl.BlockSpec(memory_space=pltpu.HBM)
NT = (((1,), (1,)), ((), ()))
TN = (((0,), (0,)), ((), ()))
NN = (((1,), (0,)), ((), ()))


def params(mib, **more):
    return pltpu.CompilerParams(vmem_limit_bytes=mib * 2**20, **more)


def cost(flops, nbytes, trans=0):
    return pl.CostEstimate(
        flops=flops // 1000, bytes_accessed=nbytes // 1000, transcendentals=trans // 1000
    )


def dot(a, b, dims=NN):
    return lax.dot_general(a, b, dims, preferred_element_type=F32)


def norm_rows(rows):
    wide = rows.astype(F32)
    centred = wide - jnp.mean(wide, axis=-1, keepdims=True)
    variance = jnp.mean(centred * centred, axis=-1, keepdims=True)
    inv_std = lax.rsqrt(variance + EPS)
    return centred * inv_std, inv_std


def build_order(nat_ref, perm_ref):
    for r in range(D // TILE):
        rows = slice(TILE * r, TILE * (r + 1))
        column = jnp.broadcast_to(nat_ref[:, rows], (TILE, TILE)).T
        for a in range(D // TILE):
            feature = lax.broadcasted_iota(jnp.int32, (TILE, TILE), 1) + TILE * a
            hit = column == feature.astype(F32)
            perm_ref[rows, TILE * a : TILE * (a + 1)] = jnp.where(hit, 1.0, 0.0).astype(BF)


def prep_kernel(patches_ref, gain_ref, nat_ref, normed_ref, normed_t_ref, perm_ref):
    build_order(nat_ref, perm_ref)
    standard, _ = norm_rows(patches_ref[...])
    normed = (standard * gain_ref[...]).astype(BF)
    normed_ref[...] = dot(normed, perm_ref[...], NT).astype(BF)
    normed_t_ref[...] = dot(perm_ref[...], normed, NT).astype(BF)


def prep(patches, gain, nat):
    return pl.pallas_call(
        prep_kernel,
        in_specs=[VM] * 3,
        out_specs=[VM] * 2,
        out_shape=[
            jax.ShapeDtypeStruct((ROWS, D), BF),
            jax.ShapeDtypeStruct((D, ROWS), BF),
        ],
        scratch_shapes=[pltpu.VMEM((D, D), BF)],
        compiler_params=params(58),
        cost_estimate=cost(4 * ROWS * D * D, 6 * ROWS * D),
        name="prep",
    )(patches, gain, nat)


def build_kernel(own_ref, w_ref, seg_ref, out_ref):
    lane = lax.broadcasted_iota(jnp.int32, (1, TILE), 1)
    owners = jnp.zeros((1, TILE), jnp.int32)
    for t in range(TILES):
        owners = jnp.where(lane == t, own_ref[t], owners)
    for half in range(2):
        for k in range(LANES):
            first = D * (k // 5) + HALF * half + TILE * (k % 5)
            out_ref[half, OWN * k : OWN * (k + 1), :] = w_ref[:, first : first + TILE]
        extras = OWN * LANES
        out_ref[half, extras:MSG, :] = jnp.zeros((MSG - extras, TILE), BF)
        out_ref[half, extras : extras + 1, :] = owners.astype(F32).astype(BF)
        out_ref[half, extras + 1 : extras + 1 + TILES, :] = (
            seg_ref[...].astype(F32).astype(BF)
        )
    for d in range(2, N_DP):
        out_ref[d] = out_ref[d % 2]


def build(owners, weight, segments):
    return pl.pallas_call(
        build_kernel,
        in_specs=[SM, VM, VM],
        out_specs=VM,
        out_shape=jax.ShapeDtypeStruct((N_DP, MSG, TILE), BF),
        compiler_params=params(58),
        cost_estimate=cost(0, 2 * N_DP * MSG * TILE),
        name="build",
    )(owners, weight, segments)


def compact_kernel(group_ref, msg_ref, w_ref, seg_ref, own_ref):
    group = group_ref[0]
    extras = OWN * LANES
    seg_ref[...] = jnp.zeros_like(seg_ref)
    for s in range(N_DP):
        for k in range(LANES):
            w_ref[OWN * s : OWN * (s + 1), TILE * k : TILE * (k + 1)] = msg_ref[
                s, OWN * k : OWN * (k + 1), :
            ]
        own_ref[s : s + 1, :] = msg_ref[s, extras : extras + 1, :].astype(F32)
    for rel in range(2):
        src = group + rel * (1 - 2 * (group % 2))
        seg_ref[TILES * rel : TILES * (rel + 1), :] = msg_ref[
            src, extras + 1 : extras + 1 + TILES, :
        ].astype(F32)


def compact(group, messages):
    return pl.pallas_call(
        compact_kernel,
        in_specs=[SM, VM],
        out_specs=[VM] * 3,
        out_shape=[
            jax.ShapeDtypeStruct((BLOCK, COLS), BF),
            jax.ShapeDtypeStruct((8, TILE), F32),
            jax.ShapeDtypeStruct((N_DP, TILE), F32),
        ],
        compiler_params=params(12),
        cost_estimate=cost(0, 4 * N_DP * MSG * TILE),
        name="compact",
    )(group, messages)


def to_heads_kernel(fwd_ref, in_ref, out_ref):
    for d in range(N_DP):
        half = slice(HALF * (d % 2), HALF * (d % 2 + 1))
        for k in range(2 * TILES):
            u = TILES * (2 * (d // 2) + ((d % 2) ^ (k // TILES))) + k % TILES
            out_ref[d, k] = in_ref[fwd_ref[u], :, half]


def to_heads(fwd, strips):
    return pl.pallas_call(
        to_heads_kernel,
        in_specs=[SM, VM],
        out_specs=VM,
        out_shape=jax.ShapeDtypeStruct((N_DP, 2 * TILES, STRIP, HALF), BF),
        cost_estimate=cost(0, 4 * ROWS * D),
        compiler_params=params(12),
        name="to_heads",
    )(fwd, strips)


def place_kernel(idx_ref, left_ref, right_ref, out_ref):
    out_ref[0, :, :HALF] = left_ref[0, 0]
    out_ref[0, :, HALF:] = right_ref[0, 0]


def place(index, slots):
    def half(c):
        return pl.BlockSpec(
            (1, 1, TILE, HALF), lambda p, g: (g[p] + c, g[TILES + p], 0, 0)
        )

    spec = pltpu.PrefetchScalarGridSpec(
        num_scalar_prefetch=1,
        grid=(TILES,),
        in_specs=[half(0), half(1)],
        out_specs=pl.BlockSpec((1, TILE, D), lambda p, g: (p, 0, 0)),
    )
    return pl.pallas_call(
        place_kernel,
        grid_spec=spec,
        out_shape=jax.ShapeDtypeStruct((TILES, TILE, D), BF),
        compiler_params=params(12),
        cost_estimate=cost(0, 4 * ROWS * D),
        name="place",
    )(index, slots, slots)


def window_masks(i):
    lane = lax.broadcasted_iota(jnp.int32, (TILE, 256), 1)
    start = 32 * i
    first = (lane >= start) & (lane < start + HDIM)
    second = (lane >= start + HDIM) & (lane < start + 2 * HDIM)
    return first, second


def stack_heads(window, masks):
    zero = jnp.zeros_like(window)
    return jnp.concatenate([jnp.where(m, window, zero) for m in masks], axis=0)


def pick_heads(stacked, masks):
    zero = jnp.zeros((TILE, 256), F32)
    return jnp.where(
        masks[0], stacked[:TILE], jnp.where(masks[1], stacked[TILE:], zero)
    )


def halves(fn, *arrays):
    return jnp.concatenate(
        [fn(*(a[:, :TILE] for a in arrays)), fn(*(a[:, TILE:] for a in arrays))], axis=1
    )


def wide_max(a):
    return jnp.broadcast_to(jnp.max(a, axis=-1, keepdims=True), a.shape)


def wide_sum(a):
    return jnp.broadcast_to(jnp.sum(a, axis=-1, keepdims=True), a.shape)


CHUNKS = [pl.ds(0, 768), pl.ds(768, 768), pl.ds(1536, 384)]


def start(copies):
    for copy in copies:
        copy.start()


def wait(copies):
    for copy in copies:
        copy.wait()


def load_weight(pieces, weight, sems):
    return [
        [
            pltpu.make_async_copy(
                piece.at[:, cols],
                weight.at[pl.ds(PART * b, PART), cols],
                sems.at[n, b],
            )
            for b, piece in enumerate(pieces)
        ]
        for n, cols in enumerate(CHUNKS)
    ]


def load_rows(refs, rows, sems):
    return [
        pltpu.make_async_copy(ref, rows.at[pl.ds(ROWS * h, ROWS)], sems.at[h])
        for h, ref in enumerate(refs)
    ]


def load_features(refs, normed_t, sems):
    return [
        pltpu.make_async_copy(ref, normed_t.at[:, pl.ds(ROWS * h, ROWS)], sems.at[h])
        for h, ref in enumerate(refs)
    ]


def gradient(normed_t, dqkv, weight, outs, staged, gain_part, sems):
    copies = []
    places = [(0, 0), (1, 0), (2, 0), (4, PART), (4, 0), (5, 0), (5, PART), (3, 0)]
    for c, cols in enumerate(CHUNKS):
        for n in range(0, PIECES, 2):
            rows = slice(PART * n, PART * (n + 2))
            both = dot(normed_t[rows, :], dqkv[:, cols])
            product = both * weight[rows, cols].astype(F32)
            lanes = sum(
                product[:, TILE * k : TILE * (k + 1)] for k in range(cols.size // TILE)
            )
            gain_part[rows, :] = lanes if c == 0 else gain_part[rows, :] + lanes
            both = both.astype(BF)
            for k in (n, n + 1):
                staged[k, :, cols] = both[PART * (k - n) : PART * (k - n + 1)]
                copies.append(
                    pltpu.make_async_copy(
                        staged.at[k, :, cols],
                        outs[places[k][0]].at[pl.ds(places[k][1], PART), cols],
                        sems.at[c, k],
                    )
                )
                copies[-1].start()
    wait(copies)


def main_kernel(
    idx_ref,
    seg_ref,
    normed_ref,
    partner_ref,
    normed_t_ref,
    partner_t_ref,
    cot_ref,
    *refs,
):
    pieces, slots_ref, dqkv_ref = refs[:PIECES], refs[PIECES], refs[PIECES + 1]
    grads, gain_ref = refs[PIECES + 2 : PIECES + 8], refs[PIECES + 8]
    (
        normed,
        qkv,
        cot,
        weight,
        normed_t,
        dqkv,
        out_tiles,
        staged,
        row_sems,
        cot_sems,
        w_sems,
        t_sems,
        slot_sems,
        dqkv_sems,
        grad_sems,
    ) = refs[PIECES + 9 :]
    row_copies = load_rows((normed_ref, partner_ref), normed, row_sems)
    w_copies = load_weight(pieces, weight, w_sems)
    cot_copies = [
        pltpu.make_async_copy(cot_ref.at[j], cot.at[:, j], cot_sems.at[j])
        for j in range(N_DP)
    ]
    t_copies = load_features((normed_t_ref, partner_t_ref), normed_t, t_sems)
    start(row_copies)
    for copies in w_copies:
        start(copies)
    start(cot_copies)
    start(t_copies)
    wait(row_copies)
    for c, cols in enumerate(CHUNKS):
        wait(w_copies[c])
        qkv[:, cols] = dot(normed[...], weight[:, cols]).astype(BF)
    wait(cot_copies)

    def leave(t):
        rows = pl.ds(pl.multiple_of(t * TILE, TILE), TILE)
        return [
            pltpu.make_async_copy(
                out_tiles.at[t],
                slots_ref.at[idx_ref[t], idx_ref[2 * TILES + t]],
                slot_sems.at[t],
            ),
            pltpu.make_async_copy(dqkv.at[rows], dqkv_ref.at[rows], dqkv_sems.at[t]),
        ]

    @pl.loop(0, TILES)
    def _(step):
        pairs = range(8)
        tiles = [2 * step, 2 * step + 1]
        rows = [pl.ds(pl.multiple_of(t * TILE, TILE), TILE) for t in tiles]
        same = []
        for t in tiles:
            seg = jnp.broadcast_to(seg_ref[pl.ds(t, 1), :], (TILE, TILE))
            equal = seg == seg.T
            same.append(jnp.concatenate([equal, equal], axis=1))
        masks = [window_masks(i % 4) for i in pairs]
        windows = [slice(128 * (i % 4), 128 * (i % 4) + 256) for i in pairs]

        def window(a, i):
            first = HALF * a + 128 * (i % 4)
            return qkv[rows[i // 4], first : first + 256]

        q = [window(0, i) for i in pairs]
        d_out = [
            cot[tiles[i // 4], :, :, windows[i]].reshape(TILE, 256) for i in pairs
        ]
        kk = [stack_heads(window(1, i), masks[i]) for i in pairs]
        vv = [stack_heads(window(2, i), masks[i]) for i in pairs]
        scores = [dot(q[i], kk[i], NT) for i in pairs]
        d_probs = [dot(d_out[i], vv[i], NT) for i in pairs]
        scores = [
            jnp.where(same[i // 4], scores[i] * (SCALE * LOG2E), MASKED) for i in pairs
        ]
        tops = [halves(wide_max, x) for x in scores]
        expo = [jnp.exp2(x - m) for x, m in zip(scores, tops)]
        sums = [halves(wide_sum, x) for x in expo]
        weights = [x * (1.0 / total) for x, total in zip(expo, sums)]
        rounded = [x.astype(BF) for x in weights]
        outs = [dot(rounded[i], vv[i]) for i in pairs]
        dvs = [dot(rounded[i], d_out[i], TN) for i in pairs]
        inner = [halves(wide_sum, d_probs[i] * weights[i]) for i in pairs]
        d_scores = [
            (weights[i] * (d_probs[i] - inner[i]) * SCALE).astype(BF) for i in pairs
        ]
        dqs = [dot(d_scores[i], kk[i]) for i in pairs]
        dks = [dot(d_scores[i], q[i], TN) for i in pairs]
        dks = [pick_heads(dks[i], masks[i]) for i in pairs]
        dvs = [pick_heads(dvs[i], masks[i]) for i in pairs]

        def lanes(vals):
            parts = [vals[0][:, :TILE]]
            for i in range(3):
                parts.append(vals[i][:, TILE:] + vals[i + 1][:, :TILE])
            parts.append(vals[3][:, TILE:])
            return jnp.concatenate([p.astype(BF) for p in parts], axis=1)

        for n, t in enumerate(tiles):
            part = slice(4 * n, 4 * n + 4)
            out_tiles[t] = lanes(outs[part])
            for a, vals in enumerate((dqs, dks, dvs)):
                dqkv[rows[n], HALF * a : HALF * (a + 1)] = lanes(vals[part])
            start(leave(t))

    wait(t_copies)
    gradient(normed_t, dqkv, weight, grads, staged, gain_ref, grad_sems)
    for t in range(2 * TILES):
        wait(leave(t))


def main(index, seg, normed, normed_t, cot, pieces):
    return pl.pallas_call(
        main_kernel,
        in_specs=[SM, VM] + [ANY] * (5 + PIECES),
        out_specs=[ANY] * 8 + [VM],
        out_shape=[
            jax.ShapeDtypeStruct((N_DP, 2, TILE, HALF), BF),
            jax.ShapeDtypeStruct((PAIR_ROWS, COLS), BF),
        ]
        + [jax.ShapeDtypeStruct((PART, COLS), BF)] * 4
        + [jax.ShapeDtypeStruct((2 * PART, COLS), BF)] * 2
        + [jax.ShapeDtypeStruct((D, TILE), F32)],
        scratch_shapes=[
            pltpu.VMEM((PAIR_ROWS, D), BF),
            pltpu.VMEM((PAIR_ROWS, COLS), BF),
            pltpu.VMEM((2 * TILES, N_DP, STRIP, HALF), BF),
            pltpu.VMEM((D, COLS), BF),
            pltpu.VMEM((D, PAIR_ROWS), BF),
            pltpu.VMEM((PAIR_ROWS, COLS), BF),
            pltpu.VMEM((2 * TILES, TILE, HALF), BF),
            pltpu.VMEM((PIECES, PART, COLS), BF),
            pltpu.SemaphoreType.DMA((2,)),
            pltpu.SemaphoreType.DMA((N_DP,)),
            pltpu.SemaphoreType.DMA((len(CHUNKS), PIECES)),
            pltpu.SemaphoreType.DMA((2,)),
            pltpu.SemaphoreType.DMA((2 * TILES,)),
            pltpu.SemaphoreType.DMA((2 * TILES,)),
            pltpu.SemaphoreType.DMA((len(CHUNKS), PIECES)),
        ],
        compiler_params=params(58),
        cost_estimate=cost(8 * 10**9, 20 * 2**20, 10**6),
        name="main",
    )(index, seg, *normed, *normed_t, cot, *pieces)


def add_parts(counts, firsts, refs):
    totals, used = [], 0
    for count in counts:
        total = jnp.zeros((PART, COLS), F32)
        for k in range(used, used + count):
            total = total + refs[k][firsts[k] : firsts[k] + PART, :].astype(F32)
        used += count
        totals.append(total)
    return totals


def add_kernel(counts, firsts, *refs):
    totals = add_parts(counts, firsts, refs)
    for out_ref, total in zip(refs[sum(counts) :], totals):
        out_ref[...] = total.astype(BF)


def column_kernel(counts, firsts, gain_ref, other_ref, *refs):
    gain = gain_ref[...] + other_ref[...]
    outs = refs[sum(counts) :]
    totals = add_parts(counts, firsts, refs)
    for n, out_ref in enumerate(outs):
        block = totals[n // 2][BLOCK * (n % 2) : BLOCK * (n % 2 + 1)]
        out_ref[0:BLOCK, :] = block.astype(BF)
        put_gain(gain, out_ref, BLOCK, RIDE)


def put_gain(gain, ref, first, last):
    hi = gain.astype(BF).astype(F32)
    lo = gain - hi
    ref[first:last, :] = jnp.zeros((last - first, COLS), BF)
    for k in range(D // TILE):
        cols = slice(TILE * k, TILE * (k + 1))
        ref[first : first + 1, cols] = hi[k : k + 1].astype(BF)
        ref[first + 1 : first + 2, cols] = lo[k : k + 1].astype(BF)


def add(groups, gains=()):
    parts = [part for group in groups for part in group]
    rows, n = (RIDE, 2 * len(groups)) if gains else (PART, len(groups))
    return pl.pallas_call(
        functools.partial(
            column_kernel if gains else add_kernel,
            [len(group) for group in groups],
            [first for _, first in parts],
        ),
        in_specs=[VM] * (len(gains) + len(parts)),
        out_specs=[VM] * n,
        out_shape=[jax.ShapeDtypeStruct((rows, COLS), BF)] * n,
        compiler_params=params(12),
        cost_estimate=cost(0, (4 if gains else 24000) * len(parts) * PART * COLS),
        name="add",
    )(*gains, *[array for array, _ in parts])


def gain_kernel(part_ref, nat_ref, gain_ref, out_ref, perm_ref):
    build_order(nat_ref, perm_ref)
    rest = jnp.sum(part_ref[...], axis=1, keepdims=True)
    rest = jnp.broadcast_to(rest, (D, TILE))
    total = jnp.zeros((1, D), F32)
    for _ in range(3):
        term = rest.astype(BF)
        rest = rest - term.astype(F32)
        total = total + dot(term, perm_ref[...], TN)[0:1]
    total = total / gain_ref[...]
    out_ref[...] = jnp.zeros_like(out_ref)
    for k in range(D // TILE):
        out_ref[k : k + 1, :] = total[:, TILE * k : TILE * (k + 1)]


def gain_back(part, nat, gain):
    return pl.pallas_call(
        gain_kernel,
        in_specs=[VM] * 3,
        out_specs=VM,
        out_shape=jax.ShapeDtypeStruct((STRIP, TILE), F32),
        scratch_shapes=[pltpu.VMEM((D, D), BF)],
        compiler_params=params(24),
        cost_estimate=cost(0, 4 * D * TILE),
        name="gain",
    )(part, nat, gain)


def back_kernel(half, nat_ref, dqkv_ref, *refs):
    pieces, (out_ref, weight, perm_ref, dqkv, w_sems, q_sem) = (
        refs[:PIECES],
        refs[PIECES:],
    )
    w_copies = load_weight(pieces, weight, w_sems)
    q_copy = pltpu.make_async_copy(dqkv_ref.at[pl.ds(ROWS * half, ROWS)], dqkv, q_sem)
    q_copy.start()
    for copies in w_copies:
        start(copies)
    build_order(nat_ref, perm_ref)
    q_copy.wait()
    for copies in w_copies:
        wait(copies)
    d_normed = dot(dqkv[...], weight[...], NT).astype(BF)
    out_ref[...] = dot(d_normed, perm_ref[...]).astype(BF)


def back(half, dqkv, pieces, nat):
    return pl.pallas_call(
        functools.partial(back_kernel, half),
        in_specs=[VM] + [ANY] * (1 + PIECES),
        out_specs=VM,
        out_shape=jax.ShapeDtypeStruct((ROWS, D), BF),
        scratch_shapes=[
            pltpu.VMEM((D, COLS), BF),
            pltpu.VMEM((D, D), BF),
            pltpu.VMEM((ROWS, COLS), BF),
            pltpu.SemaphoreType.DMA((len(CHUNKS), PIECES)),
            pltpu.SemaphoreType.DMA,
        ],
        compiler_params=params(58),
        cost_estimate=cost(2 * ROWS * D * (D + COLS), 15 * 2**20),
        name="back",
    )(nat, dqkv, *pieces)


def rows_kernel(patches_ref, gain_ref, mine_ref, other_ref, out_ref):
    standard, inv_std = norm_rows(patches_ref[...])
    d_normed = mine_ref[...].astype(F32) + other_ref[...].astype(F32)
    scaled = d_normed * gain_ref[...]
    back_rows = inv_std * (
        scaled
        - jnp.mean(scaled, axis=-1, keepdims=True)
        - standard * jnp.mean(scaled * standard, axis=-1, keepdims=True)
    )
    out_ref[...] = back_rows.astype(BF)


def rows_back(patches, gain, mine, other):
    block = pl.BlockSpec((TILE, D), lambda i: (i, 0))
    return pl.pallas_call(
        rows_kernel,
        grid=(TILES,),
        in_specs=[block, pl.BlockSpec((1, D), lambda i: (0, 0)), block, block],
        out_specs=block,
        out_shape=jax.ShapeDtypeStruct((ROWS, D), BF),
        compiler_params=params(58),
        cost_estimate=cost(20 * ROWS * D, 8 * ROWS * D),
        name="rows_back",
    )(patches, gain, mine, other)


def split_kernel(rows_ref, one_ref, two_ref, three_ref, out_ref):
    total = rows_ref[...].astype(F32)
    for ref in (one_ref, two_ref, three_ref):
        total = total + ref[...].astype(F32)
    gain = total[BLOCK : BLOCK + 1, :D] + total[BLOCK + 1 : BLOCK + 2, :D]
    gain = gain.astype(BF)
    total = total.astype(BF)
    extras = OWN * LANES
    for s in range(N_DP):
        for k in range(LANES):
            out_ref[s, OWN * k : OWN * (k + 1), :] = total[
                OWN * s : OWN * (s + 1), TILE * k : TILE * (k + 1)
            ]
        for k in range(D // TILE):
            out_ref[s, extras + k : extras + k + 1, :] = gain[
                :, TILE * k : TILE * (k + 1)
            ]


def split(rows, others):
    return pl.pallas_call(
        split_kernel,
        in_specs=[VM] * 4,
        out_specs=VM,
        out_shape=jax.ShapeDtypeStruct((N_DP, MSG, TILE), BF),
        compiler_params=params(12),
        cost_estimate=cost(0, 4 * N_DP * MSG * TILE),
        name="split",
    )(rows, *others)


def finish_kernel(msg_ref, out_ref, gain_ref):
    both = jnp.zeros((MSG, TILE), F32)
    for half in range(2):
        total = msg_ref[half].astype(F32)
        for chip in range(1, 4):
            total = total + msg_ref[2 * chip + half].astype(F32)
        both = both + total
        for k in range(LANES):
            first = D * (k // 5) + HALF * half + TILE * (k % 5)
            out_ref[:, first : first + TILE] = total[OWN * k : OWN * (k + 1)]
    gain_ref[...] = both[OWN * LANES : MSG]


def finish(messages):
    return pl.pallas_call(
        finish_kernel,
        in_specs=[VM],
        out_specs=[VM, VM],
        out_shape=[
            jax.ShapeDtypeStruct((OWN, 3 * D), F32),
            jax.ShapeDtypeStruct((D // TILE, TILE), F32),
        ],
        compiler_params=params(12),
        cost_estimate=cost(0, 6 * N_DP * MSG * TILE),
        name="finish",
    )(messages)


def ring_pairs(df, ds):
    pairs = []
    for d in range(N_DP):
        dx, dz = (ds, df) if d % 2 else (df, ds)
        for x in range(4):
            for z in range(4):
                src = 4 * ((x + dx) % 4) + (z + dz) % 4
                pairs.append((N_INNER * d + src, N_INNER * d + 4 * x + z))
    return pairs


def double_pairs(f_bits, s_bits):
    pairs = []
    for d in range(N_DP):
        x_bits, z_bits = (s_bits, f_bits) if d % 2 else (f_bits, s_bits)
        flip = 4 * x_bits + z_bits
        pairs += [(N_INNER * d + (m ^ flip), N_INNER * d + m) for m in range(N_INNER)]
    return pairs


def from_ring(value, df, ds):
    return lax.ppermute(value, ("dp", "inner"), ring_pairs(df, ds))


def swap_cores(value):
    return lax.ppermute(value, "dp", [(d ^ 1, d) for d in range(N_DP)])


def exchange(value, axis="dp"):
    return lax.all_to_all(value, axis, split_axis=0, concat_axis=0, tiled=True)


def on_device(patches, segments, owners, norm_gain, qkv_weight, cotangent):
    group = lax.axis_index("dp")
    inner = lax.axis_index("inner")
    core, x, z = group % 2, inner // 4, inner % 4
    gain = norm_gain.reshape(1, D)

    pos = jnp.arange(N_INNER)
    df, ds = pos % 4, pos // 4
    m = 4 * ((x + jnp.where(core == 0, df, ds)) % 4) + (
        z + jnp.where(core == 0, ds, df)
    ) % 4
    nat = (
        (jnp.arange(N_DP)[None, :, None] * N_INNER + m[:, None, None]) * OWN
        + jnp.arange(OWN)[None, None, :]
    ).reshape(1, D).astype(F32)

    messages = exchange(build(owners, qkv_weight, segments))
    partner_patches = swap_cores(patches)
    own_prep = prep(patches, gain, nat)
    strips = cotangent.reshape(TILES, N_DP, STRIP, D).transpose(1, 0, 2, 3)
    messages, own_prep, strips = lax.optimization_barrier((messages, own_prep, strips))
    block, seg, owners_all = compact(group.reshape(1).astype(jnp.int32), messages)
    strips = exchange(strips)

    owner_of = owners_all[:, :TILES].astype(jnp.int32).reshape(N_DP * TILES)
    u = jnp.arange(N_DP * TILES)
    earlier = (owner_of[:, None] == owner_of[None, :]) & (
        u[None, :] // TILES < u[:, None] // TILES
    )
    fwd = (TILES * owner_of + jnp.sum(earlier, axis=1)).astype(jnp.int32)
    wanted = fwd[None, :] == TILES * group + jnp.arange(TILES)[:, None]
    source = jnp.sum(jnp.where(wanted, u[None, :] // TILES, 0), axis=1)
    place_index = jnp.concatenate([2 * (source // 2), source % 2]).astype(jnp.int32)
    mine = jnp.arange(2)[:, None] ^ core
    tile = (TILES * (group - core + mine) + jnp.arange(TILES)[None, :]).reshape(-1)
    owner_here = jnp.sum(jnp.where(tile[:, None] == u[None, :], owner_of, 0), axis=1)
    slot_index = jnp.concatenate(
        [owner_here, jnp.broadcast_to(mine, (2, TILES)).reshape(-1)]
    ).astype(jnp.int32)

    heads = to_heads(fwd, strips.reshape(N_DP * TILES, STRIP, D))
    cot = exchange(heads)

    ring = [block] + [from_ring(block, f, 0) for f in (1, 2, 3)]
    near_a, near_b = jnp.concatenate(ring[:2]), jnp.concatenate(ring[2:])
    above_a, below_b = from_ring(near_a, 0, 1), from_ring(near_b, 0, -1)
    above_b, below_a = from_ring(near_b, 0, 1), from_ring(near_a, 0, -1)
    above_a, above_b, below_a, below_b = lax.optimization_barrier(
        (above_a, above_b, below_a, below_b)
    )
    far_a, far_b = from_ring(above_a, 0, 1), from_ring(below_b, 0, -1)
    pieces = [near_a, near_b, above_a, above_b, far_a, far_b, below_a, below_b]
    normed, normed_t = zip(own_prep, prep(partner_patches, gain, nat))

    out, dqkv, col_a, col_b, up_a, down_b, up, down, gain_part = main(
        slot_index, seg, normed, normed_t, cot, pieces
    )

    up, down = from_ring(up, 0, -1), from_ring(down, 0, 1)
    slots = exchange(out)
    gain_part = gain_back(gain_part, nat, gain)
    gain_other = lax.ppermute(gain_part, ("dp", "inner"), double_pairs(0, 1))
    partners = back(1, dqkv, pieces, nat)
    up, down, gain_part, gain_other, partners = lax.optimization_barrier(
        (up, down, gain_part, gain_other, partners)
    )
    other = swap_cores(partners)
    up_a, down_b = add([[(up_a, 0), (up, 0)], [(down_b, 0), (down, 0)]])
    from_up_a, from_down_b = from_ring(up_a, 0, -1), from_ring(down_b, 0, 1)
    gain_part = gain_part + gain_other
    gain_other = lax.ppermute(gain_part, ("dp", "inner"), double_pairs(0, 3))
    zero, one, two, three = add(
        [
            [(col_a, 0), (from_up_a, 0), (down, PART)],
            [(col_b, 0), (up, PART), (from_down_b, 0)],
        ],
        (gain_part, gain_other),
    )
    dqkv, _ = lax.optimization_barrier((dqkv, zero))
    mine = back(0, dqkv, pieces, nat)
    others = [from_ring(two, -2, 0), from_ring(three, 1, 0), from_ring(one, -1, 0)]
    others[0], slots, mine = lax.optimization_barrier((others[0], slots, mine))

    attended = place(place_index, slots).reshape(ROWS, D)
    grad_rows = rows_back(patches, gain, mine, other)
    grad_qkv, grad_gain = finish(exchange(split(zero, others)))
    return (attended, grad_rows, grad_qkv, grad_gain.reshape(D))


def solution(mesh):
    both = ("dp", "inner")
    placed = (
        P(both, None),
        P(both, None),
        P(both),
        P(),
        P(both, None),
        P(both, None),
    )
    return jax.shard_map(
        on_device,
        mesh=mesh,
        in_specs=placed,
        out_specs=(P(both, None), P(both, None), P(both, None), P()),
        check_vma=False,
    )
```

```python
import functools

import jax
import jax.numpy as jnp
from jax import lax
from jax.experimental import pallas as pl
from jax.experimental.pallas import tpu as pltpu
from jax.sharding import PartitionSpec as P

D = 1280
HEADS = 16
HDIM = 80
TILE = 128
TILES = 3
N_DP = 8
N_INNER = 16
ROWS = TILES * TILE
PAIR_ROWS = 2 * ROWS
HALF = D // 2
COLS = 3 * HALF
OWN = 10
BLOCK = 80
PART = 160
PIECES = 8
RIDE = 88
STRIP = 16
MSG = 160
LANES = COLS // TILE
EPS = 1e-6
MASKED = -1e30
SCALE = HDIM ** (-0.5)
LOG2E = 1.4426950408889634
BF = jnp.bfloat16
F32 = jnp.float32
VM = pl.BlockSpec(memory_space=pltpu.VMEM)
SM = pl.BlockSpec(memory_space=pltpu.SMEM)
ANY = pl.BlockSpec(memory_space=pltpu.HBM)
NT = (((1,), (1,)), ((), ()))
TN = (((0,), (0,)), ((), ()))
NN = (((1,), (0,)), ((), ()))


def params(mib, **more):
    return pltpu.CompilerParams(vmem_limit_bytes=mib * 2**20, **more)


def cost(flops, nbytes, trans=0):
    return pl.CostEstimate(
        flops=flops // 1000, bytes_accessed=nbytes // 1000, transcendentals=trans // 1000
    )


def dot(a, b, dims=NN):
    return lax.dot_general(a, b, dims, preferred_element_type=F32)


def norm_rows(rows):
    wide = rows.astype(F32)
    centred = wide - jnp.mean(wide, axis=-1, keepdims=True)
    variance = jnp.mean(centred * centred, axis=-1, keepdims=True)
    inv_std = lax.rsqrt(variance + EPS)
    return centred * inv_std, inv_std


def build_order(nat_ref, perm_ref):
    for r in range(D // TILE):
        rows = slice(TILE * r, TILE * (r + 1))
        column = jnp.broadcast_to(nat_ref[:, rows], (TILE, TILE)).T
        for a in range(D // TILE):
            feature = lax.broadcasted_iota(jnp.int32, (TILE, TILE), 1) + TILE * a
            hit = column == feature.astype(F32)
            perm_ref[rows, TILE * a : TILE * (a + 1)] = jnp.where(hit, 1.0, 0.0).astype(BF)


def prep_kernel(patches_ref, gain_ref, nat_ref, normed_ref, normed_t_ref, perm_ref):
    build_order(nat_ref, perm_ref)
    standard, _ = norm_rows(patches_ref[...])
    normed = (standard * gain_ref[...]).astype(BF)
    normed_ref[...] = dot(normed, perm_ref[...], NT).astype(BF)
    normed_t_ref[...] = dot(perm_ref[...], normed, NT).astype(BF)


def prep(patches, gain, nat):
    return pl.pallas_call(
        prep_kernel,
        in_specs=[VM] * 3,
        out_specs=[VM] * 2,
        out_shape=[
            jax.ShapeDtypeStruct((ROWS, D), BF),
            jax.ShapeDtypeStruct((D, ROWS), BF),
        ],
        scratch_shapes=[pltpu.VMEM((D, D), BF)],
        compiler_params=params(58),
        cost_estimate=cost(4 * ROWS * D * D, 6 * ROWS * D),
        name="prep",
    )(patches, gain, nat)


def build_kernel(own_ref, w_ref, seg_ref, out_ref):
    lane = lax.broadcasted_iota(jnp.int32, (1, TILE), 1)
    owners = jnp.zeros((1, TILE), jnp.int32)
    for t in range(TILES):
        owners = jnp.where(lane == t, own_ref[t], owners)
    for half in range(2):
        for k in range(LANES):
            first = D * (k // 5) + HALF * half + TILE * (k % 5)
            out_ref[half, OWN * k : OWN * (k + 1), :] = w_ref[:, first : first + TILE]
        extras = OWN * LANES
        out_ref[half, extras:MSG, :] = jnp.zeros((MSG - extras, TILE), BF)
        out_ref[half, extras : extras + 1, :] = owners.astype(F32).astype(BF)
        out_ref[half, extras + 1 : extras + 1 + TILES, :] = (
            seg_ref[...].astype(F32).astype(BF)
        )
    for d in range(2, N_DP):
        out_ref[d] = out_ref[d % 2]


def build(owners, weight, segments):
    return pl.pallas_call(
        build_kernel,
        in_specs=[SM, VM, VM],
        out_specs=VM,
        out_shape=jax.ShapeDtypeStruct((N_DP, MSG, TILE), BF),
        compiler_params=params(58),
        cost_estimate=cost(0, 2 * N_DP * MSG * TILE),
        name="build",
    )(owners, weight, segments)


def compact_kernel(group_ref, msg_ref, w_ref, seg_ref, own_ref):
    group = group_ref[0]
    extras = OWN * LANES
    seg_ref[...] = jnp.zeros_like(seg_ref)
    for s in range(N_DP):
        for k in range(LANES):
            w_ref[OWN * s : OWN * (s + 1), TILE * k : TILE * (k + 1)] = msg_ref[
                s, OWN * k : OWN * (k + 1), :
            ]
        own_ref[s : s + 1, :] = msg_ref[s, extras : extras + 1, :].astype(F32)
    for rel in range(2):
        src = group + rel * (1 - 2 * (group % 2))
        seg_ref[TILES * rel : TILES * (rel + 1), :] = msg_ref[
            src, extras + 1 : extras + 1 + TILES, :
        ].astype(F32)


def compact(group, messages):
    return pl.pallas_call(
        compact_kernel,
        in_specs=[SM, VM],
        out_specs=[VM] * 3,
        out_shape=[
            jax.ShapeDtypeStruct((BLOCK, COLS), BF),
            jax.ShapeDtypeStruct((8, TILE), F32),
            jax.ShapeDtypeStruct((N_DP, TILE), F32),
        ],
        compiler_params=params(12),
        cost_estimate=cost(0, 4 * N_DP * MSG * TILE),
        name="compact",
    )(group, messages)


def to_heads_kernel(fwd_ref, in_ref, out_ref):
    for d in range(N_DP):
        half = slice(HALF * (d % 2), HALF * (d % 2 + 1))
        for k in range(2 * TILES):
            u = TILES * (2 * (d // 2) + ((d % 2) ^ (k // TILES))) + k % TILES
            out_ref[d, k] = in_ref[fwd_ref[u], :, half]


def to_heads(fwd, strips):
    return pl.pallas_call(
        to_heads_kernel,
        in_specs=[SM, VM],
        out_specs=VM,
        out_shape=jax.ShapeDtypeStruct((N_DP, 2 * TILES, STRIP, HALF), BF),
        cost_estimate=cost(0, 4 * ROWS * D),
        compiler_params=params(12),
        name="to_heads",
    )(fwd, strips)


def place_kernel(idx_ref, left_ref, right_ref, out_ref):
    out_ref[0, :, :HALF] = left_ref[0, 0]
    out_ref[0, :, HALF:] = right_ref[0, 0]


def place(index, slots):
    def half(c):
        return pl.BlockSpec(
            (1, 1, TILE, HALF), lambda p, g: (g[p] + c, g[TILES + p], 0, 0)
        )

    spec = pltpu.PrefetchScalarGridSpec(
        num_scalar_prefetch=1,
        grid=(TILES,),
        in_specs=[half(0), half(1)],
        out_specs=pl.BlockSpec((1, TILE, D), lambda p, g: (p, 0, 0)),
    )
    return pl.pallas_call(
        place_kernel,
        grid_spec=spec,
        out_shape=jax.ShapeDtypeStruct((TILES, TILE, D), BF),
        compiler_params=params(12),
        cost_estimate=cost(0, 4 * ROWS * D),
        name="place",
    )(index, slots, slots)


def window_masks(i):
    lane = lax.broadcasted_iota(jnp.int32, (TILE, 256), 1)
    start = 32 * i
    first = (lane >= start) & (lane < start + HDIM)
    second = (lane >= start + HDIM) & (lane < start + 2 * HDIM)
    return first, second


def stack_heads(window, masks):
    zero = jnp.zeros_like(window)
    return jnp.concatenate([jnp.where(m, window, zero) for m in masks], axis=0)


def rows_of_heads(both):
    return jnp.concatenate([both[:, :TILE], both[:, TILE:]], axis=0)


def halves(fn, *arrays):
    return jnp.concatenate(
        [fn(*(a[:, :TILE] for a in arrays)), fn(*(a[:, TILE:] for a in arrays))], axis=1
    )


def wide_max(a):
    return jnp.broadcast_to(jnp.max(a, axis=-1, keepdims=True), a.shape)


def wide_sum(a):
    return jnp.broadcast_to(jnp.sum(a, axis=-1, keepdims=True), a.shape)


CHUNKS = [pl.ds(0, 768), pl.ds(768, 768), pl.ds(1536, 384)]


def start(copies):
    for copy in copies:
        copy.start()


def wait(copies):
    for copy in copies:
        copy.wait()


def load_weight(pieces, weight, sems):
    return [
        [
            pltpu.make_async_copy(
                piece.at[:, cols],
                weight.at[pl.ds(PART * b, PART), cols],
                sems.at[n, b],
            )
            for b, piece in enumerate(pieces)
        ]
        for n, cols in enumerate(CHUNKS)
    ]


def load_rows(refs, rows, sems):
    return [
        pltpu.make_async_copy(ref, rows.at[pl.ds(ROWS * h, ROWS)], sems.at[h])
        for h, ref in enumerate(refs)
    ]


def load_features(refs, normed_t, sems):
    return [
        pltpu.make_async_copy(ref, normed_t.at[:, pl.ds(ROWS * h, ROWS)], sems.at[h])
        for h, ref in enumerate(refs)
    ]


def gradient(normed_t, dqkv, weight, outs, staged, gain_part, sems):
    copies = []
    places = [(0, 0), (1, 0), (2, 0), (4, PART), (4, 0), (5, 0), (5, PART), (3, 0)]
    for c, cols in enumerate(CHUNKS):
        for n in range(0, PIECES, 2):
            rows = slice(PART * n, PART * (n + 2))
            both = dot(normed_t[rows, :], dqkv[:, cols])
            product = both * weight[rows, cols].astype(F32)
            lanes = sum(
                product[:, TILE * k : TILE * (k + 1)] for k in range(cols.size // TILE)
            )
            gain_part[rows, :] = lanes if c == 0 else gain_part[rows, :] + lanes
            both = both.astype(BF)
            for k in (n, n + 1):
                staged[k, :, cols] = both[PART * (k - n) : PART * (k - n + 1)]
                copies.append(
                    pltpu.make_async_copy(
                        staged.at[k, :, cols],
                        outs[places[k][0]].at[pl.ds(places[k][1], PART), cols],
                        sems.at[c, k],
                    )
                )
                copies[-1].start()
    wait(copies)


def main_kernel(
    idx_ref,
    seg_ref,
    normed_ref,
    partner_ref,
    normed_t_ref,
    partner_t_ref,
    cot_ref,
    *refs,
):
    pieces, slots_ref, dqkv_ref = refs[:PIECES], refs[PIECES], refs[PIECES + 1]
    grads, gain_ref = refs[PIECES + 2 : PIECES + 8], refs[PIECES + 8]
    (
        normed,
        qkv,
        cot,
        weight,
        normed_t,
        dqkv,
        out_tiles,
        staged,
        row_sems,
        cot_sems,
        w_sems,
        t_sems,
        slot_sems,
        dqkv_sems,
        grad_sems,
    ) = refs[PIECES + 9 :]
    row_copies = load_rows((normed_ref, partner_ref), normed, row_sems)
    w_copies = load_weight(pieces, weight, w_sems)
    cot_copies = [
        pltpu.make_async_copy(cot_ref.at[j], cot.at[:, j], cot_sems.at[j])
        for j in range(N_DP)
    ]
    t_copies = load_features((normed_t_ref, partner_t_ref), normed_t, t_sems)
    start(row_copies)
    for copies in w_copies:
        start(copies)
    start(cot_copies)
    start(t_copies)
    wait(row_copies)
    for c, cols in enumerate(CHUNKS):
        wait(w_copies[c])
        qkv[:, cols] = dot(normed[...], weight[:, cols]).astype(BF)
    wait(cot_copies)

    def leave(t):
        rows = pl.ds(pl.multiple_of(t * TILE, TILE), TILE)
        return [
            pltpu.make_async_copy(
                out_tiles.at[t],
                slots_ref.at[idx_ref[t], idx_ref[2 * TILES + t]],
                slot_sems.at[t],
            ),
            pltpu.make_async_copy(dqkv.at[rows], dqkv_ref.at[rows], dqkv_sems.at[t]),
        ]

    @pl.loop(0, TILES)
    def _(step):
        pairs = range(8)
        tiles = [2 * step, 2 * step + 1]
        rows = [pl.ds(pl.multiple_of(t * TILE, TILE), TILE) for t in tiles]
        same = []
        for t in tiles:
            seg = jnp.broadcast_to(seg_ref[pl.ds(t, 1), :], (TILE, TILE))
            equal = seg == seg.T
            same.append(jnp.concatenate([equal, equal], axis=1))
        masks = [window_masks(i % 4) for i in pairs]
        windows = [slice(128 * (i % 4), 128 * (i % 4) + 256) for i in pairs]

        def window(a, i):
            first = HALF * a + 128 * (i % 4)
            return qkv[rows[i // 4], first : first + 256]

        q = [window(0, i) for i in pairs]
        d_out = [
            cot[tiles[i // 4], :, :, windows[i]].reshape(TILE, 256) for i in pairs
        ]
        kk = [stack_heads(window(1, i), masks[i]) for i in pairs]
        vv = [stack_heads(window(2, i), masks[i]) for i in pairs]
        scores = [dot(q[i], kk[i], NT) for i in pairs]
        d_probs = [dot(d_out[i], vv[i], NT) for i in pairs]
        scores = [
            jnp.where(same[i // 4], scores[i] * (SCALE * LOG2E), MASKED) for i in pairs
        ]
        tops = [halves(wide_max, x) for x in scores]
        expo = [jnp.exp2(x - m) for x, m in zip(scores, tops)]
        sums = [halves(wide_sum, x) for x in expo]
        weights = [x * (1.0 / total) for x, total in zip(expo, sums)]
        rounded = [x.astype(BF) for x in weights]
        outs = [dot(rounded[i], vv[i]) for i in pairs]
        dvs = [
            dot(rows_of_heads(rounded[i]), stack_heads(d_out[i], masks[i]), TN)
            for i in pairs
        ]
        inner = [halves(wide_sum, d_probs[i] * weights[i]) for i in pairs]
        d_scores = [
            (weights[i] * (d_probs[i] - inner[i]) * SCALE).astype(BF) for i in pairs
        ]
        dqs = [dot(d_scores[i], kk[i]) for i in pairs]
        dks = [
            dot(rows_of_heads(d_scores[i]), stack_heads(q[i], masks[i]), TN)
            for i in pairs
        ]

        def lanes(vals):
            parts = [vals[0][:, :TILE]]
            for i in range(3):
                parts.append(vals[i][:, TILE:] + vals[i + 1][:, :TILE])
            parts.append(vals[3][:, TILE:])
            return jnp.concatenate([p.astype(BF) for p in parts], axis=1)

        for n, t in enumerate(tiles):
            part = slice(4 * n, 4 * n + 4)
            out_tiles[t] = lanes(outs[part])
            for a, vals in enumerate((dqs, dks, dvs)):
                dqkv[rows[n], HALF * a : HALF * (a + 1)] = lanes(vals[part])
            start(leave(t))

    wait(t_copies)
    gradient(normed_t, dqkv, weight, grads, staged, gain_ref, grad_sems)
    for t in range(2 * TILES):
        wait(leave(t))


def main(index, seg, normed, normed_t, cot, pieces):
    return pl.pallas_call(
        main_kernel,
        in_specs=[SM, VM] + [ANY] * (5 + PIECES),
        out_specs=[ANY] * 8 + [VM],
        out_shape=[
            jax.ShapeDtypeStruct((N_DP, 2, TILE, HALF), BF),
            jax.ShapeDtypeStruct((PAIR_ROWS, COLS), BF),
        ]
        + [jax.ShapeDtypeStruct((PART, COLS), BF)] * 4
        + [jax.ShapeDtypeStruct((2 * PART, COLS), BF)] * 2
        + [jax.ShapeDtypeStruct((D, TILE), F32)],
        scratch_shapes=[
            pltpu.VMEM((PAIR_ROWS, D), BF),
            pltpu.VMEM((PAIR_ROWS, COLS), BF),
            pltpu.VMEM((2 * TILES, N_DP, STRIP, HALF), BF),
            pltpu.VMEM((D, COLS), BF),
            pltpu.VMEM((D, PAIR_ROWS), BF),
            pltpu.VMEM((PAIR_ROWS, COLS), BF),
            pltpu.VMEM((2 * TILES, TILE, HALF), BF),
            pltpu.VMEM((PIECES, PART, COLS), BF),
            pltpu.SemaphoreType.DMA((2,)),
            pltpu.SemaphoreType.DMA((N_DP,)),
            pltpu.SemaphoreType.DMA((len(CHUNKS), PIECES)),
            pltpu.SemaphoreType.DMA((2,)),
            pltpu.SemaphoreType.DMA((2 * TILES,)),
            pltpu.SemaphoreType.DMA((2 * TILES,)),
            pltpu.SemaphoreType.DMA((len(CHUNKS), PIECES)),
        ],
        compiler_params=params(58),
        cost_estimate=cost(8 * 10**9, 20 * 2**20, 10**6),
        name="main",
    )(index, seg, *normed, *normed_t, cot, *pieces)


def add_parts(counts, firsts, refs):
    totals, used = [], 0
    for count in counts:
        total = jnp.zeros((PART, COLS), F32)
        for k in range(used, used + count):
            total = total + refs[k][firsts[k] : firsts[k] + PART, :].astype(F32)
        used += count
        totals.append(total)
    return totals


def add_kernel(counts, firsts, *refs):
    totals = add_parts(counts, firsts, refs)
    for out_ref, total in zip(refs[sum(counts) :], totals):
        out_ref[...] = total.astype(BF)


def column_kernel(counts, firsts, gain_ref, other_ref, *refs):
    gain = gain_ref[...] + other_ref[...]
    outs = refs[sum(counts) :]
    totals = add_parts(counts, firsts, refs)
    for n, out_ref in enumerate(outs):
        block = totals[n // 2][BLOCK * (n % 2) : BLOCK * (n % 2 + 1)]
        out_ref[0:BLOCK, :] = block.astype(BF)
        put_gain(gain, out_ref, BLOCK, RIDE)


def put_gain(gain, ref, first, last):
    hi = gain.astype(BF).astype(F32)
    lo = gain - hi
    ref[first:last, :] = jnp.zeros((last - first, COLS), BF)
    for k in range(D // TILE):
        cols = slice(TILE * k, TILE * (k + 1))
        ref[first : first + 1, cols] = hi[k : k + 1].astype(BF)
        ref[first + 1 : first + 2, cols] = lo[k : k + 1].astype(BF)


def add(groups, gains=()):
    parts = [part for group in groups for part in group]
    rows, n = (RIDE, 2 * len(groups)) if gains else (PART, len(groups))
    return pl.pallas_call(
        functools.partial(
            column_kernel if gains else add_kernel,
            [len(group) for group in groups],
            [first for _, first in parts],
        ),
        in_specs=[VM] * (len(gains) + len(parts)),
        out_specs=[VM] * n,
        out_shape=[jax.ShapeDtypeStruct((rows, COLS), BF)] * n,
        compiler_params=params(12),
        cost_estimate=cost(0, (4 if gains else 75000) * len(parts) * PART * COLS),
        name="add",
    )(*gains, *[array for array, _ in parts])


def gain_kernel(part_ref, nat_ref, gain_ref, out_ref, perm_ref):
    build_order(nat_ref, perm_ref)
    rest = jnp.sum(part_ref[...], axis=1, keepdims=True)
    rest = jnp.broadcast_to(rest, (D, TILE))
    total = jnp.zeros((1, D), F32)
    for _ in range(3):
        term = rest.astype(BF)
        rest = rest - term.astype(F32)
        total = total + dot(term, perm_ref[...], TN)[0:1]
    total = total / gain_ref[...]
    out_ref[...] = jnp.zeros_like(out_ref)
    for k in range(D // TILE):
        out_ref[k : k + 1, :] = total[:, TILE * k : TILE * (k + 1)]


def gain_back(part, nat, gain):
    return pl.pallas_call(
        gain_kernel,
        in_specs=[VM] * 3,
        out_specs=VM,
        out_shape=jax.ShapeDtypeStruct((STRIP, TILE), F32),
        scratch_shapes=[pltpu.VMEM((D, D), BF)],
        compiler_params=params(24),
        cost_estimate=cost(0, 4 * D * TILE),
        name="gain",
    )(part, nat, gain)


def back_kernel(half, nat_ref, dqkv_ref, *refs):
    pieces, (out_ref, weight, perm_ref, dqkv, w_sems, q_sem) = (
        refs[:PIECES],
        refs[PIECES:],
    )
    w_copies = load_weight(pieces, weight, w_sems)
    q_copy = pltpu.make_async_copy(dqkv_ref.at[pl.ds(ROWS * half, ROWS)], dqkv, q_sem)
    q_copy.start()
    for copies in w_copies:
        start(copies)
    build_order(nat_ref, perm_ref)
    q_copy.wait()
    for copies in w_copies:
        wait(copies)
    d_normed = dot(dqkv[...], weight[...], NT).astype(BF)
    out_ref[...] = dot(d_normed, perm_ref[...]).astype(BF)


def back(half, dqkv, pieces, nat):
    return pl.pallas_call(
        functools.partial(back_kernel, half),
        in_specs=[VM] + [ANY] * (1 + PIECES),
        out_specs=VM,
        out_shape=jax.ShapeDtypeStruct((ROWS, D), BF),
        scratch_shapes=[
            pltpu.VMEM((D, COLS), BF),
            pltpu.VMEM((D, D), BF),
            pltpu.VMEM((ROWS, COLS), BF),
            pltpu.SemaphoreType.DMA((len(CHUNKS), PIECES)),
            pltpu.SemaphoreType.DMA,
        ],
        compiler_params=params(58),
        cost_estimate=cost(2 * ROWS * D * (D + COLS), 15 * 2**20),
        name="back",
    )(nat, dqkv, *pieces)


def rows_kernel(patches_ref, gain_ref, mine_ref, other_ref, out_ref):
    standard, inv_std = norm_rows(patches_ref[...])
    d_normed = mine_ref[...].astype(F32) + other_ref[...].astype(F32)
    scaled = d_normed * gain_ref[...]
    back_rows = inv_std * (
        scaled
        - jnp.mean(scaled, axis=-1, keepdims=True)
        - standard * jnp.mean(scaled * standard, axis=-1, keepdims=True)
    )
    out_ref[...] = back_rows.astype(BF)


def rows_back(patches, gain, mine, other):
    block = pl.BlockSpec((TILE, D), lambda i: (i, 0))
    return pl.pallas_call(
        rows_kernel,
        grid=(TILES,),
        in_specs=[block, pl.BlockSpec((1, D), lambda i: (0, 0)), block, block],
        out_specs=block,
        out_shape=jax.ShapeDtypeStruct((ROWS, D), BF),
        compiler_params=params(58),
        cost_estimate=cost(20 * ROWS * D, 8 * ROWS * D),
        name="rows_back",
    )(patches, gain, mine, other)


def split_kernel(rows_ref, one_ref, two_ref, three_ref, out_ref):
    total = rows_ref[...].astype(F32)
    for ref in (one_ref, two_ref, three_ref):
        total = total + ref[...].astype(F32)
    gain = total[BLOCK : BLOCK + 1, :D] + total[BLOCK + 1 : BLOCK + 2, :D]
    gain = gain.astype(BF)
    total = total.astype(BF)
    extras = OWN * LANES
    for s in range(N_DP):
        for k in range(LANES):
            out_ref[s, OWN * k : OWN * (k + 1), :] = total[
                OWN * s : OWN * (s + 1), TILE * k : TILE * (k + 1)
            ]
        for k in range(D // TILE):
            out_ref[s, extras + k : extras + k + 1, :] = gain[
                :, TILE * k : TILE * (k + 1)
            ]


def split(rows, others):
    return pl.pallas_call(
        split_kernel,
        in_specs=[VM] * 4,
        out_specs=VM,
        out_shape=jax.ShapeDtypeStruct((N_DP, MSG, TILE), BF),
        compiler_params=params(12),
        cost_estimate=cost(0, 4 * N_DP * MSG * TILE),
        name="split",
    )(rows, *others)


def finish_kernel(msg_ref, out_ref, gain_ref):
    both = jnp.zeros((MSG, TILE), F32)
    for half in range(2):
        total = msg_ref[half].astype(F32)
        for chip in range(1, 4):
            total = total + msg_ref[2 * chip + half].astype(F32)
        both = both + total
        for k in range(LANES):
            first = D * (k // 5) + HALF * half + TILE * (k % 5)
            out_ref[:, first : first + TILE] = total[OWN * k : OWN * (k + 1)]
    gain_ref[...] = both[OWN * LANES : MSG]


def finish(messages):
    return pl.pallas_call(
        finish_kernel,
        in_specs=[VM],
        out_specs=[VM, VM],
        out_shape=[
            jax.ShapeDtypeStruct((OWN, 3 * D), F32),
            jax.ShapeDtypeStruct((D // TILE, TILE), F32),
        ],
        compiler_params=params(12),
        cost_estimate=cost(0, 6 * N_DP * MSG * TILE),
        name="finish",
    )(messages)


def ring_pairs(df, ds):
    pairs = []
    for d in range(N_DP):
        dx, dz = (ds, df) if d % 2 else (df, ds)
        for x in range(4):
            for z in range(4):
                src = 4 * ((x + dx) % 4) + (z + dz) % 4
                pairs.append((N_INNER * d + src, N_INNER * d + 4 * x + z))
    return pairs


def double_pairs(f_bits, s_bits):
    pairs = []
    for d in range(N_DP):
        x_bits, z_bits = (s_bits, f_bits) if d % 2 else (f_bits, s_bits)
        flip = 4 * x_bits + z_bits
        pairs += [(N_INNER * d + (m ^ flip), N_INNER * d + m) for m in range(N_INNER)]
    return pairs


def from_ring(value, df, ds):
    return lax.ppermute(value, ("dp", "inner"), ring_pairs(df, ds))


def swap_cores(value):
    return lax.ppermute(value, "dp", [(d ^ 1, d) for d in range(N_DP)])


def exchange(value, axis="dp"):
    return lax.all_to_all(value, axis, split_axis=0, concat_axis=0, tiled=True)


def on_device(patches, segments, owners, norm_gain, qkv_weight, cotangent):
    group = lax.axis_index("dp")
    inner = lax.axis_index("inner")
    core, x, z = group % 2, inner // 4, inner % 4
    gain = norm_gain.reshape(1, D)

    pos = jnp.arange(N_INNER)
    df, ds = pos % 4, pos // 4
    m = 4 * ((x + jnp.where(core == 0, df, ds)) % 4) + (
        z + jnp.where(core == 0, ds, df)
    ) % 4
    nat = (
        (jnp.arange(N_DP)[None, :, None] * N_INNER + m[:, None, None]) * OWN
        + jnp.arange(OWN)[None, None, :]
    ).reshape(1, D).astype(F32)

    messages = exchange(build(owners, qkv_weight, segments))
    partner_patches = swap_cores(patches)
    own_prep = prep(patches, gain, nat)
    strips = cotangent.reshape(TILES, N_DP, STRIP, D).transpose(1, 0, 2, 3)
    messages, strips = lax.optimization_barrier((messages, strips))
    block, seg, owners_all = compact(group.reshape(1).astype(jnp.int32), messages)
    strips, own_prep = lax.optimization_barrier((exchange(strips), own_prep))

    owner_of = owners_all[:, :TILES].astype(jnp.int32).reshape(N_DP * TILES)
    u = jnp.arange(N_DP * TILES)
    earlier = (owner_of[:, None] == owner_of[None, :]) & (
        u[None, :] // TILES < u[:, None] // TILES
    )
    fwd = (TILES * owner_of + jnp.sum(earlier, axis=1)).astype(jnp.int32)
    wanted = fwd[None, :] == TILES * group + jnp.arange(TILES)[:, None]
    source = jnp.sum(jnp.where(wanted, u[None, :] // TILES, 0), axis=1)
    place_index = jnp.concatenate([2 * (source // 2), source % 2]).astype(jnp.int32)
    mine = jnp.arange(2)[:, None] ^ core
    tile = (TILES * (group - core + mine) + jnp.arange(TILES)[None, :]).reshape(-1)
    owner_here = jnp.sum(jnp.where(tile[:, None] == u[None, :], owner_of, 0), axis=1)
    slot_index = jnp.concatenate(
        [owner_here, jnp.broadcast_to(mine, (2, TILES)).reshape(-1)]
    ).astype(jnp.int32)

    heads = to_heads(fwd, strips.reshape(N_DP * TILES, STRIP, D))
    cot = exchange(heads)

    ring = [block] + [from_ring(block, f, 0) for f in (1, 2, 3)]
    near_a, near_b = jnp.concatenate(ring[:2]), jnp.concatenate(ring[2:])
    above_a, below_b = from_ring(near_a, 0, 1), from_ring(near_b, 0, -1)
    above_b, below_a = from_ring(near_b, 0, 1), from_ring(near_a, 0, -1)
    above_a, above_b, below_a, below_b = lax.optimization_barrier(
        (above_a, above_b, below_a, below_b)
    )
    far_a, far_b = from_ring(above_a, 0, 1), from_ring(below_b, 0, -1)
    pieces = [near_a, near_b, above_a, above_b, far_a, far_b, below_a, below_b]
    normed, normed_t = zip(own_prep, prep(partner_patches, gain, nat))

    out, dqkv, col_a, col_b, up_a, down_b, up, down, gain_part = main(
        slot_index, seg, normed, normed_t, cot, pieces
    )

    up, down = from_ring(up, 0, -1), from_ring(down, 0, 1)
    slots = exchange(out)
    gain_part = gain_back(gain_part, nat, gain)
    gain_other = lax.ppermute(gain_part, ("dp", "inner"), double_pairs(0, 1))
    partners = back(1, dqkv, pieces, nat)
    up, down, gain_part, gain_other, partners = lax.optimization_barrier(
        (up, down, gain_part, gain_other, partners)
    )
    other = swap_cores(partners)
    up_a, down_b = add([[(up_a, 0), (up, 0)], [(down_b, 0), (down, 0)]])
    from_up_a, from_down_b = from_ring(up_a, 0, -1), from_ring(down_b, 0, 1)
    gain_part = gain_part + gain_other
    gain_other = lax.ppermute(gain_part, ("dp", "inner"), double_pairs(0, 3))
    zero, one, two, three = add(
        [
            [(col_a, 0), (from_up_a, 0), (down, PART)],
            [(col_b, 0), (up, PART), (from_down_b, 0)],
        ],
        (gain_part, gain_other),
    )
    dqkv, _ = lax.optimization_barrier((dqkv, zero))
    mine = back(0, dqkv, pieces, nat)
    others = [from_ring(two, -2, 0), from_ring(three, 1, 0), from_ring(one, -1, 0)]
    others[0], slots, mine = lax.optimization_barrier((others[0], slots, mine))

    attended = place(place_index, slots).reshape(ROWS, D)
    grad_rows = rows_back(patches, gain, mine, other)
    grad_qkv, grad_gain = finish(exchange(split(zero, others)))
    return (attended, grad_rows, grad_qkv, grad_gain.reshape(D))


def solution(mesh):
    both = ("dp", "inner")
    placed = (
        P(both, None),
        P(both, None),
        P(both),
        P(),
        P(both, None),
        P(both, None),
    )
    return jax.shard_map(
        on_device,
        mesh=mesh,
        in_specs=placed,
        out_specs=(P(both, None), P(both, None), P(both, None), P()),
        check_vma=False,
    )
```

```python
import functools

import jax
import jax.numpy as jnp
from jax import lax
from jax.experimental import pallas as pl
from jax.experimental.pallas import tpu as pltpu
from jax.sharding import PartitionSpec as P

D = 1280
HEADS = 16
HDIM = 80
TILE = 128
TILES = 3
N_DP = 8
N_INNER = 16
ROWS = TILES * TILE
PAIR_ROWS = 2 * ROWS
HALF = D // 2
COLS = 3 * HALF
OWN = 10
BLOCK = 80
PART = 160
PIECES = 8
RIDE = 88
STRIP = 16
MSG = 160
LANES = COLS // TILE
EPS = 1e-6
MASKED = -1e30
SCALE = HDIM ** (-0.5)
LOG2E = 1.4426950408889634
BF = jnp.bfloat16
F32 = jnp.float32
VM = pl.BlockSpec(memory_space=pltpu.VMEM)
SM = pl.BlockSpec(memory_space=pltpu.SMEM)
ANY = pl.BlockSpec(memory_space=pltpu.HBM)
NT = (((1,), (1,)), ((), ()))
TN = (((0,), (0,)), ((), ()))
NN = (((1,), (0,)), ((), ()))


def params(mib, **more):
    return pltpu.CompilerParams(vmem_limit_bytes=mib * 2**20, **more)


def cost(flops, nbytes, trans=0):
    return pl.CostEstimate(
        flops=flops // 1000, bytes_accessed=nbytes // 1000, transcendentals=trans // 1000
    )


def dot(a, b, dims=NN):
    return lax.dot_general(a, b, dims, preferred_element_type=F32)


def norm_rows(rows):
    wide = rows.astype(F32)
    centred = wide - jnp.mean(wide, axis=-1, keepdims=True)
    variance = jnp.mean(centred * centred, axis=-1, keepdims=True)
    inv_std = lax.rsqrt(variance + EPS)
    return centred * inv_std, inv_std


def build_order(nat_ref, perm_ref):
    for r in range(D // TILE):
        rows = slice(TILE * r, TILE * (r + 1))
        column = jnp.broadcast_to(nat_ref[:, rows], (TILE, TILE)).T
        for a in range(D // TILE):
            feature = lax.broadcasted_iota(jnp.int32, (TILE, TILE), 1) + TILE * a
            hit = column == feature.astype(F32)
            perm_ref[rows, TILE * a : TILE * (a + 1)] = jnp.where(hit, 1.0, 0.0).astype(BF)


def prep_kernel(patches_ref, gain_ref, nat_ref, normed_ref, normed_t_ref, perm_ref):
    build_order(nat_ref, perm_ref)
    standard, _ = norm_rows(patches_ref[...])
    normed = (standard * gain_ref[...]).astype(BF)
    normed_ref[...] = dot(normed, perm_ref[...], NT).astype(BF)
    normed_t_ref[...] = dot(perm_ref[...], normed, NT).astype(BF)


def prep(patches, gain, nat):
    return pl.pallas_call(
        prep_kernel,
        in_specs=[VM] * 3,
        out_specs=[VM] * 2,
        out_shape=[
            jax.ShapeDtypeStruct((ROWS, D), BF),
            jax.ShapeDtypeStruct((D, ROWS), BF),
        ],
        scratch_shapes=[pltpu.VMEM((D, D), BF)],
        compiler_params=params(58),
        cost_estimate=cost(4 * ROWS * D * D, 6 * ROWS * D),
        name="prep",
    )(patches, gain, nat)


def build_kernel(own_ref, w_ref, seg_ref, out_ref):
    lane = lax.broadcasted_iota(jnp.int32, (1, TILE), 1)
    owners = jnp.zeros((1, TILE), jnp.int32)
    for t in range(TILES):
        owners = jnp.where(lane == t, own_ref[t], owners)
    for half in range(2):
        for k in range(LANES):
            first = D * (k // 5) + HALF * half + TILE * (k % 5)
            out_ref[half, OWN * k : OWN * (k + 1), :] = w_ref[:, first : first + TILE]
        extras = OWN * LANES
        out_ref[half, extras:MSG, :] = jnp.zeros((MSG - extras, TILE), BF)
        out_ref[half, extras : extras + 1, :] = owners.astype(F32).astype(BF)
        out_ref[half, extras + 1 : extras + 1 + TILES, :] = (
            seg_ref[...].astype(F32).astype(BF)
        )
    for d in range(2, N_DP):
        out_ref[d] = out_ref[d % 2]


def build(owners, weight, segments):
    return pl.pallas_call(
        build_kernel,
        in_specs=[SM, VM, VM],
        out_specs=VM,
        out_shape=jax.ShapeDtypeStruct((N_DP, MSG, TILE), BF),
        compiler_params=params(58),
        cost_estimate=cost(0, 2 * N_DP * MSG * TILE),
        name="build",
    )(owners, weight, segments)


def compact_kernel(group_ref, msg_ref, w_ref, seg_ref, own_ref):
    group = group_ref[0]
    extras = OWN * LANES
    seg_ref[...] = jnp.zeros_like(seg_ref)
    for s in range(N_DP):
        for k in range(LANES):
            w_ref[OWN * s : OWN * (s + 1), TILE * k : TILE * (k + 1)] = msg_ref[
                s, OWN * k : OWN * (k + 1), :
            ]
        own_ref[s : s + 1, :] = msg_ref[s, extras : extras + 1, :].astype(F32)
    for rel in range(2):
        src = group + rel * (1 - 2 * (group % 2))
        seg_ref[TILES * rel : TILES * (rel + 1), :] = msg_ref[
            src, extras + 1 : extras + 1 + TILES, :
        ].astype(F32)


def compact(group, messages):
    return pl.pallas_call(
        compact_kernel,
        in_specs=[SM, VM],
        out_specs=[VM] * 3,
        out_shape=[
            jax.ShapeDtypeStruct((BLOCK, COLS), BF),
            jax.ShapeDtypeStruct((8, TILE), F32),
            jax.ShapeDtypeStruct((N_DP, TILE), F32),
        ],
        compiler_params=params(12),
        cost_estimate=cost(0, 4 * N_DP * MSG * TILE),
        name="compact",
    )(group, messages)


def to_heads_kernel(fwd_ref, in_ref, out_ref):
    for d in range(N_DP):
        half = slice(HALF * (d % 2), HALF * (d % 2 + 1))
        for k in range(2 * TILES):
            u = TILES * (2 * (d // 2) + ((d % 2) ^ (k // TILES))) + k % TILES
            out_ref[d, k] = in_ref[fwd_ref[u], :, half]


def to_heads(fwd, strips):
    return pl.pallas_call(
        to_heads_kernel,
        in_specs=[SM, VM],
        out_specs=VM,
        out_shape=jax.ShapeDtypeStruct((N_DP, 2 * TILES, STRIP, HALF), BF),
        cost_estimate=cost(0, 4 * ROWS * D),
        compiler_params=params(12),
        name="to_heads",
    )(fwd, strips)


def place_kernel(idx_ref, left_ref, right_ref, out_ref):
    out_ref[0, :, :HALF] = left_ref[0, 0]
    out_ref[0, :, HALF:] = right_ref[0, 0]


def place(index, slots):
    def half(c):
        return pl.BlockSpec(
            (1, 1, TILE, HALF), lambda p, g: (g[p] + c, g[TILES + p], 0, 0)
        )

    spec = pltpu.PrefetchScalarGridSpec(
        num_scalar_prefetch=1,
        grid=(TILES,),
        in_specs=[half(0), half(1)],
        out_specs=pl.BlockSpec((1, TILE, D), lambda p, g: (p, 0, 0)),
    )
    return pl.pallas_call(
        place_kernel,
        grid_spec=spec,
        out_shape=jax.ShapeDtypeStruct((TILES, TILE, D), BF),
        compiler_params=params(12),
        cost_estimate=cost(0, 4 * ROWS * D),
        name="place",
    )(index, slots, slots)


def window_masks(i):
    lane = lax.broadcasted_iota(jnp.int32, (TILE, 256), 1)
    start = 32 * i
    first = (lane >= start) & (lane < start + HDIM)
    second = (lane >= start + HDIM) & (lane < start + 2 * HDIM)
    return first, second


def stack_heads(window, masks):
    zero = jnp.zeros_like(window)
    return jnp.concatenate([jnp.where(m, window, zero) for m in masks], axis=0)


def rows_of_heads(both):
    return jnp.concatenate([both[:, :TILE], both[:, TILE:]], axis=0)


def halves(fn, *arrays):
    return jnp.concatenate(
        [fn(*(a[:, :TILE] for a in arrays)), fn(*(a[:, TILE:] for a in arrays))], axis=1
    )


def wide_max(a):
    return jnp.broadcast_to(jnp.max(a, axis=-1, keepdims=True), a.shape)


CHUNKS = [pl.ds(0, 384), pl.ds(384, 768), pl.ds(1152, 768)]


def start(copies):
    for copy in copies:
        copy.start()


def wait(copies):
    for copy in copies:
        copy.wait()


def load_weight(pieces, weight, sems):
    return [
        [
            pltpu.make_async_copy(
                piece.at[:, cols],
                weight.at[pl.ds(PART * b, PART), cols],
                sems.at[n, b],
            )
            for b, piece in enumerate(pieces)
        ]
        for n, cols in enumerate(CHUNKS)
    ]


def load_rows(refs, rows, sems):
    return [
        pltpu.make_async_copy(ref, rows.at[pl.ds(ROWS * h, ROWS)], sems.at[h])
        for h, ref in enumerate(refs)
    ]


def load_features(refs, normed_t, sems):
    return [
        pltpu.make_async_copy(ref, normed_t.at[:, pl.ds(ROWS * h, ROWS)], sems.at[h])
        for h, ref in enumerate(refs)
    ]


def gradient(normed_t, dqkv, weight, outs, staged, gain_part, sems):
    copies = []
    places = [(0, 0), (1, 0), (2, 0), (4, PART), (4, 0), (5, 0), (5, PART), (3, 0)]
    for c, cols in enumerate(CHUNKS):
        for n in range(0, PIECES, 2):
            rows = slice(PART * n, PART * (n + 2))
            both = dot(normed_t[rows, :], dqkv[:, cols])
            product = both * weight[rows, cols].astype(F32)
            lanes = sum(
                product[:, TILE * k : TILE * (k + 1)] for k in range(cols.size // TILE)
            )
            gain_part[rows, :] = lanes if c == 0 else gain_part[rows, :] + lanes
            both = both.astype(BF)
            for k in (n, n + 1):
                staged[k, :, cols] = both[PART * (k - n) : PART * (k - n + 1)]
                copies.append(
                    pltpu.make_async_copy(
                        staged.at[k, :, cols],
                        outs[places[k][0]].at[pl.ds(places[k][1], PART), cols],
                        sems.at[c, k],
                    )
                )
                copies[-1].start()
    wait(copies)


def main_kernel(
    idx_ref,
    seg_ref,
    normed_ref,
    partner_ref,
    normed_t_ref,
    partner_t_ref,
    cot_ref,
    *refs,
):
    pieces, slots_ref, dqkv_ref = refs[:PIECES], refs[PIECES], refs[PIECES + 1]
    grads, gain_ref = refs[PIECES + 2 : PIECES + 8], refs[PIECES + 8]
    (
        normed,
        qkv,
        cot,
        weight,
        normed_t,
        dqkv,
        out_tiles,
        staged,
        row_sems,
        cot_sems,
        w_sems,
        t_sems,
        slot_sems,
        dqkv_sems,
        grad_sems,
    ) = refs[PIECES + 9 :]
    row_copies = load_rows((normed_ref, partner_ref), normed, row_sems)
    w_copies = load_weight(pieces, weight, w_sems)
    cot_copies = [
        pltpu.make_async_copy(cot_ref.at[j], cot.at[:, j], cot_sems.at[j])
        for j in range(N_DP)
    ]
    t_copies = load_features((normed_t_ref, partner_t_ref), normed_t, t_sems)
    start(row_copies)
    for copies in w_copies:
        start(copies)
    start(cot_copies)
    start(t_copies)
    wait(row_copies)
    for c, cols in enumerate(CHUNKS):
        wait(w_copies[c])
        qkv[:, cols] = dot(normed[...], weight[:, cols]).astype(BF)
    wait(cot_copies)

    def leave(t):
        rows = pl.ds(pl.multiple_of(t * TILE, TILE), TILE)
        return [
            pltpu.make_async_copy(
                out_tiles.at[t],
                slots_ref.at[idx_ref[t], idx_ref[2 * TILES + t]],
                slot_sems.at[t],
            ),
            pltpu.make_async_copy(dqkv.at[rows], dqkv_ref.at[rows], dqkv_sems.at[t]),
        ]

    @pl.loop(0, TILES)
    def _(step):
        pairs = range(8)
        tiles = [2 * step, 2 * step + 1]
        rows = [pl.ds(pl.multiple_of(t * TILE, TILE), TILE) for t in tiles]
        same = []
        for t in tiles:
            seg = jnp.broadcast_to(seg_ref[pl.ds(t, 1), :], (TILE, TILE))
            equal = seg == seg.T
            same.append(jnp.concatenate([equal, equal], axis=1))
        masks = [window_masks(i % 4) for i in pairs]
        row_head = lax.broadcasted_iota(jnp.int32, (256, 256), 0) // TILE
        lane_head = lax.broadcasted_iota(jnp.int32, (256, 256), 1) // TILE
        ones = jnp.where(row_head == lane_head, 1.0, 0.0).astype(BF)
        windows = [slice(128 * (i % 4), 128 * (i % 4) + 256) for i in pairs]

        def window(a, i):
            first = HALF * a + 128 * (i % 4)
            return qkv[rows[i // 4], first : first + 256]

        q = [window(0, i) for i in pairs]
        d_out = [
            cot[tiles[i // 4], :, :, windows[i]].reshape(TILE, 256) for i in pairs
        ]
        kk = [stack_heads(window(1, i), masks[i]) for i in pairs]
        vv = [stack_heads(window(2, i), masks[i]) for i in pairs]
        scores = [dot(q[i], kk[i], NT) for i in pairs]
        d_probs = [dot(d_out[i], vv[i], NT) for i in pairs]
        scores = [
            jnp.where(same[i // 4], scores[i] * (SCALE * LOG2E), MASKED) for i in pairs
        ]
        tops = [halves(wide_max, x) for x in scores]
        expo = [jnp.exp2(x - m) for x, m in zip(scores, tops)]
        sums = [dot(x.astype(BF), ones) for x in expo]
        weights = [x * (1.0 / total) for x, total in zip(expo, sums)]
        rounded = [x.astype(BF) for x in weights]
        outs = [dot(rounded[i], vv[i]) for i in pairs]
        dvs = [
            dot(rows_of_heads(rounded[i]), stack_heads(d_out[i], masks[i]), TN)
            for i in pairs
        ]
        inner = [dot((d_probs[i] * weights[i]).astype(BF), ones) for i in pairs]
        d_scores = [
            (weights[i] * (d_probs[i] - inner[i]) * SCALE).astype(BF) for i in pairs
        ]
        dqs = [dot(d_scores[i], kk[i]) for i in pairs]
        dks = [
            dot(rows_of_heads(d_scores[i]), stack_heads(q[i], masks[i]), TN)
            for i in pairs
        ]

        def lanes(vals):
            parts = [vals[0][:, :TILE]]
            for i in range(3):
                parts.append(vals[i][:, TILE:] + vals[i + 1][:, :TILE])
            parts.append(vals[3][:, TILE:])
            return jnp.concatenate([p.astype(BF) for p in parts], axis=1)

        for n, t in enumerate(tiles):
            part = slice(4 * n, 4 * n + 4)
            out_tiles[t] = lanes(outs[part])
            for a, vals in enumerate((dqs, dks, dvs)):
                dqkv[rows[n], HALF * a : HALF * (a + 1)] = lanes(vals[part])
            start(leave(t))

    wait(t_copies)
    gradient(normed_t, dqkv, weight, grads, staged, gain_ref, grad_sems)
    for t in range(2 * TILES):
        wait(leave(t))


def main(index, seg, normed, normed_t, cot, pieces):
    return pl.pallas_call(
        main_kernel,
        in_specs=[SM, VM] + [ANY] * (5 + PIECES),
        out_specs=[ANY] * 8 + [VM],
        out_shape=[
            jax.ShapeDtypeStruct((N_DP, 2, TILE, HALF), BF),
            jax.ShapeDtypeStruct((PAIR_ROWS, COLS), BF),
        ]
        + [jax.ShapeDtypeStruct((PART, COLS), BF)] * 4
        + [jax.ShapeDtypeStruct((2 * PART, COLS), BF)] * 2
        + [jax.ShapeDtypeStruct((D, TILE), F32)],
        scratch_shapes=[
            pltpu.VMEM((PAIR_ROWS, D), BF),
            pltpu.VMEM((PAIR_ROWS, COLS), BF),
            pltpu.VMEM((2 * TILES, N_DP, STRIP, HALF), BF),
            pltpu.VMEM((D, COLS), BF),
            pltpu.VMEM((D, PAIR_ROWS), BF),
            pltpu.VMEM((PAIR_ROWS, COLS), BF),
            pltpu.VMEM((2 * TILES, TILE, HALF), BF),
            pltpu.VMEM((PIECES, PART, COLS), BF),
            pltpu.SemaphoreType.DMA((2,)),
            pltpu.SemaphoreType.DMA((N_DP,)),
            pltpu.SemaphoreType.DMA((len(CHUNKS), PIECES)),
            pltpu.SemaphoreType.DMA((2,)),
            pltpu.SemaphoreType.DMA((2 * TILES,)),
            pltpu.SemaphoreType.DMA((2 * TILES,)),
            pltpu.SemaphoreType.DMA((len(CHUNKS), PIECES)),
        ],
        compiler_params=params(58),
        cost_estimate=cost(8 * 10**9, 20 * 2**20, 10**6),
        name="main",
    )(index, seg, *normed, *normed_t, cot, *pieces)


def add_parts(counts, firsts, refs):
    totals, used = [], 0
    for count in counts:
        total = jnp.zeros((PART, COLS), F32)
        for k in range(used, used + count):
            total = total + refs[k][firsts[k] : firsts[k] + PART, :].astype(F32)
        used += count
        totals.append(total)
    return totals


def add_kernel(counts, firsts, *refs):
    totals = add_parts(counts, firsts, refs)
    for out_ref, total in zip(refs[sum(counts) :], totals):
        out_ref[...] = total.astype(BF)


def column_kernel(counts, firsts, gain_ref, other_ref, *refs):
    gain = gain_ref[...] + other_ref[...]
    outs = refs[sum(counts) :]
    totals = add_parts(counts, firsts, refs)
    for n, out_ref in enumerate(outs):
        block = totals[n // 2][BLOCK * (n % 2) : BLOCK * (n % 2 + 1)]
        out_ref[0:BLOCK, :] = block.astype(BF)
        put_gain(gain, out_ref, BLOCK, RIDE)


def put_gain(gain, ref, first, last):
    hi = gain.astype(BF).astype(F32)
    lo = gain - hi
    ref[first:last, :] = jnp.zeros((last - first, COLS), BF)
    for k in range(D // TILE):
        cols = slice(TILE * k, TILE * (k + 1))
        ref[first : first + 1, cols] = hi[k : k + 1].astype(BF)
        ref[first + 1 : first + 2, cols] = lo[k : k + 1].astype(BF)


def add(groups, gains=()):
    parts = [part for group in groups for part in group]
    rows, n = (RIDE, 2 * len(groups)) if gains else (PART, len(groups))
    return pl.pallas_call(
        functools.partial(
            column_kernel if gains else add_kernel,
            [len(group) for group in groups],
            [first for _, first in parts],
        ),
        in_specs=[VM] * (len(gains) + len(parts)),
        out_specs=[VM] * n,
        out_shape=[jax.ShapeDtypeStruct((rows, COLS), BF)] * n,
        compiler_params=params(12),
        cost_estimate=cost(0, 4 * len(parts) * PART * COLS),
        name="add",
    )(*gains, *[array for array, _ in parts])


def gain_kernel(part_ref, nat_ref, gain_ref, out_ref, perm_ref):
    build_order(nat_ref, perm_ref)
    rest = jnp.sum(part_ref[...], axis=1, keepdims=True)
    rest = jnp.broadcast_to(rest, (D, TILE))
    total = jnp.zeros((1, D), F32)
    for _ in range(3):
        term = rest.astype(BF)
        rest = rest - term.astype(F32)
        total = total + dot(term, perm_ref[...], TN)[0:1]
    total = total / gain_ref[...]
    out_ref[...] = jnp.zeros_like(out_ref)
    for k in range(D // TILE):
        out_ref[k : k + 1, :] = total[:, TILE * k : TILE * (k + 1)]


def gain_back(part, nat, gain):
    return pl.pallas_call(
        gain_kernel,
        in_specs=[VM] * 3,
        out_specs=VM,
        out_shape=jax.ShapeDtypeStruct((STRIP, TILE), F32),
        scratch_shapes=[pltpu.VMEM((D, D), BF)],
        compiler_params=params(24),
        cost_estimate=cost(0, 4 * D * TILE),
        name="gain",
    )(part, nat, gain)


def back_kernel(half, nat_ref, dqkv_ref, *refs):
    pieces, (out_ref, weight, perm_ref, dqkv, w_sems, q_sem) = (
        refs[:PIECES],
        refs[PIECES:],
    )
    w_copies = load_weight(pieces, weight, w_sems)
    q_copy = pltpu.make_async_copy(dqkv_ref.at[pl.ds(ROWS * half, ROWS)], dqkv, q_sem)
    q_copy.start()
    for copies in w_copies:
        start(copies)
    build_order(nat_ref, perm_ref)
    q_copy.wait()
    for copies in w_copies:
        wait(copies)
    d_normed = dot(dqkv[...], weight[...], NT).astype(BF)
    out_ref[...] = dot(d_normed, perm_ref[...]).astype(BF)


def back(half, dqkv, pieces, nat):
    return pl.pallas_call(
        functools.partial(back_kernel, half),
        in_specs=[VM] + [ANY] * (1 + PIECES),
        out_specs=VM,
        out_shape=jax.ShapeDtypeStruct((ROWS, D), BF),
        scratch_shapes=[
            pltpu.VMEM((D, COLS), BF),
            pltpu.VMEM((D, D), BF),
            pltpu.VMEM((ROWS, COLS), BF),
            pltpu.SemaphoreType.DMA((len(CHUNKS), PIECES)),
            pltpu.SemaphoreType.DMA,
        ],
        compiler_params=params(58),
        cost_estimate=cost(2 * ROWS * D * (D + COLS), 15 * 2**20),
        name="back",
    )(nat, dqkv, *pieces)


def rows_kernel(patches_ref, gain_ref, mine_ref, other_ref, out_ref):
    standard, inv_std = norm_rows(patches_ref[...])
    d_normed = mine_ref[...].astype(F32) + other_ref[...].astype(F32)
    scaled = d_normed * gain_ref[...]
    back_rows = inv_std * (
        scaled
        - jnp.mean(scaled, axis=-1, keepdims=True)
        - standard * jnp.mean(scaled * standard, axis=-1, keepdims=True)
    )
    out_ref[...] = back_rows.astype(BF)


def rows_back(patches, gain, mine, other):
    block = pl.BlockSpec((TILE, D), lambda i: (i, 0))
    return pl.pallas_call(
        rows_kernel,
        grid=(TILES,),
        in_specs=[block, pl.BlockSpec((1, D), lambda i: (0, 0)), block, block],
        out_specs=block,
        out_shape=jax.ShapeDtypeStruct((ROWS, D), BF),
        compiler_params=params(58),
        cost_estimate=cost(20 * ROWS * D, 8 * ROWS * D),
        name="rows_back",
    )(patches, gain, mine, other)


def split_kernel(rows_ref, one_ref, two_ref, three_ref, out_ref):
    total = rows_ref[...].astype(F32)
    for ref in (one_ref, two_ref, three_ref):
        total = total + ref[...].astype(F32)
    gain = total[BLOCK : BLOCK + 1, :D] + total[BLOCK + 1 : BLOCK + 2, :D]
    gain = gain.astype(BF)
    total = total.astype(BF)
    extras = OWN * LANES
    for s in range(N_DP):
        for k in range(LANES):
            out_ref[s, OWN * k : OWN * (k + 1), :] = total[
                OWN * s : OWN * (s + 1), TILE * k : TILE * (k + 1)
            ]
        for k in range(D // TILE):
            out_ref[s, extras + k : extras + k + 1, :] = gain[
                :, TILE * k : TILE * (k + 1)
            ]


def split(rows, others):
    return pl.pallas_call(
        split_kernel,
        in_specs=[VM] * 4,
        out_specs=VM,
        out_shape=jax.ShapeDtypeStruct((N_DP, MSG, TILE), BF),
        compiler_params=params(12),
        cost_estimate=cost(0, 4 * N_DP * MSG * TILE),
        name="split",
    )(rows, *others)


def finish_kernel(msg_ref, out_ref, gain_ref):
    both = jnp.zeros((MSG, TILE), F32)
    for half in range(2):
        total = msg_ref[half].astype(F32)
        for chip in range(1, 4):
            total = total + msg_ref[2 * chip + half].astype(F32)
        both = both + total
        for k in range(LANES):
            first = D * (k // 5) + HALF * half + TILE * (k % 5)
            out_ref[:, first : first + TILE] = total[OWN * k : OWN * (k + 1)]
    gain_ref[...] = both[OWN * LANES : MSG]


def finish(messages):
    return pl.pallas_call(
        finish_kernel,
        in_specs=[VM],
        out_specs=[VM, VM],
        out_shape=[
            jax.ShapeDtypeStruct((OWN, 3 * D), F32),
            jax.ShapeDtypeStruct((D // TILE, TILE), F32),
        ],
        compiler_params=params(12),
        cost_estimate=cost(0, 6 * N_DP * MSG * TILE),
        name="finish",
    )(messages)


def ring_pairs(df, ds):
    pairs = []
    for d in range(N_DP):
        dx, dz = (ds, df) if d % 2 else (df, ds)
        for x in range(4):
            for z in range(4):
                src = 4 * ((x + dx) % 4) + (z + dz) % 4
                pairs.append((N_INNER * d + src, N_INNER * d + 4 * x + z))
    return pairs


def double_pairs(f_bits, s_bits):
    pairs = []
    for d in range(N_DP):
        x_bits, z_bits = (s_bits, f_bits) if d % 2 else (f_bits, s_bits)
        flip = 4 * x_bits + z_bits
        pairs += [(N_INNER * d + (m ^ flip), N_INNER * d + m) for m in range(N_INNER)]
    return pairs


def from_ring(value, df, ds):
    return lax.ppermute(value, ("dp", "inner"), ring_pairs(df, ds))


def swap_cores(value):
    return lax.ppermute(value, "dp", [(d ^ 1, d) for d in range(N_DP)])


def exchange(value, axis="dp"):
    return lax.all_to_all(value, axis, split_axis=0, concat_axis=0, tiled=True)


def on_device(patches, segments, owners, norm_gain, qkv_weight, cotangent):
    group = lax.axis_index("dp")
    inner = lax.axis_index("inner")
    core, x, z = group % 2, inner // 4, inner % 4
    gain = norm_gain.reshape(1, D)

    pos = jnp.arange(N_INNER)
    df, ds = pos % 4, pos // 4
    m = 4 * ((x + jnp.where(core == 0, df, ds)) % 4) + (
        z + jnp.where(core == 0, ds, df)
    ) % 4
    nat = (
        (jnp.arange(N_DP)[None, :, None] * N_INNER + m[:, None, None]) * OWN
        + jnp.arange(OWN)[None, None, :]
    ).reshape(1, D).astype(F32)

    messages = exchange(build(owners, qkv_weight, segments))
    partner_patches = swap_cores(patches)
    strips = cotangent.reshape(TILES, N_DP, STRIP, D).transpose(1, 0, 2, 3)
    messages, strips = lax.optimization_barrier((messages, strips))
    block, seg, owners_all = compact(group.reshape(1).astype(jnp.int32), messages)
    strips = exchange(strips)

    owner_of = owners_all[:, :TILES].astype(jnp.int32).reshape(N_DP * TILES)
    u = jnp.arange(N_DP * TILES)
    earlier = (owner_of[:, None] == owner_of[None, :]) & (
        u[None, :] // TILES < u[:, None] // TILES
    )
    fwd = (TILES * owner_of + jnp.sum(earlier, axis=1)).astype(jnp.int32)
    wanted = fwd[None, :] == TILES * group + jnp.arange(TILES)[:, None]
    source = jnp.sum(jnp.where(wanted, u[None, :] // TILES, 0), axis=1)
    place_index = jnp.concatenate([2 * (source // 2), source % 2]).astype(jnp.int32)
    mine = jnp.arange(2)[:, None] ^ core
    tile = (TILES * (group - core + mine) + jnp.arange(TILES)[None, :]).reshape(-1)
    owner_here = jnp.sum(jnp.where(tile[:, None] == u[None, :], owner_of, 0), axis=1)
    slot_index = jnp.concatenate(
        [owner_here, jnp.broadcast_to(mine, (2, TILES)).reshape(-1)]
    ).astype(jnp.int32)

    ring = [block] + [from_ring(block, f, 0) for f in (1, 2, 3)]
    near_a, near_b = jnp.concatenate(ring[:2]), jnp.concatenate(ring[2:])
    later_patches, near_b = lax.optimization_barrier((patches, near_b))
    own_prep = prep(later_patches, gain, nat)
    strips, own_prep = lax.optimization_barrier((strips, own_prep))

    heads = to_heads(fwd, strips.reshape(N_DP * TILES, STRIP, D))
    cot = exchange(heads)

    above_a, below_b = from_ring(near_a, 0, 1), from_ring(near_b, 0, -1)
    above_b, below_a = from_ring(near_b, 0, 1), from_ring(near_a, 0, -1)
    above_a, above_b, below_a, below_b = lax.optimization_barrier(
        (above_a, above_b, below_a, below_b)
    )
    far_a, far_b = from_ring(above_a, 0, 1), from_ring(below_b, 0, -1)
    pieces = [near_a, near_b, above_a, above_b, far_a, far_b, below_a, below_b]
    normed, normed_t = zip(own_prep, prep(partner_patches, gain, nat))

    out, dqkv, col_a, col_b, up_a, down_b, up, down, gain_part = main(
        slot_index, seg, normed, normed_t, cot, pieces
    )

    up, down = from_ring(up, 0, -1), from_ring(down, 0, 1)
    slots = exchange(out)
    gain_part = gain_back(gain_part, nat, gain)
    gain_other = lax.ppermute(gain_part, ("dp", "inner"), double_pairs(0, 1))
    partners = back(1, dqkv, pieces, nat)
    up, down, gain_part, gain_other, partners = lax.optimization_barrier(
        (up, down, gain_part, gain_other, partners)
    )
    other = swap_cores(partners)
    up_a, down_b = add([[(up_a, 0), (up, 0)], [(down_b, 0), (down, 0)]])
    from_up_a, from_down_b = from_ring(up_a, 0, -1), from_ring(down_b, 0, 1)
    gain_part = gain_part + gain_other
    gain_other = lax.ppermute(gain_part, ("dp", "inner"), double_pairs(0, 3))
    zero, one, two, three = add(
        [
            [(col_a, 0), (from_up_a, 0), (down, PART)],
            [(col_b, 0), (up, PART), (from_down_b, 0)],
        ],
        (gain_part, gain_other),
    )
    dqkv, _ = lax.optimization_barrier((dqkv, zero))
    mine = back(0, dqkv, pieces, nat)
    others = [from_ring(two, -2, 0), from_ring(three, 1, 0), from_ring(one, -1, 0)]
    others[0], slots, mine = lax.optimization_barrier((others[0], slots, mine))

    attended = place(place_index, slots).reshape(ROWS, D)
    grad_rows = rows_back(patches, gain, mine, other)
    grad_qkv, grad_gain = finish(exchange(split(zero, others)))
    return (attended, grad_rows, grad_qkv, grad_gain.reshape(D))


def solution(mesh):
    both = ("dp", "inner")
    placed = (
        P(both, None),
        P(both, None),
        P(both),
        P(),
        P(both, None),
        P(both, None),
    )
    return jax.shard_map(
        on_device,
        mesh=mesh,
        in_specs=placed,
        out_specs=(P(both, None), P(both, None), P(both, None), P()),
        check_vma=False,
    )
```

```python
import functools

import jax
import jax.numpy as jnp
from jax import lax
from jax.experimental import pallas as pl
from jax.experimental.pallas import tpu as pltpu
from jax.sharding import PartitionSpec as P

D = 1280
HEADS = 16
HDIM = 80
TILE = 128
TILES = 3
N_DP = 8
N_INNER = 16
ROWS = TILES * TILE
PAIR_ROWS = 2 * ROWS
HALF = D // 2
COLS = 3 * HALF
OWN = 10
BLOCK = 80
PART = 160
PIECES = 8
RIDE = 88
STRIP = 16
MSG = 160
LANES = COLS // TILE
EPS = 1e-6
MASKED = -1e30
SCALE = HDIM ** (-0.5)
LOG2E = 1.4426950408889634
BF = jnp.bfloat16
F32 = jnp.float32
VM = pl.BlockSpec(memory_space=pltpu.VMEM)
SM = pl.BlockSpec(memory_space=pltpu.SMEM)
ANY = pl.BlockSpec(memory_space=pltpu.HBM)
NT = (((1,), (1,)), ((), ()))
TN = (((0,), (0,)), ((), ()))
NN = (((1,), (0,)), ((), ()))


def params(mib, **more):
    return pltpu.CompilerParams(vmem_limit_bytes=mib * 2**20, **more)


def cost(flops, nbytes, trans=0):
    return pl.CostEstimate(
        flops=flops // 1000, bytes_accessed=nbytes // 1000, transcendentals=trans // 1000
    )


def dot(a, b, dims=NN):
    return lax.dot_general(a, b, dims, preferred_element_type=F32)


def norm_rows(rows):
    wide = rows.astype(F32)
    centred = wide - jnp.mean(wide, axis=-1, keepdims=True)
    variance = jnp.mean(centred * centred, axis=-1, keepdims=True)
    inv_std = lax.rsqrt(variance + EPS)
    return centred * inv_std, inv_std


def build_order(nat_ref, perm_ref):
    for r in range(D // TILE):
        rows = slice(TILE * r, TILE * (r + 1))
        column = jnp.broadcast_to(nat_ref[:, rows], (TILE, TILE)).T
        for a in range(D // TILE):
            feature = lax.broadcasted_iota(jnp.int32, (TILE, TILE), 1) + TILE * a
            hit = column == feature.astype(F32)
            perm_ref[rows, TILE * a : TILE * (a + 1)] = jnp.where(hit, 1.0, 0.0).astype(BF)


def prep_kernel(patches_ref, gain_ref, nat_ref, normed_ref, normed_t_ref, perm_ref):
    build_order(nat_ref, perm_ref)
    standard, _ = norm_rows(patches_ref[...])
    normed = (standard * gain_ref[...]).astype(BF)
    normed_ref[...] = dot(normed, perm_ref[...], NT).astype(BF)
    normed_t_ref[...] = dot(perm_ref[...], normed, NT).astype(BF)


def prep(patches, gain, nat):
    return pl.pallas_call(
        prep_kernel,
        in_specs=[VM] * 3,
        out_specs=[VM] * 2,
        out_shape=[
            jax.ShapeDtypeStruct((ROWS, D), BF),
            jax.ShapeDtypeStruct((D, ROWS), BF),
        ],
        scratch_shapes=[pltpu.VMEM((D, D), BF)],
        compiler_params=params(58),
        cost_estimate=cost(4 * ROWS * D * D, 6 * ROWS * D),
        name="prep",
    )(patches, gain, nat)


def build_kernel(own_ref, w_ref, seg_ref, out_ref):
    lane = lax.broadcasted_iota(jnp.int32, (1, TILE), 1)
    owners = jnp.zeros((1, TILE), jnp.int32)
    for t in range(TILES):
        owners = jnp.where(lane == t, own_ref[t], owners)
    for half in range(2):
        for k in range(LANES):
            first = D * (k // 5) + HALF * half + TILE * (k % 5)
            out_ref[half, OWN * k : OWN * (k + 1), :] = w_ref[:, first : first + TILE]
        extras = OWN * LANES
        out_ref[half, extras:MSG, :] = jnp.zeros((MSG - extras, TILE), BF)
        out_ref[half, extras : extras + 1, :] = owners.astype(F32).astype(BF)
        out_ref[half, extras + 1 : extras + 1 + TILES, :] = (
            seg_ref[...].astype(F32).astype(BF)
        )
    for d in range(2, N_DP):
        out_ref[d] = out_ref[d % 2]


def build(owners, weight, segments):
    return pl.pallas_call(
        build_kernel,
        in_specs=[SM, VM, VM],
        out_specs=VM,
        out_shape=jax.ShapeDtypeStruct((N_DP, MSG, TILE), BF),
        compiler_params=params(58),
        cost_estimate=cost(0, 2 * N_DP * MSG * TILE),
        name="build",
    )(owners, weight, segments)


def compact_kernel(group_ref, msg_ref, w_ref, seg_ref, own_ref):
    group = group_ref[0]
    extras = OWN * LANES
    seg_ref[...] = jnp.zeros_like(seg_ref)
    for s in range(N_DP):
        for k in range(LANES):
            w_ref[OWN * s : OWN * (s + 1), TILE * k : TILE * (k + 1)] = msg_ref[
                s, OWN * k : OWN * (k + 1), :
            ]
        own_ref[s : s + 1, :] = msg_ref[s, extras : extras + 1, :].astype(F32)
    for rel in range(2):
        src = group + rel * (1 - 2 * (group % 2))
        seg_ref[TILES * rel : TILES * (rel + 1), :] = msg_ref[
            src, extras + 1 : extras + 1 + TILES, :
        ].astype(F32)


def compact(group, messages):
    return pl.pallas_call(
        compact_kernel,
        in_specs=[SM, VM],
        out_specs=[VM] * 3,
        out_shape=[
            jax.ShapeDtypeStruct((BLOCK, COLS), BF),
            jax.ShapeDtypeStruct((8, TILE), F32),
            jax.ShapeDtypeStruct((N_DP, TILE), F32),
        ],
        compiler_params=params(12),
        cost_estimate=cost(0, 4 * N_DP * MSG * TILE),
        name="compact",
    )(group, messages)


def to_heads_kernel(fwd_ref, in_ref, out_ref):
    for d in range(N_DP):
        half = slice(HALF * (d % 2), HALF * (d % 2 + 1))
        for k in range(2 * TILES):
            u = TILES * (2 * (d // 2) + ((d % 2) ^ (k // TILES))) + k % TILES
            out_ref[d, k] = in_ref[fwd_ref[u], :, half]


def to_heads(fwd, strips):
    return pl.pallas_call(
        to_heads_kernel,
        in_specs=[SM, VM],
        out_specs=VM,
        out_shape=jax.ShapeDtypeStruct((N_DP, 2 * TILES, STRIP, HALF), BF),
        cost_estimate=cost(0, 4 * ROWS * D),
        compiler_params=params(12),
        name="to_heads",
    )(fwd, strips)


def place_kernel(idx_ref, left_ref, right_ref, out_ref):
    out_ref[0, :, :HALF] = left_ref[0, 0]
    out_ref[0, :, HALF:] = right_ref[0, 0]


def place(index, slots):
    def half(c):
        return pl.BlockSpec(
            (1, 1, TILE, HALF), lambda p, g: (g[p] + c, g[TILES + p], 0, 0)
        )

    spec = pltpu.PrefetchScalarGridSpec(
        num_scalar_prefetch=1,
        grid=(TILES,),
        in_specs=[half(0), half(1)],
        out_specs=pl.BlockSpec((1, TILE, D), lambda p, g: (p, 0, 0)),
    )
    return pl.pallas_call(
        place_kernel,
        grid_spec=spec,
        out_shape=jax.ShapeDtypeStruct((TILES, TILE, D), BF),
        compiler_params=params(12),
        cost_estimate=cost(0, 4 * ROWS * D),
        name="place",
    )(index, slots, slots)


def window_masks(i):
    lane = lax.broadcasted_iota(jnp.int32, (TILE, 256), 1)
    start = 32 * i
    first = (lane >= start) & (lane < start + HDIM)
    second = (lane >= start + HDIM) & (lane < start + 2 * HDIM)
    return first, second


def stack_heads(window, masks):
    zero = jnp.zeros_like(window)
    return jnp.concatenate([jnp.where(m, window, zero) for m in masks], axis=0)


def rows_of_heads(both):
    return jnp.concatenate([both[:, :TILE], both[:, TILE:]], axis=0)


def halves(fn, *arrays):
    return jnp.concatenate(
        [fn(*(a[:, :TILE] for a in arrays)), fn(*(a[:, TILE:] for a in arrays))], axis=1
    )


def wide_max(a):
    return jnp.broadcast_to(jnp.max(a, axis=-1, keepdims=True), a.shape)


def wide_sum(a):
    return jnp.broadcast_to(jnp.sum(a, axis=-1, keepdims=True), a.shape)


GRAD_CHUNKS = [pl.ds(0, 512), pl.ds(512, 512), pl.ds(1024, 512), pl.ds(1536, 384)]
CHUNKS = [pl.ds(0, 384), pl.ds(384, 768), pl.ds(1152, 768)]


def start(copies):
    for copy in copies:
        copy.start()


def wait(copies):
    for copy in copies:
        copy.wait()


def load_weight(pieces, weight, sems):
    return [
        [
            pltpu.make_async_copy(
                piece.at[:, cols],
                weight.at[pl.ds(PART * b, PART), cols],
                sems.at[n, b],
            )
            for b, piece in enumerate(pieces)
        ]
        for n, cols in enumerate(CHUNKS)
    ]


def load_rows(refs, rows, sems):
    return [
        pltpu.make_async_copy(ref, rows.at[pl.ds(ROWS * h, ROWS)], sems.at[h])
        for h, ref in enumerate(refs)
    ]


def load_features(refs, normed_t, sems):
    return [
        pltpu.make_async_copy(ref, normed_t.at[:, pl.ds(ROWS * h, ROWS)], sems.at[h])
        for h, ref in enumerate(refs)
    ]


def gradient(normed_t, dqkv, weight, outs, staged, gain_part, sems):
    copies = []
    places = [(0, 0), (1, 0), (2, 0), (4, PART), (4, 0), (5, 0), (5, PART), (3, 0)]
    for c, cols in enumerate(GRAD_CHUNKS):
        whole = dot(normed_t[...], dqkv[:, cols])
        product = whole * weight[:, cols].astype(F32)
        lanes = sum(
            product[:, TILE * k : TILE * (k + 1)] for k in range(cols.size // TILE)
        )
        gain_part[...] = lanes if c == 0 else gain_part[...] + lanes
        for k in range(PIECES):
            staged[k, :, cols] = whole[PART * k : PART * (k + 1)].astype(BF)
            copies.append(
                pltpu.make_async_copy(
                    staged.at[k, :, cols],
                    outs[places[k][0]].at[pl.ds(places[k][1], PART), cols],
                    sems.at[c, k],
                )
            )
            copies[-1].start()
    wait(copies)


def main_kernel(
    idx_ref,
    seg_ref,
    normed_ref,
    partner_ref,
    normed_t_ref,
    partner_t_ref,
    cot_ref,
    *refs,
):
    pieces, slots_ref, dqkv_ref = refs[:PIECES], refs[PIECES], refs[PIECES + 1]
    grads, gain_ref = refs[PIECES + 2 : PIECES + 8], refs[PIECES + 8]
    (
        normed,
        qkv,
        cot,
        weight,
        normed_t,
        dqkv,
        out_tiles,
        staged,
        row_sems,
        cot_sems,
        w_sems,
        t_sems,
        slot_sems,
        dqkv_sems,
        grad_sems,
    ) = refs[PIECES + 9 :]
    row_copies = load_rows((normed_ref, partner_ref), normed, row_sems)
    w_copies = load_weight(pieces, weight, w_sems)
    cot_copies = [
        pltpu.make_async_copy(cot_ref.at[j], cot.at[:, j], cot_sems.at[j])
        for j in range(N_DP)
    ]
    t_copies = load_features((normed_t_ref, partner_t_ref), normed_t, t_sems)
    start(row_copies)
    for copies in w_copies:
        start(copies)
    start(cot_copies)
    start(t_copies)
    wait(row_copies)
    for c, cols in enumerate(CHUNKS):
        wait(w_copies[c])
        qkv[:, cols] = dot(normed[...], weight[:, cols]).astype(BF)
    wait(cot_copies)

    def leave(t):
        rows = pl.ds(pl.multiple_of(t * TILE, TILE), TILE)
        return [
            pltpu.make_async_copy(
                out_tiles.at[t],
                slots_ref.at[idx_ref[t], idx_ref[2 * TILES + t]],
                slot_sems.at[t],
            ),
            pltpu.make_async_copy(dqkv.at[rows], dqkv_ref.at[rows], dqkv_sems.at[t]),
        ]

    @pl.loop(0, TILES)
    def _(step):
        pairs = range(8)
        tiles = [2 * step, 2 * step + 1]
        rows = [pl.ds(pl.multiple_of(t * TILE, TILE), TILE) for t in tiles]
        same = []
        for t in tiles:
            seg = jnp.broadcast_to(seg_ref[pl.ds(t, 1), :], (TILE, TILE))
            equal = seg == seg.T
            same.append(jnp.concatenate([equal, equal], axis=1))
        masks = [window_masks(i % 4) for i in pairs]
        windows = [slice(128 * (i % 4), 128 * (i % 4) + 256) for i in pairs]

        def window(a, i):
            first = HALF * a + 128 * (i % 4)
            return qkv[rows[i // 4], first : first + 256]

        q = [window(0, i) for i in pairs]
        d_out = [
            cot[tiles[i // 4], :, :, windows[i]].reshape(TILE, 256) for i in pairs
        ]
        kk = [stack_heads(window(1, i), masks[i]) for i in pairs]
        vv = [stack_heads(window(2, i), masks[i]) for i in pairs]
        scores = [dot(q[i], kk[i], NT) for i in pairs]
        d_probs = [dot(d_out[i], vv[i], NT) for i in pairs]
        scores = [
            jnp.where(same[i // 4], scores[i] * (SCALE * LOG2E), MASKED) for i in pairs
        ]
        tops = [halves(wide_max, x) for x in scores]
        expo = [jnp.exp2(x - m) for x, m in zip(scores, tops)]
        sums = [halves(wide_sum, x) for x in expo]
        weights = [x * (1.0 / total) for x, total in zip(expo, sums)]
        rounded = [x.astype(BF) for x in weights]
        outs = [dot(rounded[i], vv[i]) for i in pairs]
        dvs = [
            dot(rows_of_heads(rounded[i]), stack_heads(d_out[i], masks[i]), TN)
            for i in pairs
        ]
        inner = [halves(wide_sum, d_probs[i] * weights[i]) for i in pairs]
        d_scores = [
            (weights[i] * (d_probs[i] - inner[i]) * SCALE).astype(BF) for i in pairs
        ]
        dqs = [dot(d_scores[i], kk[i]) for i in pairs]
        dks = [
            dot(rows_of_heads(d_scores[i]), stack_heads(q[i], masks[i]), TN)
            for i in pairs
        ]

        def lanes(vals):
            parts = [vals[0][:, :TILE]]
            for i in range(3):
                parts.append(vals[i][:, TILE:] + vals[i + 1][:, :TILE])
            parts.append(vals[3][:, TILE:])
            return jnp.concatenate([p.astype(BF) for p in parts], axis=1)

        for n, t in enumerate(tiles):
            part = slice(4 * n, 4 * n + 4)
            out_tiles[t] = lanes(outs[part])
            for a, vals in enumerate((dqs, dks, dvs)):
                dqkv[rows[n], HALF * a : HALF * (a + 1)] = lanes(vals[part])
            start(leave(t))

    wait(t_copies)
    gradient(normed_t, dqkv, weight, grads, staged, gain_ref, grad_sems)
    for t in range(2 * TILES):
        wait(leave(t))


def main(index, seg, normed, normed_t, cot, pieces):
    return pl.pallas_call(
        main_kernel,
        in_specs=[SM, VM] + [ANY] * (5 + PIECES),
        out_specs=[ANY] * 8 + [VM],
        out_shape=[
            jax.ShapeDtypeStruct((N_DP, 2, TILE, HALF), BF),
            jax.ShapeDtypeStruct((PAIR_ROWS, COLS), BF),
        ]
        + [jax.ShapeDtypeStruct((PART, COLS), BF)] * 4
        + [jax.ShapeDtypeStruct((2 * PART, COLS), BF)] * 2
        + [jax.ShapeDtypeStruct((D, TILE), F32)],
        scratch_shapes=[
            pltpu.VMEM((PAIR_ROWS, D), BF),
            pltpu.VMEM((PAIR_ROWS, COLS), BF),
            pltpu.VMEM((2 * TILES, N_DP, STRIP, HALF), BF),
            pltpu.VMEM((D, COLS), BF),
            pltpu.VMEM((D, PAIR_ROWS), BF),
            pltpu.VMEM((PAIR_ROWS, COLS), BF),
            pltpu.VMEM((2 * TILES, TILE, HALF), BF),
            pltpu.VMEM((PIECES, PART, COLS), BF),
            pltpu.SemaphoreType.DMA((2,)),
            pltpu.SemaphoreType.DMA((N_DP,)),
            pltpu.SemaphoreType.DMA((len(CHUNKS), PIECES)),
            pltpu.SemaphoreType.DMA((2,)),
            pltpu.SemaphoreType.DMA((2 * TILES,)),
            pltpu.SemaphoreType.DMA((2 * TILES,)),
            pltpu.SemaphoreType.DMA((len(GRAD_CHUNKS), PIECES)),
        ],
        compiler_params=params(58),
        cost_estimate=cost(8 * 10**9, 20 * 2**20, 10**6),
        name="main",
    )(index, seg, *normed, *normed_t, cot, *pieces)


def add_parts(counts, firsts, refs):
    totals, used = [], 0
    for count in counts:
        total = jnp.zeros((PART, COLS), F32)
        for k in range(used, used + count):
            total = total + refs[k][firsts[k] : firsts[k] + PART, :].astype(F32)
        used += count
        totals.append(total)
    return totals


def add_kernel(counts, firsts, *refs):
    totals = add_parts(counts, firsts, refs)
    for out_ref, total in zip(refs[sum(counts) :], totals):
        out_ref[...] = total.astype(BF)


def column_kernel(counts, firsts, gain_ref, other_ref, *refs):
    gain = gain_ref[...] + other_ref[...]
    outs = refs[sum(counts) :]
    totals = add_parts(counts, firsts, refs)
    for n, out_ref in enumerate(outs):
        block = totals[n // 2][BLOCK * (n % 2) : BLOCK * (n % 2 + 1)]
        out_ref[0:BLOCK, :] = block.astype(BF)
        put_gain(gain, out_ref, BLOCK, RIDE)


def put_gain(gain, ref, first, last):
    hi = gain.astype(BF).astype(F32)
    lo = gain - hi
    ref[first:last, :] = jnp.zeros((last - first, COLS), BF)
    for k in range(D // TILE):
        cols = slice(TILE * k, TILE * (k + 1))
        ref[first : first + 1, cols] = hi[k : k + 1].astype(BF)
        ref[first + 1 : first + 2, cols] = lo[k : k + 1].astype(BF)


def add(groups, gains=()):
    parts = [part for group in groups for part in group]
    rows, n = (RIDE, 2 * len(groups)) if gains else (PART, len(groups))
    return pl.pallas_call(
        functools.partial(
            column_kernel if gains else add_kernel,
            [len(group) for group in groups],
            [first for _, first in parts],
        ),
        in_specs=[VM] * (len(gains) + len(parts)),
        out_specs=[VM] * n,
        out_shape=[jax.ShapeDtypeStruct((rows, COLS), BF)] * n,
        compiler_params=params(12),
        cost_estimate=cost(0, 4 * len(parts) * PART * COLS),
        name="add",
    )(*gains, *[array for array, _ in parts])


def gain_kernel(part_ref, nat_ref, gain_ref, out_ref, perm_ref):
    build_order(nat_ref, perm_ref)
    rest = jnp.sum(part_ref[...], axis=1, keepdims=True)
    rest = jnp.broadcast_to(rest, (D, TILE))
    total = jnp.zeros((1, D), F32)
    for _ in range(3):
        term = rest.astype(BF)
        rest = rest - term.astype(F32)
        total = total + dot(term, perm_ref[...], TN)[0:1]
    total = total / gain_ref[...]
    out_ref[...] = jnp.zeros_like(out_ref)
    for k in range(D // TILE):
        out_ref[k : k + 1, :] = total[:, TILE * k : TILE * (k + 1)]


def gain_back(part, nat, gain):
    return pl.pallas_call(
        gain_kernel,
        in_specs=[VM] * 3,
        out_specs=VM,
        out_shape=jax.ShapeDtypeStruct((STRIP, TILE), F32),
        scratch_shapes=[pltpu.VMEM((D, D), BF)],
        compiler_params=params(24),
        cost_estimate=cost(0, 4 * D * TILE),
        name="gain",
    )(part, nat, gain)


def back_kernel(half, nat_ref, dqkv_ref, *refs):
    pieces, (out_ref, weight, perm_ref, dqkv, w_sems, q_sems) = (
        refs[:PIECES],
        refs[PIECES:],
    )
    w_copies = load_weight(pieces, weight, w_sems)
    rows = pl.ds(ROWS * half, ROWS)
    for c, cols in enumerate(CHUNKS):
        w_copies[c].append(
            pltpu.make_async_copy(
                dqkv_ref.at[rows, cols], dqkv.at[:, cols], q_sems.at[c]
            )
        )
        start(w_copies[c])
    build_order(nat_ref, perm_ref)
    d_normed = jnp.zeros((ROWS, D), F32)
    for c, cols in enumerate(CHUNKS):
        wait(w_copies[c])
        d_normed = d_normed + dot(dqkv[:, cols], weight[:, cols], NT)
    out_ref[...] = dot(d_normed.astype(BF), perm_ref[...]).astype(BF)


def back(half, dqkv, pieces, nat):
    return pl.pallas_call(
        functools.partial(back_kernel, half),
        in_specs=[VM] + [ANY] * (1 + PIECES),
        out_specs=VM,
        out_shape=jax.ShapeDtypeStruct((ROWS, D), BF),
        scratch_shapes=[
            pltpu.VMEM((D, COLS), BF),
            pltpu.VMEM((D, D), BF),
            pltpu.VMEM((ROWS, COLS), BF),
            pltpu.SemaphoreType.DMA((len(CHUNKS), PIECES)),
            pltpu.SemaphoreType.DMA((len(CHUNKS),)),
        ],
        compiler_params=params(58),
        cost_estimate=cost(2 * ROWS * D * (D + COLS), 15 * 2**20),
        name="back",
    )(nat, dqkv, *pieces)


def rows_kernel(patches_ref, gain_ref, mine_ref, other_ref, out_ref):
    standard, inv_std = norm_rows(patches_ref[...])
    d_normed = mine_ref[...].astype(F32) + other_ref[...].astype(F32)
    scaled = d_normed * gain_ref[...]
    back_rows = inv_std * (
        scaled
        - jnp.mean(scaled, axis=-1, keepdims=True)
        - standard * jnp.mean(scaled * standard, axis=-1, keepdims=True)
    )
    out_ref[...] = back_rows.astype(BF)


def rows_back(patches, gain, mine, other):
    block = pl.BlockSpec((TILE, D), lambda i: (i, 0))
    return pl.pallas_call(
        rows_kernel,
        grid=(TILES,),
        in_specs=[block, pl.BlockSpec((1, D), lambda i: (0, 0)), block, block],
        out_specs=block,
        out_shape=jax.ShapeDtypeStruct((ROWS, D), BF),
        compiler_params=params(58),
        cost_estimate=cost(20 * ROWS * D, 8 * ROWS * D),
        name="rows_back",
    )(patches, gain, mine, other)


def split_kernel(rows_ref, one_ref, two_ref, three_ref, out_ref):
    total = rows_ref[...].astype(F32)
    for ref in (one_ref, two_ref, three_ref):
        total = total + ref[...].astype(F32)
    gain = total[BLOCK : BLOCK + 1, :D] + total[BLOCK + 1 : BLOCK + 2, :D]
    gain = gain.astype(BF)
    total = total.astype(BF)
    extras = OWN * LANES
    for s in range(N_DP):
        for k in range(LANES):
            out_ref[s, OWN * k : OWN * (k + 1), :] = total[
                OWN * s : OWN * (s + 1), TILE * k : TILE * (k + 1)
            ]
        for k in range(D // TILE):
            out_ref[s, extras + k : extras + k + 1, :] = gain[
                :, TILE * k : TILE * (k + 1)
            ]


def split(rows, others):
    return pl.pallas_call(
        split_kernel,
        in_specs=[VM] * 4,
        out_specs=VM,
        out_shape=jax.ShapeDtypeStruct((N_DP, MSG, TILE), BF),
        compiler_params=params(12),
        cost_estimate=cost(0, 4 * N_DP * MSG * TILE),
        name="split",
    )(rows, *others)


def finish_kernel(msg_ref, out_ref, gain_ref):
    both = jnp.zeros((MSG, TILE), F32)
    for half in range(2):
        total = msg_ref[half].astype(F32)
        for chip in range(1, 4):
            total = total + msg_ref[2 * chip + half].astype(F32)
        both = both + total
        for k in range(LANES):
            first = D * (k // 5) + HALF * half + TILE * (k % 5)
            out_ref[:, first : first + TILE] = total[OWN * k : OWN * (k + 1)]
    gain_ref[...] = both[OWN * LANES : MSG]


def finish(messages):
    return pl.pallas_call(
        finish_kernel,
        in_specs=[VM],
        out_specs=[VM, VM],
        out_shape=[
            jax.ShapeDtypeStruct((OWN, 3 * D), F32),
            jax.ShapeDtypeStruct((D // TILE, TILE), F32),
        ],
        compiler_params=params(12),
        cost_estimate=cost(0, 6 * N_DP * MSG * TILE),
        name="finish",
    )(messages)


def ring_pairs(df, ds):
    pairs = []
    for d in range(N_DP):
        dx, dz = (ds, df) if d % 2 else (df, ds)
        for x in range(4):
            for z in range(4):
                src = 4 * ((x + dx) % 4) + (z + dz) % 4
                pairs.append((N_INNER * d + src, N_INNER * d + 4 * x + z))
    return pairs


def double_pairs(f_bits, s_bits):
    pairs = []
    for d in range(N_DP):
        x_bits, z_bits = (s_bits, f_bits) if d % 2 else (f_bits, s_bits)
        flip = 4 * x_bits + z_bits
        pairs += [(N_INNER * d + (m ^ flip), N_INNER * d + m) for m in range(N_INNER)]
    return pairs


def from_ring(value, df, ds):
    return lax.ppermute(value, ("dp", "inner"), ring_pairs(df, ds))


def swap_cores(value):
    return lax.ppermute(value, "dp", [(d ^ 1, d) for d in range(N_DP)])


def exchange(value, axis="dp"):
    return lax.all_to_all(value, axis, split_axis=0, concat_axis=0, tiled=True)


def on_device(patches, segments, owners, norm_gain, qkv_weight, cotangent):
    group = lax.axis_index("dp")
    inner = lax.axis_index("inner")
    core, x, z = group % 2, inner // 4, inner % 4
    gain = norm_gain.reshape(1, D)

    pos = jnp.arange(N_INNER)
    df, ds = pos % 4, pos // 4
    m = 4 * ((x + jnp.where(core == 0, df, ds)) % 4) + (
        z + jnp.where(core == 0, ds, df)
    ) % 4
    nat = (
        (jnp.arange(N_DP)[None, :, None] * N_INNER + m[:, None, None]) * OWN
        + jnp.arange(OWN)[None, None, :]
    ).reshape(1, D).astype(F32)

    messages = exchange(build(owners, qkv_weight, segments))
    partner_patches = swap_cores(patches)
    strips = cotangent.reshape(TILES, N_DP, STRIP, D).transpose(1, 0, 2, 3)
    messages, strips = lax.optimization_barrier((messages, strips))
    block, seg, owners_all = compact(group.reshape(1).astype(jnp.int32), messages)
    strips = exchange(strips)

    owner_of = owners_all[:, :TILES].astype(jnp.int32).reshape(N_DP * TILES)
    u = jnp.arange(N_DP * TILES)
    earlier = (owner_of[:, None] == owner_of[None, :]) & (
        u[None, :] // TILES < u[:, None] // TILES
    )
    fwd = (TILES * owner_of + jnp.sum(earlier, axis=1)).astype(jnp.int32)
    wanted = fwd[None, :] == TILES * group + jnp.arange(TILES)[:, None]
    source = jnp.sum(jnp.where(wanted, u[None, :] // TILES, 0), axis=1)
    place_index = jnp.concatenate([2 * (source // 2), source % 2]).astype(jnp.int32)
    mine = jnp.arange(2)[:, None] ^ core
    tile = (TILES * (group - core + mine) + jnp.arange(TILES)[None, :]).reshape(-1)
    owner_here = jnp.sum(jnp.where(tile[:, None] == u[None, :], owner_of, 0), axis=1)
    slot_index = jnp.concatenate(
        [owner_here, jnp.broadcast_to(mine, (2, TILES)).reshape(-1)]
    ).astype(jnp.int32)

    ring = [block] + [from_ring(block, f, 0) for f in (1, 2, 3)]
    near_a, near_b = jnp.concatenate(ring[:2]), jnp.concatenate(ring[2:])
    later_patches, near_b = lax.optimization_barrier((patches, near_b))
    own_prep = prep(later_patches, gain, nat)
    strips, own_prep = lax.optimization_barrier((strips, own_prep))

    heads = to_heads(fwd, strips.reshape(N_DP * TILES, STRIP, D))
    cot = exchange(heads)

    above_a, below_b = from_ring(near_a, 0, 1), from_ring(near_b, 0, -1)
    above_b, below_a = from_ring(near_b, 0, 1), from_ring(near_a, 0, -1)
    above_a, above_b, below_a, below_b = lax.optimization_barrier(
        (above_a, above_b, below_a, below_b)
    )
    far_a, far_b = from_ring(above_a, 0, 1), from_ring(below_b, 0, -1)
    pieces = [near_a, near_b, above_a, above_b, far_a, far_b, below_a, below_b]
    normed, normed_t = zip(own_prep, prep(partner_patches, gain, nat))

    out, dqkv, col_a, col_b, up_a, down_b, up, down, gain_part = main(
        slot_index, seg, normed, normed_t, cot, pieces
    )

    up, down = from_ring(up, 0, -1), from_ring(down, 0, 1)
    slots = exchange(out)
    gain_part = gain_back(gain_part, nat, gain)
    gain_other = lax.ppermute(gain_part, ("dp", "inner"), double_pairs(0, 1))
    partners = back(1, dqkv, pieces, nat)
    up, down, gain_part, gain_other, partners = lax.optimization_barrier(
        (up, down, gain_part, gain_other, partners)
    )
    other = swap_cores(partners)
    up_a, down_b = add([[(up_a, 0), (up, 0)], [(down_b, 0), (down, 0)]])
    from_up_a, from_down_b = from_ring(up_a, 0, -1), from_ring(down_b, 0, 1)
    gain_part = gain_part + gain_other
    gain_other = lax.ppermute(gain_part, ("dp", "inner"), double_pairs(0, 3))
    zero, one, two, three = add(
        [
            [(col_a, 0), (from_up_a, 0), (down, PART)],
            [(col_b, 0), (up, PART), (from_down_b, 0)],
        ],
        (gain_part, gain_other),
    )
    dqkv, _ = lax.optimization_barrier((dqkv, zero))
    mine = back(0, dqkv, pieces, nat)
    others = [from_ring(two, -2, 0), from_ring(three, 1, 0), from_ring(one, -1, 0)]
    others[0], slots, mine = lax.optimization_barrier((others[0], slots, mine))

    attended = place(place_index, slots).reshape(ROWS, D)
    grad_rows = rows_back(patches, gain, mine, other)
    grad_qkv, grad_gain = finish(exchange(split(zero, others)))
    return (attended, grad_rows, grad_qkv, grad_gain.reshape(D))


def solution(mesh):
    both = ("dp", "inner")
    placed = (
        P(both, None),
        P(both, None),
        P(both),
        P(),
        P(both, None),
        P(both, None),
    )
    return jax.shard_map(
        on_device,
        mesh=mesh,
        in_specs=placed,
        out_specs=(P(both, None), P(both, None), P(both, None), P()),
        check_vma=False,
    )
```

```python
import functools

import jax
import jax.numpy as jnp
from jax import lax
from jax.experimental import pallas as pl
from jax.experimental.pallas import tpu as pltpu
from jax.sharding import PartitionSpec as P

D = 1280
HEADS = 16
HDIM = 80
TILE = 128
TILES = 3
N_DP = 8
N_INNER = 16
ROWS = TILES * TILE
PAIR_ROWS = 2 * ROWS
HALF = D // 2
COLS = 3 * HALF
OWN = 10
BLOCK = 80
PART = 160
PIECES = 8
RIDE = 88
STRIP = 16
MSG = 160
LANES = COLS // TILE
EPS = 1e-6
MASKED = -1e30
SCALE = HDIM ** (-0.5)
LOG2E = 1.4426950408889634
BF = jnp.bfloat16
F32 = jnp.float32
VM = pl.BlockSpec(memory_space=pltpu.VMEM)
SM = pl.BlockSpec(memory_space=pltpu.SMEM)
ANY = pl.BlockSpec(memory_space=pltpu.HBM)
NT = (((1,), (1,)), ((), ()))
TN = (((0,), (0,)), ((), ()))
NN = (((1,), (0,)), ((), ()))


def params(mib, **more):
    return pltpu.CompilerParams(vmem_limit_bytes=mib * 2**20, **more)


def cost(flops, nbytes, trans=0):
    return pl.CostEstimate(
        flops=flops // 1000, bytes_accessed=nbytes // 1000, transcendentals=trans // 1000
    )


def dot(a, b, dims=NN):
    return lax.dot_general(a, b, dims, preferred_element_type=F32)


def norm_rows(rows):
    wide = rows.astype(F32)
    centred = wide - jnp.mean(wide, axis=-1, keepdims=True)
    variance = jnp.mean(centred * centred, axis=-1, keepdims=True)
    inv_std = lax.rsqrt(variance + EPS)
    return centred * inv_std, inv_std


def build_order(nat_ref, perm_ref):
    for r in range(D // TILE):
        rows = slice(TILE * r, TILE * (r + 1))
        column = jnp.broadcast_to(nat_ref[:, rows], (TILE, TILE)).T
        for a in range(D // TILE):
            feature = lax.broadcasted_iota(jnp.int32, (TILE, TILE), 1) + TILE * a
            hit = column == feature.astype(F32)
            perm_ref[rows, TILE * a : TILE * (a + 1)] = jnp.where(hit, 1.0, 0.0).astype(BF)


def prep_kernel(patches_ref, gain_ref, nat_ref, normed_ref, normed_t_ref, perm_ref):
    build_order(nat_ref, perm_ref)
    standard, _ = norm_rows(patches_ref[...])
    normed = (standard * gain_ref[...]).astype(BF)
    normed_ref[...] = dot(normed, perm_ref[...], NT).astype(BF)
    normed_t_ref[...] = dot(perm_ref[...], normed, NT).astype(BF)


def prep(patches, gain, nat):
    return pl.pallas_call(
        prep_kernel,
        in_specs=[VM] * 3,
        out_specs=[VM] * 2,
        out_shape=[
            jax.ShapeDtypeStruct((ROWS, D), BF),
            jax.ShapeDtypeStruct((D, ROWS), BF),
        ],
        scratch_shapes=[pltpu.VMEM((D, D), BF)],
        compiler_params=params(58),
        cost_estimate=cost(4 * ROWS * D * D, 6 * ROWS * D),
        name="prep",
    )(patches, gain, nat)


def build_kernel(own_ref, w_ref, seg_ref, out_ref):
    lane = lax.broadcasted_iota(jnp.int32, (1, TILE), 1)
    owners = jnp.zeros((1, TILE), jnp.int32)
    for t in range(TILES):
        owners = jnp.where(lane == t, own_ref[t], owners)
    for half in range(2):
        for k in range(LANES):
            first = D * (k // 5) + HALF * half + TILE * (k % 5)
            out_ref[half, OWN * k : OWN * (k + 1), :] = w_ref[:, first : first + TILE]
        extras = OWN * LANES
        out_ref[half, extras:MSG, :] = jnp.zeros((MSG - extras, TILE), BF)
        out_ref[half, extras : extras + 1, :] = owners.astype(F32).astype(BF)
        out_ref[half, extras + 1 : extras + 1 + TILES, :] = (
            seg_ref[...].astype(F32).astype(BF)
        )
    for d in range(2, N_DP):
        out_ref[d] = out_ref[d % 2]


def build(owners, weight, segments):
    return pl.pallas_call(
        build_kernel,
        in_specs=[SM, VM, VM],
        out_specs=VM,
        out_shape=jax.ShapeDtypeStruct((N_DP, MSG, TILE), BF),
        compiler_params=params(58),
        cost_estimate=cost(0, 2 * N_DP * MSG * TILE),
        name="build",
    )(owners, weight, segments)


def compact_kernel(group_ref, msg_ref, w_ref, seg_ref, own_ref):
    group = group_ref[0]
    extras = OWN * LANES
    seg_ref[...] = jnp.zeros_like(seg_ref)
    for s in range(N_DP):
        for k in range(LANES):
            w_ref[OWN * s : OWN * (s + 1), TILE * k : TILE * (k + 1)] = msg_ref[
                s, OWN * k : OWN * (k + 1), :
            ]
        own_ref[s : s + 1, :] = msg_ref[s, extras : extras + 1, :].astype(F32)
    for rel in range(2):
        src = group + rel * (1 - 2 * (group % 2))
        seg_ref[TILES * rel : TILES * (rel + 1), :] = msg_ref[
            src, extras + 1 : extras + 1 + TILES, :
        ].astype(F32)


def compact(group, messages):
    return pl.pallas_call(
        compact_kernel,
        in_specs=[SM, VM],
        out_specs=[VM] * 3,
        out_shape=[
            jax.ShapeDtypeStruct((BLOCK, COLS), BF),
            jax.ShapeDtypeStruct((8, TILE), F32),
            jax.ShapeDtypeStruct((N_DP, TILE), F32),
        ],
        compiler_params=params(12),
        cost_estimate=cost(0, 4 * N_DP * MSG * TILE),
        name="compact",
    )(group, messages)


def to_heads_kernel(fwd_ref, in_ref, out_ref):
    for d in range(N_DP):
        half = slice(HALF * (d % 2), HALF * (d % 2 + 1))
        for k in range(2 * TILES):
            u = TILES * (2 * (d // 2) + ((d % 2) ^ (k // TILES))) + k % TILES
            out_ref[d, k] = in_ref[fwd_ref[u], :, half]


def to_heads(fwd, strips):
    return pl.pallas_call(
        to_heads_kernel,
        in_specs=[SM, VM],
        out_specs=VM,
        out_shape=jax.ShapeDtypeStruct((N_DP, 2 * TILES, STRIP, HALF), BF),
        cost_estimate=cost(0, 4 * ROWS * D),
        compiler_params=params(12),
        name="to_heads",
    )(fwd, strips)


def place_kernel(idx_ref, left_ref, right_ref, out_ref):
    out_ref[0, :, :HALF] = left_ref[0, 0]
    out_ref[0, :, HALF:] = right_ref[0, 0]


def place(index, slots):
    def half(c):
        return pl.BlockSpec(
            (1, 1, TILE, HALF), lambda p, g: (g[p] + c, g[TILES + p], 0, 0)
        )

    spec = pltpu.PrefetchScalarGridSpec(
        num_scalar_prefetch=1,
        grid=(TILES,),
        in_specs=[half(0), half(1)],
        out_specs=pl.BlockSpec((1, TILE, D), lambda p, g: (p, 0, 0)),
    )
    return pl.pallas_call(
        place_kernel,
        grid_spec=spec,
        out_shape=jax.ShapeDtypeStruct((TILES, TILE, D), BF),
        compiler_params=params(12),
        cost_estimate=cost(0, 4 * ROWS * D),
        name="place",
    )(index, slots, slots)


def window_masks(i):
    lane = lax.broadcasted_iota(jnp.int32, (TILE, 256), 1)
    start = 32 * i
    first = (lane >= start) & (lane < start + HDIM)
    second = (lane >= start + HDIM) & (lane < start + 2 * HDIM)
    return first, second


def stack_heads(window, masks):
    zero = jnp.zeros_like(window)
    return jnp.concatenate([jnp.where(m, window, zero) for m in masks], axis=0)


def rows_of_heads(both):
    return jnp.concatenate([both[:, :TILE], both[:, TILE:]], axis=0)


def halves(fn, *arrays):
    return jnp.concatenate(
        [fn(*(a[:, :TILE] for a in arrays)), fn(*(a[:, TILE:] for a in arrays))], axis=1
    )


def wide_max(a):
    return jnp.broadcast_to(jnp.max(a, axis=-1, keepdims=True), a.shape)


def wide_sum(a):
    return jnp.broadcast_to(jnp.sum(a, axis=-1, keepdims=True), a.shape)


CHUNKS = [pl.ds(0, 768), pl.ds(768, 768), pl.ds(1536, 384)]


def start(copies):
    for copy in copies:
        copy.start()


def wait(copies):
    for copy in copies:
        copy.wait()


def load_weight(pieces, weight, sems):
    return [
        [
            pltpu.make_async_copy(
                piece.at[:, cols],
                weight.at[pl.ds(PART * b, PART), cols],
                sems.at[n, b],
            )
            for b, piece in enumerate(pieces)
        ]
        for n, cols in enumerate(CHUNKS)
    ]


def load_rows(refs, rows, sems):
    return [
        pltpu.make_async_copy(ref, rows.at[pl.ds(ROWS * h, ROWS)], sems.at[h])
        for h, ref in enumerate(refs)
    ]


def load_features(refs, normed_t, sems):
    return [
        pltpu.make_async_copy(ref, normed_t.at[:, pl.ds(ROWS * h, ROWS)], sems.at[h])
        for h, ref in enumerate(refs)
    ]


def gradient(normed_t, dqkv, weight, outs, staged, gain_part, sems):
    copies = []
    for c, cols in enumerate(CHUNKS):
        for n in range(0, PIECES, 2):
            rows = slice(PART * n, PART * (n + 2))
            both = dot(normed_t[rows, :], dqkv[:, cols])
            product = both * weight[rows, cols].astype(F32)
            lanes = sum(
                product[:, TILE * k : TILE * (k + 1)] for k in range(cols.size // TILE)
            )
            gain_part[rows, :] = lanes if c == 0 else gain_part[rows, :] + lanes
            both = both.astype(BF)
            for k in (n, n + 1):
                staged[k, :, cols] = both[PART * (k - n) : PART * (k - n + 1)]
                copies.append(
                    pltpu.make_async_copy(
                        staged.at[k, :, cols],
                        outs[k].at[:, cols],
                        sems.at[c, k],
                    )
                )
                copies[-1].start()
    wait(copies)


def main_kernel(
    idx_ref,
    seg_ref,
    normed_ref,
    partner_ref,
    normed_t_ref,
    partner_t_ref,
    cot_ref,
    *refs,
):
    pieces, slots_ref, dqkv_ref = refs[:PIECES], refs[PIECES], refs[PIECES + 1]
    grads, gain_ref = refs[PIECES + 2 : 2 * PIECES + 2], refs[2 * PIECES + 2]
    (
        normed,
        qkv,
        cot,
        weight,
        normed_t,
        dqkv,
        out_tiles,
        staged,
        row_sems,
        cot_sems,
        w_sems,
        t_sems,
        slot_sems,
        dqkv_sems,
        grad_sems,
    ) = refs[2 * PIECES + 3 :]
    row_copies = load_rows((normed_ref, partner_ref), normed, row_sems)
    w_copies = load_weight(pieces, weight, w_sems)
    cot_copies = [
        pltpu.make_async_copy(cot_ref.at[j], cot.at[:, j], cot_sems.at[j])
        for j in range(N_DP)
    ]
    t_copies = load_features((normed_t_ref, partner_t_ref), normed_t, t_sems)
    start(row_copies)
    for copies in w_copies:
        start(copies)
    start(cot_copies)
    start(t_copies)
    wait(row_copies)
    for c, cols in enumerate(CHUNKS):
        wait(w_copies[c])
        qkv[:, cols] = dot(normed[...], weight[:, cols]).astype(BF)
    wait(cot_copies)

    def leave(t):
        rows = pl.ds(pl.multiple_of(t * TILE, TILE), TILE)
        return [
            pltpu.make_async_copy(
                out_tiles.at[t],
                slots_ref.at[idx_ref[t], idx_ref[2 * TILES + t]],
                slot_sems.at[t],
            ),
            pltpu.make_async_copy(dqkv.at[rows], dqkv_ref.at[rows], dqkv_sems.at[t]),
        ]

    @pl.loop(0, TILES)
    def _(step):
        pairs = range(8)
        tiles = [2 * step, 2 * step + 1]
        rows = [pl.ds(pl.multiple_of(t * TILE, TILE), TILE) for t in tiles]
        same = []
        for t in tiles:
            seg = jnp.broadcast_to(seg_ref[pl.ds(t, 1), :], (TILE, TILE))
            equal = seg == seg.T
            same.append(jnp.concatenate([equal, equal], axis=1))
        masks = [window_masks(i % 4) for i in pairs]
        windows = [slice(128 * (i % 4), 128 * (i % 4) + 256) for i in pairs]

        def window(a, i):
            first = HALF * a + 128 * (i % 4)
            return qkv[rows[i // 4], first : first + 256]

        q = [window(0, i) for i in pairs]
        d_out = [
            cot[tiles[i // 4], :, :, windows[i]].reshape(TILE, 256) for i in pairs
        ]
        kk = [stack_heads(window(1, i), masks[i]) for i in pairs]
        vv = [stack_heads(window(2, i), masks[i]) for i in pairs]
        scores = [dot(q[i], kk[i], NT) for i in pairs]
        d_probs = [dot(d_out[i], vv[i], NT) for i in pairs]
        scores = [
            jnp.where(same[i // 4], scores[i] * (SCALE * LOG2E), MASKED) for i in pairs
        ]
        tops = [halves(wide_max, x) for x in scores]
        expo = [jnp.exp2(x - m) for x, m in zip(scores, tops)]
        sums = [halves(wide_sum, x) for x in expo]
        weights = [x * (1.0 / total) for x, total in zip(expo, sums)]
        rounded = [x.astype(BF) for x in weights]
        outs = [dot(rounded[i], vv[i]) for i in pairs]
        dvs = [
            dot(rows_of_heads(rounded[i]), stack_heads(d_out[i], masks[i]), TN)
            for i in pairs
        ]
        inner = [halves(wide_sum, d_probs[i] * weights[i]) for i in pairs]
        d_scores = [
            (weights[i] * (d_probs[i] - inner[i]) * SCALE).astype(BF) for i in pairs
        ]
        dqs = [dot(d_scores[i], kk[i]) for i in pairs]
        dks = [
            dot(rows_of_heads(d_scores[i]), stack_heads(q[i], masks[i]), TN)
            for i in pairs
        ]

        def lanes(vals):
            parts = [vals[0][:, :TILE]]
            for i in range(3):
                parts.append(vals[i][:, TILE:] + vals[i + 1][:, :TILE])
            parts.append(vals[3][:, TILE:])
            return jnp.concatenate([p.astype(BF) for p in parts], axis=1)

        for n, t in enumerate(tiles):
            part = slice(4 * n, 4 * n + 4)
            out_tiles[t] = lanes(outs[part])
            for a, vals in enumerate((dqs, dks, dvs)):
                dqkv[rows[n], HALF * a : HALF * (a + 1)] = lanes(vals[part])
            start(leave(t))

    wait(t_copies)
    gradient(normed_t, dqkv, weight, grads, staged, gain_ref, grad_sems)
    for t in range(2 * TILES):
        wait(leave(t))


def main(index, seg, normed, normed_t, cot, pieces):
    return pl.pallas_call(
        main_kernel,
        in_specs=[SM, VM] + [ANY] * (5 + PIECES),
        out_specs=[ANY] * (2 + PIECES) + [VM],
        out_shape=[
            jax.ShapeDtypeStruct((N_DP, 2, TILE, HALF), BF),
            jax.ShapeDtypeStruct((PAIR_ROWS, COLS), BF),
        ]
        + [jax.ShapeDtypeStruct((PART, COLS), BF)] * PIECES
        + [jax.ShapeDtypeStruct((D, TILE), F32)],
        scratch_shapes=[
            pltpu.VMEM((PAIR_ROWS, D), BF),
            pltpu.VMEM((PAIR_ROWS, COLS), BF),
            pltpu.VMEM((2 * TILES, N_DP, STRIP, HALF), BF),
            pltpu.VMEM((D, COLS), BF),
            pltpu.VMEM((D, PAIR_ROWS), BF),
            pltpu.VMEM((PAIR_ROWS, COLS), BF),
            pltpu.VMEM((2 * TILES, TILE, HALF), BF),
            pltpu.VMEM((PIECES, PART, COLS), BF),
            pltpu.SemaphoreType.DMA((2,)),
            pltpu.SemaphoreType.DMA((N_DP,)),
            pltpu.SemaphoreType.DMA((len(CHUNKS), PIECES)),
            pltpu.SemaphoreType.DMA((2,)),
            pltpu.SemaphoreType.DMA((2 * TILES,)),
            pltpu.SemaphoreType.DMA((2 * TILES,)),
            pltpu.SemaphoreType.DMA((len(CHUNKS), PIECES)),
        ],
        compiler_params=params(58),
        cost_estimate=cost(8 * 10**9, 20 * 2**20, 10**6),
        name="main",
    )(index, seg, *normed, *normed_t, cot, *pieces)


def add_parts(counts, firsts, refs):
    totals, used = [], 0
    for count in counts:
        total = jnp.zeros((PART, COLS), F32)
        for k in range(used, used + count):
            total = total + refs[k][firsts[k] : firsts[k] + PART, :].astype(F32)
        used += count
        totals.append(total)
    return totals


def add_kernel(counts, firsts, *refs):
    totals = add_parts(counts, firsts, refs)
    for out_ref, total in zip(refs[sum(counts) :], totals):
        out_ref[...] = total.astype(BF)


def column_kernel(counts, firsts, gain_ref, other_ref, *refs):
    gain = gain_ref[...] + other_ref[...]
    outs = refs[sum(counts) :]
    totals = add_parts(counts, firsts, refs)
    for n, out_ref in enumerate(outs):
        block = totals[n // 2][BLOCK * (n % 2) : BLOCK * (n % 2 + 1)]
        out_ref[0:BLOCK, :] = block.astype(BF)
        put_gain(gain, out_ref, BLOCK, RIDE)


def put_gain(gain, ref, first, last):
    hi = gain.astype(BF).astype(F32)
    lo = gain - hi
    ref[first:last, :] = jnp.zeros((last - first, COLS), BF)
    for k in range(D // TILE):
        cols = slice(TILE * k, TILE * (k + 1))
        ref[first : first + 1, cols] = hi[k : k + 1].astype(BF)
        ref[first + 1 : first + 2, cols] = lo[k : k + 1].astype(BF)


def add(groups, gains=()):
    parts = [part for group in groups for part in group]
    rows, n = (RIDE, 2 * len(groups)) if gains else (PART, len(groups))
    return pl.pallas_call(
        functools.partial(
            column_kernel if gains else add_kernel,
            [len(group) for group in groups],
            [first for _, first in parts],
        ),
        in_specs=[VM] * (len(gains) + len(parts)),
        out_specs=[VM] * n,
        out_shape=[jax.ShapeDtypeStruct((rows, COLS), BF)] * n,
        compiler_params=params(12),
        cost_estimate=cost(0, 4 * len(parts) * PART * COLS),
        name="add",
    )(*gains, *[array for array, _ in parts])


def gain_kernel(part_ref, nat_ref, gain_ref, out_ref, perm_ref):
    build_order(nat_ref, perm_ref)
    rest = jnp.sum(part_ref[...], axis=1, keepdims=True)
    rest = jnp.broadcast_to(rest, (D, TILE))
    total = jnp.zeros((1, D), F32)
    for _ in range(3):
        term = rest.astype(BF)
        rest = rest - term.astype(F32)
        total = total + dot(term, perm_ref[...], TN)[0:1]
    total = total / gain_ref[...]
    out_ref[...] = jnp.zeros_like(out_ref)
    for k in range(D // TILE):
        out_ref[k : k + 1, :] = total[:, TILE * k : TILE * (k + 1)]


def gain_back(part, nat, gain):
    return pl.pallas_call(
        gain_kernel,
        in_specs=[VM] * 3,
        out_specs=VM,
        out_shape=jax.ShapeDtypeStruct((STRIP, TILE), F32),
        scratch_shapes=[pltpu.VMEM((D, D), BF)],
        compiler_params=params(24),
        cost_estimate=cost(0, 4 * D * TILE),
        name="gain",
    )(part, nat, gain)


def back_kernel(half, nat_ref, dqkv_ref, *refs):
    pieces, (out_ref, weight, perm_ref, dqkv, w_sems, q_sem) = (
        refs[:PIECES],
        refs[PIECES:],
    )
    w_copies = load_weight(pieces, weight, w_sems)
    q_copy = pltpu.make_async_copy(dqkv_ref.at[pl.ds(ROWS * half, ROWS)], dqkv, q_sem)
    q_copy.start()
    for copies in w_copies:
        start(copies)
    build_order(nat_ref, perm_ref)
    q_copy.wait()
    for copies in w_copies:
        wait(copies)
    d_normed = dot(dqkv[...], weight[...], NT).astype(BF)
    out_ref[...] = dot(d_normed, perm_ref[...]).astype(BF)


def back(half, dqkv, pieces, nat):
    return pl.pallas_call(
        functools.partial(back_kernel, half),
        in_specs=[VM] + [ANY] * (1 + PIECES),
        out_specs=VM,
        out_shape=jax.ShapeDtypeStruct((ROWS, D), BF),
        scratch_shapes=[
            pltpu.VMEM((D, COLS), BF),
            pltpu.VMEM((D, D), BF),
            pltpu.VMEM((ROWS, COLS), BF),
            pltpu.SemaphoreType.DMA((len(CHUNKS), PIECES)),
            pltpu.SemaphoreType.DMA,
        ],
        compiler_params=params(58),
        cost_estimate=cost(2 * ROWS * D * (D + COLS), 15 * 2**20),
        name="back",
    )(nat, dqkv, *pieces)


def rows_kernel(patches_ref, gain_ref, mine_ref, other_ref, out_ref):
    standard, inv_std = norm_rows(patches_ref[...])
    d_normed = mine_ref[...].astype(F32) + other_ref[...].astype(F32)
    scaled = d_normed * gain_ref[...]
    back_rows = inv_std * (
        scaled
        - jnp.mean(scaled, axis=-1, keepdims=True)
        - standard * jnp.mean(scaled * standard, axis=-1, keepdims=True)
    )
    out_ref[...] = back_rows.astype(BF)


def rows_back(patches, gain, mine, other):
    block = pl.BlockSpec((TILE, D), lambda i: (i, 0))
    return pl.pallas_call(
        rows_kernel,
        grid=(TILES,),
        in_specs=[block, pl.BlockSpec((1, D), lambda i: (0, 0)), block, block],
        out_specs=block,
        out_shape=jax.ShapeDtypeStruct((ROWS, D), BF),
        compiler_params=params(58),
        cost_estimate=cost(20 * ROWS * D, 8 * ROWS * D),
        name="rows_back",
    )(patches, gain, mine, other)


def split_kernel(rows_ref, one_ref, two_ref, three_ref, out_ref):
    total = rows_ref[...].astype(F32)
    for ref in (one_ref, two_ref, three_ref):
        total = total + ref[...].astype(F32)
    gain = total[BLOCK : BLOCK + 1, :D] + total[BLOCK + 1 : BLOCK + 2, :D]
    gain = gain.astype(BF)
    total = total.astype(BF)
    extras = OWN * LANES
    for s in range(N_DP):
        for k in range(LANES):
            out_ref[s, OWN * k : OWN * (k + 1), :] = total[
                OWN * s : OWN * (s + 1), TILE * k : TILE * (k + 1)
            ]
        for k in range(D // TILE):
            out_ref[s, extras + k : extras + k + 1, :] = gain[
                :, TILE * k : TILE * (k + 1)
            ]


def split(rows, others):
    return pl.pallas_call(
        split_kernel,
        in_specs=[VM] * 4,
        out_specs=VM,
        out_shape=jax.ShapeDtypeStruct((N_DP, MSG, TILE), BF),
        compiler_params=params(12),
        cost_estimate=cost(0, 4 * N_DP * MSG * TILE),
        name="split",
    )(rows, *others)


def finish_kernel(msg_ref, out_ref, gain_ref):
    both = jnp.zeros((MSG, TILE), F32)
    for half in range(2):
        total = msg_ref[half].astype(F32)
        for chip in range(1, 4):
            total = total + msg_ref[2 * chip + half].astype(F32)
        both = both + total
        for k in range(LANES):
            first = D * (k // 5) + HALF * half + TILE * (k % 5)
            out_ref[:, first : first + TILE] = total[OWN * k : OWN * (k + 1)]
    gain_ref[...] = both[OWN * LANES : MSG]


def finish(messages):
    return pl.pallas_call(
        finish_kernel,
        in_specs=[VM],
        out_specs=[VM, VM],
        out_shape=[
            jax.ShapeDtypeStruct((OWN, 3 * D), F32),
            jax.ShapeDtypeStruct((D // TILE, TILE), F32),
        ],
        compiler_params=params(12),
        cost_estimate=cost(0, 6 * N_DP * MSG * TILE),
        name="finish",
    )(messages)


def ring_pairs(df, ds):
    pairs = []
    for d in range(N_DP):
        dx, dz = (ds, df) if d % 2 else (df, ds)
        for x in range(4):
            for z in range(4):
                src = 4 * ((x + dx) % 4) + (z + dz) % 4
                pairs.append((N_INNER * d + src, N_INNER * d + 4 * x + z))
    return pairs


def double_pairs(f_bits, s_bits):
    pairs = []
    for d in range(N_DP):
        x_bits, z_bits = (s_bits, f_bits) if d % 2 else (f_bits, s_bits)
        flip = 4 * x_bits + z_bits
        pairs += [(N_INNER * d + (m ^ flip), N_INNER * d + m) for m in range(N_INNER)]
    return pairs


def from_ring(value, df, ds):
    return lax.ppermute(value, ("dp", "inner"), ring_pairs(df, ds))


def swap_cores(value):
    return lax.ppermute(value, "dp", [(d ^ 1, d) for d in range(N_DP)])


def exchange(value, axis="dp"):
    return lax.all_to_all(value, axis, split_axis=0, concat_axis=0, tiled=True)


def on_device(patches, segments, owners, norm_gain, qkv_weight, cotangent):
    group = lax.axis_index("dp")
    inner = lax.axis_index("inner")
    core, x, z = group % 2, inner // 4, inner % 4
    gain = norm_gain.reshape(1, D)

    pos = jnp.arange(N_INNER)
    df, ds = pos % 4, pos // 4
    m = 4 * ((x + jnp.where(core == 0, df, ds)) % 4) + (
        z + jnp.where(core == 0, ds, df)
    ) % 4
    nat = (
        (jnp.arange(N_DP)[None, :, None] * N_INNER + m[:, None, None]) * OWN
        + jnp.arange(OWN)[None, None, :]
    ).reshape(1, D).astype(F32)

    messages = exchange(build(owners, qkv_weight, segments))
    partner_patches = swap_cores(patches)
    strips = cotangent.reshape(TILES, N_DP, STRIP, D).transpose(1, 0, 2, 3)
    messages, strips = lax.optimization_barrier((messages, strips))
    block, seg, owners_all = compact(group.reshape(1).astype(jnp.int32), messages)
    strips = exchange(strips)

    owner_of = owners_all[:, :TILES].astype(jnp.int32).reshape(N_DP * TILES)
    u = jnp.arange(N_DP * TILES)
    earlier = (owner_of[:, None] == owner_of[None, :]) & (
        u[None, :] // TILES < u[:, None] // TILES
    )
    fwd = (TILES * owner_of + jnp.sum(earlier, axis=1)).astype(jnp.int32)
    wanted = fwd[None, :] == TILES * group + jnp.arange(TILES)[:, None]
    source = jnp.sum(jnp.where(wanted, u[None, :] // TILES, 0), axis=1)
    place_index = jnp.concatenate([2 * (source // 2), source % 2]).astype(jnp.int32)
    mine = jnp.arange(2)[:, None] ^ core
    tile = (TILES * (group - core + mine) + jnp.arange(TILES)[None, :]).reshape(-1)
    owner_here = jnp.sum(jnp.where(tile[:, None] == u[None, :], owner_of, 0), axis=1)
    slot_index = jnp.concatenate(
        [owner_here, jnp.broadcast_to(mine, (2, TILES)).reshape(-1)]
    ).astype(jnp.int32)

    ring = [block] + [from_ring(block, f, 0) for f in (1, 2, 3)]
    near_a, near_b = jnp.concatenate(ring[:2]), jnp.concatenate(ring[2:])
    later_patches, near_b = lax.optimization_barrier((patches, near_b))
    own_prep = prep(later_patches, gain, nat)
    strips, own_prep = lax.optimization_barrier((strips, own_prep))

    heads = to_heads(fwd, strips.reshape(N_DP * TILES, STRIP, D))
    cot = exchange(heads)

    above_a, below_b = from_ring(near_a, 0, 1), from_ring(near_b, 0, -1)
    above_b, below_a = from_ring(near_b, 0, 1), from_ring(near_a, 0, -1)
    above_a, above_b, below_a, below_b = lax.optimization_barrier(
        (above_a, above_b, below_a, below_b)
    )
    far_a, far_b = from_ring(above_a, 0, 1), from_ring(below_b, 0, -1)
    pieces = [near_a, near_b, above_a, above_b, far_a, far_b, below_a, below_b]
    normed, normed_t = zip(own_prep, prep(partner_patches, gain, nat))

    out, dqkv, *parts, gain_part = main(slot_index, seg, normed, normed_t, cot, pieces)
    col_a, col_b, up_a, up_b, far_up, far_down, down_a, down_b = parts

    far_up, far_down = from_ring(far_up, 0, -1), from_ring(far_down, 0, 1)
    up_b, down_a = from_ring(up_b, 0, -1), from_ring(down_a, 0, 1)
    slots = exchange(out)
    gain_part = gain_back(gain_part, nat, gain)
    far_up, far_down, gain_part = lax.optimization_barrier((far_up, far_down, gain_part))
    up_a, down_b = add([[(up_a, 0), (far_up, 0)], [(down_b, 0), (far_down, 0)]])
    gain_other = lax.ppermute(gain_part, ("dp", "inner"), double_pairs(0, 1))
    from_up_a, from_down_b = from_ring(up_a, 0, -1), from_ring(down_b, 0, 1)
    dqkv, up_b, down_a = lax.optimization_barrier((dqkv, up_b, down_a))
    partners = back(1, dqkv, pieces, nat)
    gain_part = gain_part + gain_other
    gain_other = lax.ppermute(gain_part, ("dp", "inner"), double_pairs(0, 3))
    from_up_a, from_down_b, partners = lax.optimization_barrier(
        (from_up_a, from_down_b, partners)
    )
    other = swap_cores(partners)
    zero, one, two, three = add(
        [
            [(col_a, 0), (from_up_a, 0), (down_a, 0)],
            [(col_b, 0), (up_b, 0), (from_down_b, 0)],
        ],
        (gain_part, gain_other),
    )
    dqkv, _ = lax.optimization_barrier((dqkv, zero))
    mine = back(0, dqkv, pieces, nat)
    others = [from_ring(two, -2, 0), from_ring(three, 1, 0), from_ring(one, -1, 0)]
    others[0], slots, mine = lax.optimization_barrier((others[0], slots, mine))

    attended = place(place_index, slots).reshape(ROWS, D)
    grad_rows = rows_back(patches, gain, mine, other)
    grad_qkv, grad_gain = finish(exchange(split(zero, others)))
    return (attended, grad_rows, grad_qkv, grad_gain.reshape(D))


def solution(mesh):
    both = ("dp", "inner")
    placed = (
        P(both, None),
        P(both, None),
        P(both),
        P(),
        P(both, None),
        P(both, None),
    )
    return jax.shard_map(
        on_device,
        mesh=mesh,
        in_specs=placed,
        out_specs=(P(both, None), P(both, None), P(both, None), P()),
        check_vma=False,
    )
```

```python
import functools

import jax
import jax.numpy as jnp
from jax import lax
from jax.experimental import pallas as pl
from jax.experimental.pallas import tpu as pltpu
from jax.sharding import PartitionSpec as P

D = 1280
HEADS = 16
HDIM = 80
TILE = 128
TILES = 3
N_DP = 8
N_INNER = 16
ROWS = TILES * TILE
PAIR_ROWS = 2 * ROWS
HALF = D // 2
COLS = 3 * HALF
OWN = 10
BLOCK = 80
PART = 160
PIECES = 8
RIDE = 88
STRIP = 16
MSG = 160
LANES = COLS // TILE
EPS = 1e-6
MASKED = -1e30
SCALE = HDIM ** (-0.5)
LOG2E = 1.4426950408889634
BF = jnp.bfloat16
F32 = jnp.float32
VM = pl.BlockSpec(memory_space=pltpu.VMEM)
SM = pl.BlockSpec(memory_space=pltpu.SMEM)
ANY = pl.BlockSpec(memory_space=pltpu.HBM)
NT = (((1,), (1,)), ((), ()))
TN = (((0,), (0,)), ((), ()))
NN = (((1,), (0,)), ((), ()))


def params(mib, **more):
    return pltpu.CompilerParams(vmem_limit_bytes=mib * 2**20, **more)


def cost(flops, nbytes, trans=0):
    return pl.CostEstimate(
        flops=flops // 1000, bytes_accessed=nbytes // 1000, transcendentals=trans // 1000
    )


def dot(a, b, dims=NN):
    return lax.dot_general(a, b, dims, preferred_element_type=F32)


def norm_rows(rows):
    wide = rows.astype(F32)
    centred = wide - jnp.mean(wide, axis=-1, keepdims=True)
    variance = jnp.mean(centred * centred, axis=-1, keepdims=True)
    inv_std = lax.rsqrt(variance + EPS)
    return centred * inv_std, inv_std


def build_order(nat_ref, perm_ref):
    for r in range(D // TILE):
        rows = slice(TILE * r, TILE * (r + 1))
        column = jnp.broadcast_to(nat_ref[:, rows], (TILE, TILE)).T
        for a in range(D // TILE):
            feature = lax.broadcasted_iota(jnp.int32, (TILE, TILE), 1) + TILE * a
            hit = column == feature.astype(F32)
            perm_ref[rows, TILE * a : TILE * (a + 1)] = jnp.where(hit, 1.0, 0.0).astype(BF)


def prep_kernel(patches_ref, gain_ref, nat_ref, normed_ref, normed_t_ref, perm_ref):
    build_order(nat_ref, perm_ref)
    standard, _ = norm_rows(patches_ref[...])
    normed = (standard * gain_ref[...]).astype(BF)
    normed_ref[...] = dot(normed, perm_ref[...], NT).astype(BF)
    normed_t_ref[...] = dot(perm_ref[...], normed, NT).astype(BF)


def prep(patches, gain, nat):
    return pl.pallas_call(
        prep_kernel,
        in_specs=[VM] * 3,
        out_specs=[VM] * 2,
        out_shape=[
            jax.ShapeDtypeStruct((ROWS, D), BF),
            jax.ShapeDtypeStruct((D, ROWS), BF),
        ],
        scratch_shapes=[pltpu.VMEM((D, D), BF)],
        compiler_params=params(58),
        cost_estimate=cost(4 * ROWS * D * D, 6 * ROWS * D),
        name="prep",
    )(patches, gain, nat)


def build_kernel(own_ref, w_ref, seg_ref, out_ref):
    lane = lax.broadcasted_iota(jnp.int32, (1, TILE), 1)
    owners = jnp.zeros((1, TILE), jnp.int32)
    for t in range(TILES):
        owners = jnp.where(lane == t, own_ref[t], owners)
    for half in range(2):
        for k in range(LANES):
            first = D * (k // 5) + HALF * half + TILE * (k % 5)
            out_ref[half, OWN * k : OWN * (k + 1), :] = w_ref[:, first : first + TILE]
        extras = OWN * LANES
        out_ref[half, extras:MSG, :] = jnp.zeros((MSG - extras, TILE), BF)
        out_ref[half, extras : extras + 1, :] = owners.astype(F32).astype(BF)
        out_ref[half, extras + 1 : extras + 1 + TILES, :] = (
            seg_ref[...].astype(F32).astype(BF)
        )
    for d in range(2, N_DP):
        out_ref[d] = out_ref[d % 2]


def build(owners, weight, segments):
    return pl.pallas_call(
        build_kernel,
        in_specs=[SM, VM, VM],
        out_specs=VM,
        out_shape=jax.ShapeDtypeStruct((N_DP, MSG, TILE), BF),
        compiler_params=params(58),
        cost_estimate=cost(0, 2 * N_DP * MSG * TILE),
        name="build",
    )(owners, weight, segments)


def compact_kernel(group_ref, msg_ref, w_ref, seg_ref, own_ref):
    group = group_ref[0]
    extras = OWN * LANES
    seg_ref[...] = jnp.zeros_like(seg_ref)
    for s in range(N_DP):
        for k in range(LANES):
            w_ref[OWN * s : OWN * (s + 1), TILE * k : TILE * (k + 1)] = msg_ref[
                s, OWN * k : OWN * (k + 1), :
            ]
        own_ref[s : s + 1, :] = msg_ref[s, extras : extras + 1, :].astype(F32)
    for rel in range(2):
        src = group + rel * (1 - 2 * (group % 2))
        seg_ref[TILES * rel : TILES * (rel + 1), :] = msg_ref[
            src, extras + 1 : extras + 1 + TILES, :
        ].astype(F32)


def compact(group, messages):
    return pl.pallas_call(
        compact_kernel,
        in_specs=[SM, VM],
        out_specs=[VM] * 3,
        out_shape=[
            jax.ShapeDtypeStruct((BLOCK, COLS), BF),
            jax.ShapeDtypeStruct((8, TILE), F32),
            jax.ShapeDtypeStruct((N_DP, TILE), F32),
        ],
        compiler_params=params(12),
        cost_estimate=cost(0, 4 * N_DP * MSG * TILE),
        name="compact",
    )(group, messages)


def to_heads_kernel(fwd_ref, in_ref, out_ref):
    for d in range(N_DP):
        half = slice(HALF * (d % 2), HALF * (d % 2 + 1))
        for k in range(2 * TILES):
            u = TILES * (2 * (d // 2) + ((d % 2) ^ (k // TILES))) + k % TILES
            out_ref[d, k] = in_ref[fwd_ref[u], :, half]


def to_heads(fwd, strips):
    return pl.pallas_call(
        to_heads_kernel,
        in_specs=[SM, VM],
        out_specs=VM,
        out_shape=jax.ShapeDtypeStruct((N_DP, 2 * TILES, STRIP, HALF), BF),
        cost_estimate=cost(0, 4 * ROWS * D),
        compiler_params=params(12),
        name="to_heads",
    )(fwd, strips)


def place_kernel(idx_ref, left_ref, right_ref, out_ref):
    out_ref[0, :, :HALF] = left_ref[0, 0]
    out_ref[0, :, HALF:] = right_ref[0, 0]


def place(index, slots):
    def half(c):
        return pl.BlockSpec(
            (1, 1, TILE, HALF), lambda p, g: (g[p] + c, g[TILES + p], 0, 0)
        )

    spec = pltpu.PrefetchScalarGridSpec(
        num_scalar_prefetch=1,
        grid=(TILES,),
        in_specs=[half(0), half(1)],
        out_specs=pl.BlockSpec((1, TILE, D), lambda p, g: (p, 0, 0)),
    )
    return pl.pallas_call(
        place_kernel,
        grid_spec=spec,
        out_shape=jax.ShapeDtypeStruct((TILES, TILE, D), BF),
        compiler_params=params(12),
        cost_estimate=cost(0, 4 * ROWS * D),
        name="place",
    )(index, slots, slots)


def window_masks(i):
    lane = lax.broadcasted_iota(jnp.int32, (TILE, 256), 1)
    start = 32 * i
    first = (lane >= start) & (lane < start + HDIM)
    second = (lane >= start + HDIM) & (lane < start + 2 * HDIM)
    return first, second


def stack_heads(window, masks):
    zero = jnp.zeros_like(window)
    return jnp.concatenate([jnp.where(m, window, zero) for m in masks], axis=0)


def rows_of_heads(both):
    return jnp.concatenate([both[:, :TILE], both[:, TILE:]], axis=0)


def halves(fn, *arrays):
    return jnp.concatenate(
        [fn(*(a[:, :TILE] for a in arrays)), fn(*(a[:, TILE:] for a in arrays))], axis=1
    )


def wide_max(a):
    return jnp.broadcast_to(jnp.max(a, axis=-1, keepdims=True), a.shape)


def wide_sum(a):
    return jnp.broadcast_to(jnp.sum(a, axis=-1, keepdims=True), a.shape)


CHUNKS = [pl.ds(0, 768), pl.ds(768, 768), pl.ds(1536, 384)]


def start(copies):
    for copy in copies:
        copy.start()


def wait(copies):
    for copy in copies:
        copy.wait()


def load_weight(pieces, weight, sems):
    return [
        [
            pltpu.make_async_copy(
                piece.at[:, cols],
                weight.at[pl.ds(PART * b, PART), cols],
                sems.at[n, b],
            )
            for b, piece in enumerate(pieces)
        ]
        for n, cols in enumerate(CHUNKS)
    ]


def load_rows(refs, rows, sems):
    return [
        pltpu.make_async_copy(ref, rows.at[pl.ds(ROWS * h, ROWS)], sems.at[h])
        for h, ref in enumerate(refs)
    ]


def load_features(refs, normed_t, sems):
    return [
        pltpu.make_async_copy(ref, normed_t.at[:, pl.ds(ROWS * h, ROWS)], sems.at[h])
        for h, ref in enumerate(refs)
    ]


def gradient(normed_t, dqkv, weight, outs, staged, gain_part, sems):
    copies = []
    for c, cols in enumerate(CHUNKS):
        for n in range(0, PIECES, 2):
            rows = slice(PART * n, PART * (n + 2))
            both = dot(normed_t[rows, :], dqkv[:, cols])
            product = both * weight[rows, cols].astype(F32)
            lanes = sum(
                product[:, TILE * k : TILE * (k + 1)] for k in range(cols.size // TILE)
            )
            gain_part[rows, :] = lanes if c == 0 else gain_part[rows, :] + lanes
            both = both.astype(BF)
            for k in (n, n + 1):
                staged[k, :, cols] = both[PART * (k - n) : PART * (k - n + 1)]
                copies.append(
                    pltpu.make_async_copy(
                        staged.at[k, :, cols],
                        outs[k].at[:, cols],
                        sems.at[c, k],
                    )
                )
                copies[-1].start()
    wait(copies)


def main_kernel(
    idx_ref,
    seg_ref,
    normed_ref,
    partner_ref,
    normed_t_ref,
    partner_t_ref,
    cot_ref,
    *refs,
):
    pieces, slots_ref, dqkv_ref = refs[:PIECES], refs[PIECES], refs[PIECES + 1]
    grads, gain_ref = refs[PIECES + 2 : 2 * PIECES + 2], refs[2 * PIECES + 2]
    (
        normed,
        qkv,
        cot,
        weight,
        normed_t,
        dqkv,
        out_tiles,
        staged,
        row_sems,
        cot_sems,
        w_sems,
        t_sems,
        slot_sems,
        dqkv_sems,
        grad_sems,
    ) = refs[2 * PIECES + 3 :]
    row_copies = load_rows((normed_ref, partner_ref), normed, row_sems)
    w_copies = load_weight(pieces, weight, w_sems)
    cot_copies = [
        pltpu.make_async_copy(cot_ref.at[j], cot.at[:, j], cot_sems.at[j])
        for j in range(N_DP)
    ]
    t_copies = load_features((normed_t_ref, partner_t_ref), normed_t, t_sems)
    start(row_copies)
    for copies in w_copies:
        start(copies)
    start(cot_copies)
    start(t_copies)
    wait(row_copies)
    for c, cols in enumerate(CHUNKS):
        wait(w_copies[c])
        qkv[:, cols] = dot(normed[...], weight[:, cols]).astype(BF)
    wait(cot_copies)

    def leave(t):
        rows = pl.ds(pl.multiple_of(t * TILE, TILE), TILE)
        return [
            pltpu.make_async_copy(
                out_tiles.at[t],
                slots_ref.at[idx_ref[t], idx_ref[2 * TILES + t]],
                slot_sems.at[t],
            ),
            pltpu.make_async_copy(dqkv.at[rows], dqkv_ref.at[rows], dqkv_sems.at[t]),
        ]

    @pl.loop(0, TILES)
    def _(step):
        pairs = range(8)
        tiles = [2 * step, 2 * step + 1]
        rows = [pl.ds(pl.multiple_of(t * TILE, TILE), TILE) for t in tiles]
        same = []
        for t in tiles:
            seg = jnp.broadcast_to(seg_ref[pl.ds(t, 1), :], (TILE, TILE))
            equal = seg == seg.T
            same.append(jnp.concatenate([equal, equal], axis=1))
        masks = [window_masks(i % 4) for i in pairs]
        windows = [slice(128 * (i % 4), 128 * (i % 4) + 256) for i in pairs]

        def window(a, i):
            first = HALF * a + 128 * (i % 4)
            return qkv[rows[i // 4], first : first + 256]

        q = [window(0, i) for i in pairs]
        d_out = [
            cot[tiles[i // 4], :, :, windows[i]].reshape(TILE, 256) for i in pairs
        ]
        kk = [stack_heads(window(1, i), masks[i]) for i in pairs]
        vv = [stack_heads(window(2, i), masks[i]) for i in pairs]
        scores = [dot(q[i], kk[i], NT) for i in pairs]
        d_probs = [dot(d_out[i], vv[i], NT) for i in pairs]
        scores = [
            jnp.where(same[i // 4], scores[i] * (SCALE * LOG2E), MASKED) for i in pairs
        ]
        tops = [halves(wide_max, x) for x in scores]
        expo = [jnp.exp2(x - m) for x, m in zip(scores, tops)]
        sums = [halves(wide_sum, x) for x in expo]
        weights = [x * (1.0 / total) for x, total in zip(expo, sums)]
        rounded = [x.astype(BF) for x in weights]
        outs = [dot(rounded[i], vv[i]) for i in pairs]
        dvs = [
            dot(rows_of_heads(rounded[i]), stack_heads(d_out[i], masks[i]), TN)
            for i in pairs
        ]
        inner = [halves(wide_sum, d_probs[i] * weights[i]) for i in pairs]
        d_scores = [
            (weights[i] * (d_probs[i] - inner[i]) * SCALE).astype(BF) for i in pairs
        ]
        dqs = [dot(d_scores[i], kk[i]) for i in pairs]
        dks = [
            dot(rows_of_heads(d_scores[i]), stack_heads(q[i], masks[i]), TN)
            for i in pairs
        ]

        def lanes(vals):
            parts = [vals[0][:, :TILE]]
            for i in range(3):
                parts.append(vals[i][:, TILE:] + vals[i + 1][:, :TILE])
            parts.append(vals[3][:, TILE:])
            return jnp.concatenate([p.astype(BF) for p in parts], axis=1)

        for n, t in enumerate(tiles):
            part = slice(4 * n, 4 * n + 4)
            out_tiles[t] = lanes(outs[part])
            for a, vals in enumerate((dqs, dks, dvs)):
                dqkv[rows[n], HALF * a : HALF * (a + 1)] = lanes(vals[part])
            start(leave(t))

    wait(t_copies)
    gradient(normed_t, dqkv, weight, grads, staged, gain_ref, grad_sems)
    for t in range(2 * TILES):
        wait(leave(t))


def main(index, seg, normed, normed_t, cot, pieces):
    return pl.pallas_call(
        main_kernel,
        in_specs=[SM, VM] + [ANY] * (5 + PIECES),
        out_specs=[ANY] * (2 + PIECES) + [VM],
        out_shape=[
            jax.ShapeDtypeStruct((N_DP, 2, TILE, HALF), BF),
            jax.ShapeDtypeStruct((PAIR_ROWS, COLS), BF),
        ]
        + [jax.ShapeDtypeStruct((PART, COLS), BF)] * PIECES
        + [jax.ShapeDtypeStruct((D, TILE), F32)],
        scratch_shapes=[
            pltpu.VMEM((PAIR_ROWS, D), BF),
            pltpu.VMEM((PAIR_ROWS, COLS), BF),
            pltpu.VMEM((2 * TILES, N_DP, STRIP, HALF), BF),
            pltpu.VMEM((D, COLS), BF),
            pltpu.VMEM((D, PAIR_ROWS), BF),
            pltpu.VMEM((PAIR_ROWS, COLS), BF),
            pltpu.VMEM((2 * TILES, TILE, HALF), BF),
            pltpu.VMEM((PIECES, PART, COLS), BF),
            pltpu.SemaphoreType.DMA((2,)),
            pltpu.SemaphoreType.DMA((N_DP,)),
            pltpu.SemaphoreType.DMA((len(CHUNKS), PIECES)),
            pltpu.SemaphoreType.DMA((2,)),
            pltpu.SemaphoreType.DMA((2 * TILES,)),
            pltpu.SemaphoreType.DMA((2 * TILES,)),
            pltpu.SemaphoreType.DMA((len(CHUNKS), PIECES)),
        ],
        compiler_params=params(58),
        cost_estimate=cost(8 * 10**9, 20 * 2**20, 10**6),
        name="main",
    )(index, seg, *normed, *normed_t, cot, *pieces)


def add_parts(counts, firsts, refs):
    totals, used = [], 0
    for count in counts:
        total = jnp.zeros((PART, COLS), F32)
        for k in range(used, used + count):
            total = total + refs[k][firsts[k] : firsts[k] + PART, :].astype(F32)
        used += count
        totals.append(total)
    return totals


def add_kernel(counts, firsts, *refs):
    totals = add_parts(counts, firsts, refs)
    for out_ref, total in zip(refs[sum(counts) :], totals):
        out_ref[...] = total.astype(BF)


def column_kernel(counts, firsts, gain_ref, other_ref, *refs):
    gain = gain_ref[...] + other_ref[...]
    outs = refs[sum(counts) :]
    totals = add_parts(counts, firsts, refs)
    for n, out_ref in enumerate(outs):
        block = totals[n // 2][BLOCK * (n % 2) : BLOCK * (n % 2 + 1)]
        out_ref[0:BLOCK, :] = block.astype(BF)
        put_gain(gain, out_ref, BLOCK, RIDE)


def put_gain(gain, ref, first, last):
    hi = gain.astype(BF).astype(F32)
    lo = gain - hi
    ref[first:last, :] = jnp.zeros((last - first, COLS), BF)
    for k in range(D // TILE):
        cols = slice(TILE * k, TILE * (k + 1))
        ref[first : first + 1, cols] = hi[k : k + 1].astype(BF)
        ref[first + 1 : first + 2, cols] = lo[k : k + 1].astype(BF)


def add(groups, gains=()):
    parts = [part for group in groups for part in group]
    rows, n = (RIDE, 2 * len(groups)) if gains else (PART, len(groups))
    return pl.pallas_call(
        functools.partial(
            column_kernel if gains else add_kernel,
            [len(group) for group in groups],
            [first for _, first in parts],
        ),
        in_specs=[VM] * (len(gains) + len(parts)),
        out_specs=[VM] * n,
        out_shape=[jax.ShapeDtypeStruct((rows, COLS), BF)] * n,
        compiler_params=params(12),
        cost_estimate=cost(0, 4 * len(parts) * PART * COLS),
        name="add",
    )(*gains, *[array for array, _ in parts])


def gain_kernel(part_ref, nat_ref, gain_ref, out_ref, perm_ref):
    build_order(nat_ref, perm_ref)
    rest = jnp.sum(part_ref[...], axis=1, keepdims=True)
    rest = jnp.broadcast_to(rest, (D, TILE))
    total = jnp.zeros((1, D), F32)
    for _ in range(3):
        term = rest.astype(BF)
        rest = rest - term.astype(F32)
        total = total + dot(term, perm_ref[...], TN)[0:1]
    total = total / gain_ref[...]
    out_ref[...] = jnp.zeros_like(out_ref)
    for k in range(D // TILE):
        out_ref[k : k + 1, :] = total[:, TILE * k : TILE * (k + 1)]


def gain_back(part, nat, gain):
    return pl.pallas_call(
        gain_kernel,
        in_specs=[VM] * 3,
        out_specs=VM,
        out_shape=jax.ShapeDtypeStruct((STRIP, TILE), F32),
        scratch_shapes=[pltpu.VMEM((D, D), BF)],
        compiler_params=params(24),
        cost_estimate=cost(0, 4 * D * TILE),
        name="gain",
    )(part, nat, gain)


def back_kernel(half, nat_ref, dqkv_ref, *refs):
    pieces, (out_ref, weight, perm_ref, dqkv, w_sems, q_sem) = (
        refs[:PIECES],
        refs[PIECES:],
    )
    w_copies = load_weight(pieces, weight, w_sems)
    q_copy = pltpu.make_async_copy(dqkv_ref.at[pl.ds(ROWS * half, ROWS)], dqkv, q_sem)
    q_copy.start()
    for copies in w_copies:
        start(copies)
    build_order(nat_ref, perm_ref)
    q_copy.wait()
    for copies in w_copies:
        wait(copies)
    d_normed = dot(dqkv[...], weight[...], NT).astype(BF)
    out_ref[...] = dot(d_normed, perm_ref[...]).astype(BF)


def back(half, dqkv, pieces, nat):
    return pl.pallas_call(
        functools.partial(back_kernel, half),
        in_specs=[VM] + [ANY] * (1 + PIECES),
        out_specs=VM,
        out_shape=jax.ShapeDtypeStruct((ROWS, D), BF),
        scratch_shapes=[
            pltpu.VMEM((D, COLS), BF),
            pltpu.VMEM((D, D), BF),
            pltpu.VMEM((ROWS, COLS), BF),
            pltpu.SemaphoreType.DMA((len(CHUNKS), PIECES)),
            pltpu.SemaphoreType.DMA,
        ],
        compiler_params=params(58),
        cost_estimate=cost(2 * ROWS * D * (D + COLS), 15 * 2**20),
        name="back",
    )(nat, dqkv, *pieces)


def rows_kernel(patches_ref, gain_ref, mine_ref, other_ref, out_ref):
    standard, inv_std = norm_rows(patches_ref[...])
    d_normed = mine_ref[...].astype(F32) + other_ref[...].astype(F32)
    scaled = d_normed * gain_ref[...]
    back_rows = inv_std * (
        scaled
        - jnp.mean(scaled, axis=-1, keepdims=True)
        - standard * jnp.mean(scaled * standard, axis=-1, keepdims=True)
    )
    out_ref[...] = back_rows.astype(BF)


def rows_back(patches, gain, mine, other):
    block = pl.BlockSpec((TILE, D), lambda i: (i, 0))
    return pl.pallas_call(
        rows_kernel,
        grid=(TILES,),
        in_specs=[block, pl.BlockSpec((1, D), lambda i: (0, 0)), block, block],
        out_specs=block,
        out_shape=jax.ShapeDtypeStruct((ROWS, D), BF),
        compiler_params=params(58),
        cost_estimate=cost(20 * ROWS * D, 8 * ROWS * D),
        name="rows_back",
    )(patches, gain, mine, other)


def split_kernel(rows_ref, one_ref, two_ref, three_ref, out_ref):
    total = rows_ref[...].astype(F32)
    for ref in (one_ref, two_ref, three_ref):
        total = total + ref[...].astype(F32)
    gain = total[BLOCK : BLOCK + 1, :D] + total[BLOCK + 1 : BLOCK + 2, :D]
    gain = gain.astype(BF)
    total = total.astype(BF)
    extras = OWN * LANES
    for s in range(N_DP):
        for k in range(LANES):
            out_ref[s, OWN * k : OWN * (k + 1), :] = total[
                OWN * s : OWN * (s + 1), TILE * k : TILE * (k + 1)
            ]
        for k in range(D // TILE):
            out_ref[s, extras + k : extras + k + 1, :] = gain[
                :, TILE * k : TILE * (k + 1)
            ]


def split(rows, others):
    return pl.pallas_call(
        split_kernel,
        in_specs=[VM] * 4,
        out_specs=VM,
        out_shape=jax.ShapeDtypeStruct((N_DP, MSG, TILE), BF),
        compiler_params=params(12),
        cost_estimate=cost(0, 4 * N_DP * MSG * TILE),
        name="split",
    )(rows, *others)


def finish_kernel(msg_ref, out_ref, gain_ref):
    both = jnp.zeros((MSG, TILE), F32)
    for half in range(2):
        total = msg_ref[half].astype(F32)
        for chip in range(1, 4):
            total = total + msg_ref[2 * chip + half].astype(F32)
        both = both + total
        for k in range(LANES):
            first = D * (k // 5) + HALF * half + TILE * (k % 5)
            out_ref[:, first : first + TILE] = total[OWN * k : OWN * (k + 1)]
    gain_ref[...] = both[OWN * LANES : MSG]


def finish(messages):
    return pl.pallas_call(
        finish_kernel,
        in_specs=[VM],
        out_specs=[VM, VM],
        out_shape=[
            jax.ShapeDtypeStruct((OWN, 3 * D), F32),
            jax.ShapeDtypeStruct((D // TILE, TILE), F32),
        ],
        compiler_params=params(12),
        cost_estimate=cost(0, 6 * N_DP * MSG * TILE),
        name="finish",
    )(messages)


def ring_pairs(df, ds):
    pairs = []
    for d in range(N_DP):
        dx, dz = (ds, df) if d % 2 else (df, ds)
        for x in range(4):
            for z in range(4):
                src = 4 * ((x + dx) % 4) + (z + dz) % 4
                pairs.append((N_INNER * d + src, N_INNER * d + 4 * x + z))
    return pairs


def double_pairs(f_bits, s_bits):
    pairs = []
    for d in range(N_DP):
        x_bits, z_bits = (s_bits, f_bits) if d % 2 else (f_bits, s_bits)
        flip = 4 * x_bits + z_bits
        pairs += [(N_INNER * d + (m ^ flip), N_INNER * d + m) for m in range(N_INNER)]
    return pairs


def from_ring(value, df, ds):
    return lax.ppermute(value, ("dp", "inner"), ring_pairs(df, ds))


def swap_cores(value):
    return lax.ppermute(value, "dp", [(d ^ 1, d) for d in range(N_DP)])


def exchange(value, axis="dp"):
    return lax.all_to_all(value, axis, split_axis=0, concat_axis=0, tiled=True)


def on_device(patches, segments, owners, norm_gain, qkv_weight, cotangent):
    group = lax.axis_index("dp")
    inner = lax.axis_index("inner")
    core, x, z = group % 2, inner // 4, inner % 4
    gain = norm_gain.reshape(1, D)

    pos = jnp.arange(N_INNER)
    df, ds = pos % 4, pos // 4
    m = 4 * ((x + jnp.where(core == 0, df, ds)) % 4) + (
        z + jnp.where(core == 0, ds, df)
    ) % 4
    nat = (
        (jnp.arange(N_DP)[None, :, None] * N_INNER + m[:, None, None]) * OWN
        + jnp.arange(OWN)[None, None, :]
    ).reshape(1, D).astype(F32)

    messages = exchange(build(owners, qkv_weight, segments))
    partner_patches = swap_cores(patches)
    strips = cotangent.reshape(TILES, N_DP, STRIP, D).transpose(1, 0, 2, 3)
    messages, strips = lax.optimization_barrier((messages, strips))
    block, seg, owners_all = compact(group.reshape(1).astype(jnp.int32), messages)
    strips = exchange(strips)

    owner_of = owners_all[:, :TILES].astype(jnp.int32).reshape(N_DP * TILES)
    u = jnp.arange(N_DP * TILES)
    earlier = (owner_of[:, None] == owner_of[None, :]) & (
        u[None, :] // TILES < u[:, None] // TILES
    )
    fwd = (TILES * owner_of + jnp.sum(earlier, axis=1)).astype(jnp.int32)
    wanted = fwd[None, :] == TILES * group + jnp.arange(TILES)[:, None]
    source = jnp.sum(jnp.where(wanted, u[None, :] // TILES, 0), axis=1)
    place_index = jnp.concatenate([2 * (source // 2), source % 2]).astype(jnp.int32)
    mine = jnp.arange(2)[:, None] ^ core
    tile = (TILES * (group - core + mine) + jnp.arange(TILES)[None, :]).reshape(-1)
    owner_here = jnp.sum(jnp.where(tile[:, None] == u[None, :], owner_of, 0), axis=1)
    slot_index = jnp.concatenate(
        [owner_here, jnp.broadcast_to(mine, (2, TILES)).reshape(-1)]
    ).astype(jnp.int32)

    ring = [block] + [from_ring(block, f, 0) for f in (1, 2, 3)]
    near_a, near_b = jnp.concatenate(ring[:2]), jnp.concatenate(ring[2:])
    later_patches, near_b = lax.optimization_barrier((patches, near_b))
    own_prep = prep(later_patches, gain, nat)
    strips, own_prep = lax.optimization_barrier((strips, own_prep))

    heads = to_heads(fwd, strips.reshape(N_DP * TILES, STRIP, D))
    cot = exchange(heads)

    above_a, below_b = from_ring(near_a, 0, 1), from_ring(near_b, 0, -1)
    above_b, below_a = from_ring(near_b, 0, 1), from_ring(near_a, 0, -1)
    above_a, above_b, below_a, below_b = lax.optimization_barrier(
        (above_a, above_b, below_a, below_b)
    )
    far_a, far_b = from_ring(above_a, 0, 1), from_ring(below_b, 0, -1)
    pieces = [near_a, near_b, above_a, above_b, far_a, far_b, below_a, below_b]
    normed, normed_t = zip(own_prep, prep(partner_patches, gain, nat))

    out, dqkv, *parts, gain_part = main(slot_index, seg, normed, normed_t, cot, pieces)
    col_a, col_b, up_a, up_b, far_up, far_down, down_a, down_b = parts

    far_up, far_down = from_ring(far_up, 0, -1), from_ring(far_down, 0, 1)
    up_b, down_a = from_ring(up_b, 0, -1), from_ring(down_a, 0, 1)
    slots = exchange(out)
    gain_part = gain_back(gain_part, nat, gain)
    far_up, far_down, gain_part = lax.optimization_barrier((far_up, far_down, gain_part))
    up_a, down_b = add([[(up_a, 0), (far_up, 0)], [(down_b, 0), (far_down, 0)]])
    gain_other = lax.ppermute(gain_part, ("dp", "inner"), double_pairs(0, 1))
    from_up_a, from_down_b = from_ring(up_a, 0, -1), from_ring(down_b, 0, 1)
    gain_part = gain_part + gain_other
    gain_other = lax.ppermute(gain_part, ("dp", "inner"), double_pairs(0, 3))
    dqkv, up_b, down_a, gain_part = lax.optimization_barrier(
        (dqkv, up_b, down_a, gain_part)
    )
    partners = back(1, dqkv, pieces, nat)
    from_up_a, from_down_b, partners = lax.optimization_barrier(
        (from_up_a, from_down_b, partners)
    )
    other = swap_cores(partners)
    zero, one, two, three = add(
        [
            [(col_a, 0), (from_up_a, 0), (down_a, 0)],
            [(col_b, 0), (up_b, 0), (from_down_b, 0)],
        ],
        (gain_part, gain_other),
    )
    dqkv, _ = lax.optimization_barrier((dqkv, zero))
    mine = back(0, dqkv, pieces, nat)
    others = [from_ring(two, -2, 0), from_ring(three, 1, 0), from_ring(one, -1, 0)]
    others[0], slots, mine = lax.optimization_barrier((others[0], slots, mine))

    attended = place(place_index, slots).reshape(ROWS, D)
    grad_rows = rows_back(patches, gain, mine, other)
    grad_qkv, grad_gain = finish(exchange(split(zero, others)))
    return (attended, grad_rows, grad_qkv, grad_gain.reshape(D))


def solution(mesh):
    both = ("dp", "inner")
    placed = (
        P(both, None),
        P(both, None),
        P(both),
        P(),
        P(both, None),
        P(both, None),
    )
    return jax.shard_map(
        on_device,
        mesh=mesh,
        in_specs=placed,
        out_specs=(P(both, None), P(both, None), P(both, None), P()),
        check_vma=False,
    )
```
